32 devices in a mesh: dp: 8 (over z, y), mp: 4 (over x, core).
Axes of the slice: x: 2, y: 2, z: 4, core: 2. Of those that a mesh axis runs over, the one named last changes fastest.
Arguments:
- tokens_in: bfloat16 [1024, 1536], P('dp'), may hold values from -6 to 6
- text_feats: bfloat16 [8, 4, 32, 4096], P('dp'), may hold values from -6 to 6
- frame_counts: int32 [8, 4], P('dp'), may hold values from 0 to 16, as said below
- time_steps: int32 [8, 4], P('dp'), may hold values from 0 to 999
- attn_master: float32 [4, 7079424], P('mp', 'dp'), may hold values from -8 to 8
- attn_first: float32 [4, 7079424], P('mp', 'dp'), may hold values from -21.12 to 21.12
- attn_second: float32 [4, 7079424], P('mp', 'dp'), may hold values from 51.2 to 204.8
- ffn_master: float32 [4, 4718592], P('mp', 'dp'), may hold values from -0.15625 to 0.15625
- ffn_first: float32 [4, 4718592], P('mp', 'dp'), may hold values from -21.12 to 21.12
- ffn_second: float32 [4, 4718592], P('mp', 'dp'), may hold values from 51.2 to 204.8
- norm_master: float32 [6144], P('dp'), may hold values from 0.5 to 1.5
- norm_first: float32 [6144], P('dp'), may hold values from -21.12 to 21.12
- norm_second: float32 [6144], P('dp'), may hold values from 51.2 to 204.8
- step_count: int32 [1], replicated, may hold values from 1 to 3
- cotangent: bfloat16 [1024, 1536], P('dp'), may hold values from -6 to 6
Outputs:
- output: bfloat16 [1024, 1536], P('dp')
- input_grad: bfloat16 [1024, 1536], P('dp')
- attn_new: float32 [4, 7079424], P('mp', 'dp')
- attn_first_new: float32 [4, 7079424], P('mp', 'dp')
- attn_second_new: float32 [4, 7079424], P('mp', 'dp')
- attn_grad: float32 [4, 7079424], P('mp', 'dp')
- attn_copy: bfloat16 [4, 7079424], P('mp', 'dp')
- ffn_new: float32 [4, 4718592], P('mp', 'dp')
- ffn_first_new: float32 [4, 4718592], P('mp', 'dp')
- ffn_second_new: float32 [4, 4718592], P('mp', 'dp')
- ffn_grad: float32 [4, 4718592], P('mp', 'dp')
- ffn_copy: bfloat16 [4, 4718592], P('mp', 'dp')
- norm_new: float32 [6144], P('dp')
- norm_first_new: float32 [6144], P('dp')
- norm_second_new: float32 [6144], P('dp')
- norm_grad: float32 [6144], P('dp')
- norm_copy: bfloat16 [6144], P('dp')
- gate_grads: float32 [8, 1536], P('dp', 'mp')
The draws below stay inside these ranges and needn't reach their ends.
Inputs may be any that keep to these rules, and one draw needn't show every extreme that they name: `frame_counts`: A slot holds 0 or 4 to 16 frames; a pack's frames add up to at most 16; empty slots come after the used ones, and slot 0 is used.
All inputs are finite; a program needn't handle non-finite values.
Results may differ from the reference program's by a relative error of at most 0.02.
Values may be sent and summed in bfloat16 or wider, within the bound.
No kernel may reach another device: no remote copies, remote signals or barrier semaphores. Data moves between devices by JAX's collectives and lax.ppermute only.
A program may use at most 384 MiB of HBM per device.

```python
import math
import jax
import jax.numpy as jnp
from jax import lax

D = 1536
HEADS = 24
HEAD_DIM = 64
FF = 4096
TEXT_D = 4096
COND = 1024
CLIPS = 4
MAX_FRAMES = 16
MIN_FRAMES = 4
FRAME_TOK = 8
TEXT_LEN = 32
TOK_DEV = 128
PACKS = 8
TOKENS = 1024
D_LOC = 384
FF_LOC = 1024
ATTN_FLAT = 7079424
FFN_FLAT = 4718592
NORMS = 6144
N_MP = 4


def draw_frame_counts(key, part):
    wanted = jax.random.randint(key, (PACKS, CLIPS), MIN_FRAMES, MAX_FRAMES + 1)
    remaining = jnp.full((PACKS,), MAX_FRAMES, jnp.int32)
    columns = []
    for slot_index in range(CLIPS):
        desired = wanted[:, slot_index]
        taken_frames = jnp.where(desired <= remaining, desired, jnp.where(remaining >= MIN_FRAMES, remaining, 0))
        if slot_index == 0:
            taken_frames = jnp.where(jnp.arange(PACKS) == 0, MAX_FRAMES, taken_frames)
        columns.append(taken_frames.astype(jnp.int32))
        remaining = remaining - taken_frames
    return jnp.stack(columns, 1).astype(jnp.int32)


def draw_attn_master(key, part):
    segments = [(3 * D * D_LOC + D_LOC * D, D ** (-0.5)), (2 * TEXT_D * D_LOC, TEXT_D ** (-0.5)), (4 * COND * D_LOC, 1.5 * COND ** (-0.5))]
    pieces = []
    for piece_index in range(len(segments)):
        segment_size, factor = segments[piece_index]
        sub_key = jax.random.fold_in(key, piece_index)
        random_part = jax.random.normal(sub_key, (N_MP, segment_size), jnp.float32)
        pieces.append(random_part * factor)
    pieces.append(jax.random.uniform(jax.random.fold_in(key, 7), (N_MP, 3 * D_LOC), jnp.float32, 0.5, 1.5))
    gate_part = jax.random.uniform(jax.random.fold_in(key, 8), (N_MP, D_LOC), jnp.float32, -1.5, 1.5)
    pieces.append(gate_part)
    return jnp.concatenate(pieces, 1)


def plant(drawn, rng, low, high):
    longest = drawn.shape.index(max(drawn.shape))
    spots = []
    for shift in (0, 1):
        where = [jax.random.randint(jax.random.fold_in(rng, axis), (), 0, length) for axis, length in enumerate(drawn.shape)]
        where[longest] = (where[longest] + shift) % drawn.shape[longest]
        spots.append(tuple(where))
    return drawn.at[spots[0]].set(low).at[spots[1]].set(high)


def level_of(stream_key, dims, shards, low, largest):
    def one(position, shards_of):
        heights = jax.random.uniform(jax.random.fold_in(jax.random.fold_in(stream_key, 6), position), (shards_of,), jnp.float32, low / len(shards), largest / len(shards))
        return jnp.repeat(jnp.exp(heights), dims[position] // shards_of).reshape((-1,) + (1,) * (len(dims) - position - 1))

    factor_of = one(*shards[0])
    for cut in shards[1:]:
        factor_of = factor_of * one(*cut)
    return factor_of


def scatter_about(key, shape, width, most, cuts=(), kind=jnp.bfloat16):
    loudness = level_of(key, shape, cuts, -0.22, 0.18) if cuts else 1.0
    values = jax.random.normal(key, shape, jnp.float32) * width * loudness
    return jnp.minimum(jnp.maximum(values, -most), most).astype(kind)


def setup_inputs(seed: int = 0) -> dict:
    splits = jax.random.split(jax.random.key(seed), 16)
    return {
        "tokens_in": scatter_about(splits[0], (TOKENS, D), 1.0, 6.0, ((0, 8),)),
        "text_feats": scatter_about(splits[1], (PACKS, CLIPS, TEXT_LEN, TEXT_D), 1.0, 6.0, ((0, 8),)),
        "frame_counts": draw_frame_counts(jax.random.fold_in(splits[15], 71), 0),
        "time_steps": plant(jax.random.randint(splits[3], (PACKS, CLIPS), 0, 1000), jax.random.fold_in(splits[3], 1), 0, 999).astype(jnp.int32),
        "attn_master": draw_attn_master(jax.random.fold_in(splits[15], 71), 0),
        "attn_first": scatter_about(splits[5], (N_MP, ATTN_FLAT), (0.11 * TOKENS ** 0.5), 21.12, ((0, 4), (1, 8)), jnp.float32),
        "attn_second": jnp.clip(jnp.exp(math.log(204.8) - 1.3862944 * jax.random.uniform(splits[6], (N_MP, ATTN_FLAT), jnp.float32) ** level_of(splits[6], (N_MP, ATTN_FLAT), ((0, 4), (1, 8)), -0.2, 0.2)), 51.2, 204.8),
        "ffn_master": scatter_about(splits[7], (N_MP, FFN_FLAT), D ** -0.5, 0.15625, ((0, 4), (1, 8)), jnp.float32),
        "ffn_first": scatter_about(splits[8], (N_MP, FFN_FLAT), (0.11 * TOKENS ** 0.5), 21.12, ((0, 4), (1, 8)), jnp.float32),
        "ffn_second": jnp.clip(jnp.exp(math.log(204.8) - 1.3862944 * jax.random.uniform(splits[9], (N_MP, FFN_FLAT), jnp.float32) ** level_of(splits[9], (N_MP, FFN_FLAT), ((0, 4), (1, 8)), -0.2, 0.2)), 51.2, 204.8),
        "norm_master": jnp.clip(0.5 + 1.0 * jax.random.uniform(splits[10], (NORMS,), jnp.float32) ** level_of(splits[10], (NORMS,), ((0, 8),), -0.2, 0.2), 0.5, 1.5),
        "norm_first": scatter_about(splits[11], (NORMS,), (0.11 * TOKENS ** 0.5), 21.12, ((0, 8),), jnp.float32),
        "norm_second": jnp.clip(jnp.exp(math.log(204.8) - 1.3862944 * jax.random.uniform(splits[12], (NORMS,), jnp.float32) ** level_of(splits[12], (NORMS,), ((0, 8),), -0.2, 0.2)), 51.2, 204.8),
        "step_count": jax.random.randint(splits[13], (1,), 1, 4).astype(jnp.int32),
        "cotangent": scatter_about(splits[14], (TOKENS, D), 1.0, 6.0, ((0, 8),)),
    }


@jax.custom_vjp
def low(v):
    return lax.optimization_barrier(v.astype(jnp.bfloat16)).astype(jnp.float32)

@jax.custom_vjp
def low_back(v):
    return v

def low_keep(v):
    return (low(v), None)

def low_pass(kept, grad):
    return (grad,)

def back_keep(v):
    return (v, None)

def back_low(kept, grad):
    return (low(grad),)
low.defvjp(low_keep, low_pass)
low_back.defvjp(back_keep, back_low)
EPS = 1e-06
NEG = -1e+30
BETA_ONE = 0.9
BETA_TWO = 0.95
RATE = 0.03
RATE_NORM = 0.3
DECAY = 0.1
ADAM_EPS = 1e-08

def matmul(left, right):
    return jnp.dot(left, right, precision=lax.Precision.HIGHEST, preferred_element_type=jnp.float32)

def rms_norm(values):
    return values * lax.rsqrt(lax.optimization_barrier(jnp.mean(values * values, -1, keepdims=True)) + EPS)

def rope_tables(positions, head_size):
    half_size = head_size // 2
    frequency = jnp.exp(-jnp.log(10000.0) * 2.0 * jnp.arange(half_size, dtype=jnp.float32) / head_size)
    angles = positions.astype(jnp.float32)[:, None] * frequency[None, :]
    cosine = jnp.cos(angles)
    sine_table = jnp.sin(angles)
    return (jnp.concatenate([cosine, cosine], -1), jnp.concatenate([sine_table, sine_table], -1))

def rotate(values, cosine, sine_table):
    half_size = values.shape[-1] // 2
    turned = jnp.concatenate([-values[..., half_size:], values[..., :half_size]], -1)
    return values * cosine[:, None, :] + turned * sine_table[:, None, :]

def clip_layout(frames_row, length, frame_tok, clip_slots):
    clip_len = (frames_row * frame_tok).astype(jnp.int32)
    clip_end = jnp.cumsum(clip_len).astype(jnp.int32)
    clip_start = clip_end - clip_len
    row_index = jnp.arange(length, dtype=jnp.int32)
    segment = lax.optimization_barrier(jnp.sum((row_index[:, None] >= clip_end[None, :]).astype(jnp.int32), 1, dtype=jnp.int32))
    member = segment[:, None] == jnp.arange(clip_slots, dtype=jnp.int32)[None, :]
    begin_row = lax.optimization_barrier(jnp.sum(jnp.where(member, clip_start[None, :], 0), 1, dtype=jnp.int32))
    begin_row = begin_row + jnp.where(segment == clip_slots, clip_end[clip_slots - 1], 0).astype(jnp.int32)
    return (segment, member.astype(jnp.float32), row_index - begin_row)

def condition(steps_row, cond_width):
    half_size = cond_width // 2
    frequency = jnp.exp(-jnp.log(10000.0) * jnp.arange(half_size, dtype=jnp.float32) / half_size)
    angles = steps_row.astype(jnp.float32)[:, None] * frequency[None, :]
    return jax.nn.silu(jnp.concatenate([jnp.cos(angles), jnp.sin(angles)], -1))

def unpack(flat_rows, shapes):
    result = []
    offset = 0
    for piece_shape in shapes:
        piece_size = math.prod(piece_shape)
        result.append(flat_rows[:, offset:offset + piece_size].reshape((flat_rows.shape[0],) + piece_shape))
        offset += piece_size
    return result

def attend(query, keys, values, mask):
    scores = low_back(jnp.einsum('shd,thd->hst', query, keys, precision=lax.Precision.HIGHEST)) * HEAD_DIM ** (-0.5)
    scores = jnp.where(mask[None], scores, NEG)
    probs_all = jax.nn.softmax(scores, -1)
    return jnp.einsum('hst,thd->shd', low(probs_all), values, precision=lax.Precision.HIGHEST)

def layer(attn_flat, ffn_flat, norm_flat, hidden_in, text_pack, frames_row, steps_row):
    pieces = unpack(low(attn_flat), [(D, D_LOC), (D, D_LOC), (D, D_LOC), (D_LOC, D), (TEXT_D, D_LOC), (TEXT_D, D_LOC), (COND, 4, D_LOC), (D_LOC,), (D_LOC,), (D_LOC,), (D_LOC,)])
    w_query = pieces[0].transpose(1, 0, 2).reshape(D, D)
    w_key = pieces[1].transpose(1, 0, 2).reshape(D, D)
    w_value = pieces[2].transpose(1, 0, 2).reshape(D, D)
    w_out = pieces[3].reshape(D, D)
    w_text_key = pieces[4].transpose(1, 0, 2).reshape(TEXT_D, D)
    w_text_value = pieces[5].transpose(1, 0, 2).reshape(TEXT_D, D)
    w_mod = pieces[6].transpose(1, 2, 0, 3).reshape(COND, 4 * D)
    query_gain = pieces[7].reshape(HEADS, HEAD_DIM)
    key_gain = pieces[8].reshape(HEADS, HEAD_DIM)
    text_gain = pieces[9].reshape(HEADS, HEAD_DIM)
    cross_gate = pieces[10].reshape(HEADS, HEAD_DIM)
    ffn_pieces = unpack(low(ffn_flat), [(D, FF_LOC), (D, FF_LOC), (FF_LOC, D)])
    w_gate = ffn_pieces[0].transpose(1, 0, 2).reshape(D, FF)
    w_up = ffn_pieces[1].transpose(1, 0, 2).reshape(D, FF)
    w_down = ffn_pieces[2].reshape(FF, D)
    norm_gains = low(norm_flat).reshape(4, D)
    segment, member, positions = clip_layout(frames_row, TOK_DEV, FRAME_TOK, CLIPS)
    cosine, sine_table = rope_tables(positions, HEAD_DIM)
    modulation = low_back(matmul(low(condition(steps_row, COND)), w_mod)).reshape(CLIPS, 4, D)
    scale_attn = matmul(member, modulation[:, 0])
    gate_attn = matmul(member, modulation[:, 1])
    scale_ffn = matmul(member, modulation[:, 2])
    gate_ffn = matmul(member, modulation[:, 3])
    head_shape = (TOK_DEV, HEADS, HEAD_DIM)
    text_shape = (CLIPS * TEXT_LEN, HEADS, HEAD_DIM)
    normed = low(rms_norm(hidden_in) * norm_gains[0] * (1.0 + scale_attn))
    query = low_back(matmul(normed, w_query)).reshape(head_shape)
    query = low(rotate(rms_norm(query) * query_gain, cosine, sine_table))
    keys = low_back(matmul(normed, w_key)).reshape(head_shape)
    keys = low(rotate(rms_norm(keys) * key_gain, cosine, sine_table))
    values = low(low_back(matmul(normed, w_value))).reshape(head_shape)
    text_rows = text_pack.reshape(CLIPS * TEXT_LEN, TEXT_D)
    text_keys = low(rms_norm(low_back(matmul(text_rows, w_text_key)).reshape(text_shape)) * text_gain)
    text_values = low(low_back(matmul(text_rows, w_text_value))).reshape(text_shape)
    self_mask = segment[:, None] == segment[None, :]
    key_clip = jnp.arange(CLIPS * TEXT_LEN, dtype=jnp.int32) // TEXT_LEN
    cross_mask = (segment[:, None] == key_clip[None, :]) | (segment == CLIPS)[:, None]
    own = attend(query, keys, values, self_mask)
    cross = low_back(attend(query, text_keys, text_values, cross_mask))
    mixed = low(low_back(own + jnp.tanh(cross_gate) * cross)).reshape(TOK_DEV, D)
    attn_out = low_back(sum((low(matmul(mixed[:, group_index * D_LOC:(group_index + 1) * D_LOC], w_out[group_index * D_LOC:(group_index + 1) * D_LOC])) for group_index in range(N_MP))))
    middle = hidden_in + jnp.tanh(gate_attn) * rms_norm(attn_out) * norm_gains[1]
    ffn_in = low(rms_norm(middle) * norm_gains[2] * (1.0 + scale_ffn))
    gate_lin = low_back(matmul(ffn_in, w_gate))
    up_lin = low_back(matmul(ffn_in, w_up))
    hidden = low(jax.nn.silu(gate_lin) * up_lin)
    ffn_out = low_back(sum((low(matmul(hidden[:, group_index * FF_LOC:(group_index + 1) * FF_LOC], w_down[group_index * FF_LOC:(group_index + 1) * FF_LOC])) for group_index in range(N_MP))))
    return middle + jnp.tanh(gate_ffn) * rms_norm(ffn_out) * norm_gains[3]

def adamw(master, first, second, gradient, step_value, rate):
    first_new = BETA_ONE * first + (1.0 - BETA_ONE) * gradient
    second_new = BETA_TWO * second + (1.0 - BETA_TWO) * gradient * gradient
    first_fix = 1.0 - jnp.power(BETA_ONE, step_value)
    second_fix = 1.0 - jnp.power(BETA_TWO, step_value)
    update = rate * (first_new / first_fix / (jnp.sqrt(second_new / second_fix) + ADAM_EPS) + DECAY * master)
    master_new = master - update
    return (master_new, first_new, second_new, gradient, master_new.astype(jnp.bfloat16))

def reference(tokens_in, text_feats, frame_counts, time_steps, attn_master, attn_first, attn_second, ffn_master, ffn_first, ffn_second, norm_master, norm_first, norm_second, step_count, cotangent):
    inputs_all = tokens_in.astype(jnp.float32).reshape(PACKS, TOK_DEV, D)
    cot_all = cotangent.astype(jnp.float32).reshape(PACKS, TOK_DEV, D)
    text_all = text_feats.astype(jnp.float32)

    def one_pack(carry, items):
        hidden_in, cot_pack, text_pack, frames_row, steps_row = items

        def forward(attn_flat, ffn_flat, norm_flat, block_in):
            return layer(attn_flat, ffn_flat, norm_flat, block_in, text_pack, frames_row, steps_row)
        result, back = jax.vjp(forward, attn_master, ffn_master, norm_master, hidden_in)
        attn_part, ffn_part, norm_part, input_part = back(cot_pack)
        carry = (carry[0] + attn_part, carry[1] + ffn_part, carry[2] + norm_part)
        pack_gate = attn_part[:, ATTN_FLAT - D_LOC:].reshape(D)
        return (carry, (result.astype(jnp.bfloat16), input_part.astype(jnp.bfloat16), pack_gate))
    start = (jnp.zeros_like(attn_master), jnp.zeros_like(ffn_master), jnp.zeros_like(norm_master))
    totals, stacked = lax.scan(one_pack, start, (inputs_all, cot_all, text_all, frame_counts, time_steps))
    output = stacked[0].reshape(TOKENS, D)
    input_grad = stacked[1].reshape(TOKENS, D)
    gate_grads = stacked[2]
    step_value = step_count[0].astype(jnp.float32)
    attn_new, attn_first_new, attn_second_new, attn_grad, attn_copy = adamw(attn_master, attn_first, attn_second, totals[0], step_value, RATE)
    ffn_new, ffn_first_new, ffn_second_new, ffn_grad, ffn_copy = adamw(ffn_master, ffn_first, ffn_second, totals[1], step_value, RATE)
    norm_new, norm_first_new, norm_second_new, norm_grad, norm_copy = adamw(norm_master, norm_first, norm_second, totals[2], step_value, RATE_NORM)
    return (output, input_grad, attn_new, attn_first_new, attn_second_new, attn_grad, attn_copy, ffn_new, ffn_first_new, ffn_second_new, ffn_grad, ffn_copy, norm_new, norm_first_new, norm_second_new, norm_grad, norm_copy, gate_grads)
```

```python
import functools
import math

import jax
import jax.numpy as jnp
from jax import lax
from jax.experimental import pallas as pl
from jax.experimental.pallas import tpu as pltpu
from jax.sharding import PartitionSpec as P

HEAD_DIM = 64
COND = 1024
FRAME_TOK = 8
LANES = 128
TILE = 16

EPS = 1e-06
NEG = -1e30
BETA_ONE = 0.9
BETA_TWO = 0.95
RATE = 0.03
RATE_NORM = 0.3
DECAY = 0.1
ADAM_EPS = 1e-08

F32 = jnp.float32
BF16 = jnp.bfloat16
VMEM = pl.BlockSpec(memory_space=pltpu.VMEM)
SMEM = pl.BlockSpec(memory_space=pltpu.SMEM)
ANY = pl.BlockSpec(memory_space=pl.ANY)


def params(mib):
    return pltpu.CompilerParams(vmem_limit_bytes=mib << 20)


def round_up(value, unit):
    return -(-value // unit) * unit


class Layout:
    def __init__(self, total, width, parts, tile, spare=0):
        self.total, self.width, self.parts, self.spare = total, width, parts, spare
        self.unit = tile * width
        self.size = total // parts
        self.base = [d * self.size // self.unit * tile for d in range(parts)] + [
            round_up(-(-total // width), tile)
        ]
        self.off = [d * self.size - self.base[d] * width for d in range(parts)]
        self.used = round_up(max(-(-(o + self.size) // width) for o in self.off), tile)
        self.rows = self.used + spare
        self.lanes = width // LANES
        self.edge = round_up(max(self.off), TILE * LANES)

    def offset(self, index):
        return (index * self.size) % self.unit

    def spans(self, low, high):
        found = []
        for d in range(self.parts):
            first, last = max(low, self.base[d]), min(high, self.base[d + 1])
            if first < last:
                found.append((d, first - self.base[d], last - first, first - low))
        return found

    def pick(self, held, low, high):
        found = [held[d, first : first + rows] for d, first, rows, _ in self.spans(low, high)]
        return found[0] if len(found) == 1 else jnp.concatenate(found, 0)

    def cut(self, matrices, spares=None):
        short = self.base[self.parts - 1] + self.used - sum(m.shape[0] for m in matrices)
        if short > 0:
            matrices = matrices + [jnp.zeros((short, self.width), matrices[0].dtype)]
        whole = jnp.concatenate(matrices, 0)
        if spares is None and self.used * self.parts == whole.shape[0]:
            return whole.reshape(self.parts, self.used, self.width)
        pieces = [whole[b : b + self.used] for b in self.base[: self.parts]]
        if spares is not None:
            pieces = [jnp.concatenate([p, spares[d]], 0) for d, p in enumerate(pieces)]
        return jnp.stack(pieces)


class Pieces:
    def __init__(self, layout, high, ring):
        self.width = layout.width
        parts = layout.parts
        self.rows = round_up(-(-high // parts), LANES)
        self.holders = sum(base < high for base in layout.base[:parts])
        free = list(range(self.holders, parts))
        self.where, self.pairs = [], {}
        for d in range(self.holders):
            last = min(layout.base[d + 1], high)
            for number, low in enumerate(range(layout.base[d], last, self.rows)):
                owner = d
                if number:
                    near = [f for f in free if (f - d) % ring.inner == 0] or free
                    owner = near[-1]
                    free.remove(owner)
                    self.pairs.setdefault(number, []).append((d, owner))
                self.where.append((low, min(low + self.rows, last), owner))

    def send(self, block):
        self.first = block[: self.rows]
        self.sent = {
            number: lax.ppermute(
                block[number * self.rows : (number + 1) * self.rows], "dp", pairs
            )
            for number, pairs in self.pairs.items()
        }
        return self

    def moving(self):
        return self.sent

    def land(self, moved):
        self.got = functools.reduce(jnp.add, moved.values())

    def piece(self, index):
        return jnp.where(index < self.holders, self.first, self.got)

    def spans(self, low, high):
        found = []
        for start, end, owner in self.where:
            first, last = max(low, start), min(high, end)
            if first < last:
                found.append((owner, first - start, last - first, first - low))
        return found

    def pick(self, held, low, high):
        found = [held[d, first : first + rows] for d, first, rows, _ in self.spans(low, high)]
        return found[0] if len(found) == 1 else jnp.concatenate(found, 0)


def to_rows(layout, flat, index, spare=None):
    rows, lanes, size = layout.used, layout.lanes, layout.size
    whole = size // (8 * LANES) * 8
    tail = size - whole * LANES
    head = max(layout.edge // LANES, 8)
    depth = round_up(max(rows * lanes + head, head + whole + 8) + 8, 8)
    offset = layout.offset(index).astype(jnp.int32)[None]
    operands = [offset, flat]
    if layout.edge:
        tails = flat[:, size - layout.edge :].reshape(head, LANES)
        chain = [(d, d + 1) for d in range(layout.parts - 1)]
        operands.append(lax.ppermute(tails.astype(BF16), "dp", chain).astype(F32))
    if layout.spare:
        operands.append(spare)

    def kernel(off_ref, x_ref, *rest):
        if layout.spare:
            rest[-2][rows : rows + layout.spare, :] = rest[-3][...].astype(BF16)
        edge_ref = rest[0] if layout.edge else None
        out_ref, pad_ref = rest[-2:]
        if layout.edge:
            pad_ref[0:head, :] = edge_ref[...]
        pad_ref[pl.ds(head, whole), :] = x_ref[:, pl.ds(0, whole * LANES)].reshape(whole, LANES)
        left = depth - head - whole
        pad_ref[pl.ds(head + whole, left), :] = jnp.zeros((left, LANES), F32)
        for row in range(-(-tail // LANES)):
            count = min(LANES, tail - row * LANES)
            pad_ref[pl.ds(head + whole + row, 1), 0:count] = x_ref[
                :, pl.ds((whole + row) * LANES, count)
            ]
        off_rows, off_lane = off_ref[0] // LANES, off_ref[0] % LANES
        lane = lax.broadcasted_iota(jnp.int32, (rows, LANES), 1)
        for j in range(lanes):
            if layout.edge:
                before = pad_ref[pl.ds(head + j - off_rows - 1, rows, stride=lanes), :]
                here = pad_ref[pl.ds(head + j - off_rows, rows, stride=lanes), :]
                value = jnp.where(
                    lane < off_lane,
                    pltpu.roll(before, off_lane, 1),
                    pltpu.roll(here, off_lane, 1),
                )
            else:
                value = pad_ref[pl.ds(head + j, rows, stride=lanes), :]
            out_ref[0:rows, LANES * j : LANES * j + LANES] = value.astype(BF16)

    return pl.pallas_call(
        kernel,
        out_shape=jax.ShapeDtypeStruct((layout.rows, layout.width), BF16),
        in_specs=[SMEM] + [VMEM] * (len(operands) - 1),
        out_specs=VMEM,
        scratch_shapes=[pltpu.VMEM((depth, LANES), F32)],
        compiler_params=params(40),
    )(*operands)


def block_rows(layout):
    need = -(-layout.size // LANES)
    steps = max(1, need // 864)
    return round_up(-(-need // steps), 8), -(-need // round_up(-(-need // steps), 8))


def to_flat(layout, matrix, index):
    rows, lanes = layout.used, layout.lanes
    block, steps = block_rows(layout)
    depth = round_up(max(rows * lanes, block * steps + layout.unit // LANES + 1), 8) + 8
    offset = layout.offset(index).astype(jnp.int32)[None]

    def kernel(off_ref, x_ref, out_ref, pad_ref):
        for j in range(lanes):
            pad_ref[pl.ds(j, rows, stride=lanes), :] = x_ref[
                0:rows, LANES * j : LANES * j + LANES
            ]
        left = depth - rows * lanes
        pad_ref[pl.ds(rows * lanes, left), :] = jnp.zeros((left, LANES), F32)
        off_rows, off_lane = off_ref[0] // LANES, off_ref[0] % LANES
        turn = (LANES - off_lane) % LANES
        lane = lax.broadcasted_iota(jnp.int32, (block, LANES), 1)

        def body(step, carry):
            start = pl.multiple_of(step * block, 8)
            here = pad_ref[pl.ds(start + off_rows, block), :]
            if layout.edge:
                after = pad_ref[pl.ds(start + off_rows + 1, block), :]
                here = jnp.where(
                    lane < LANES - off_lane, pltpu.roll(here, turn, 1), pltpu.roll(after, turn, 1)
                )
            out_ref[pl.ds(start, block), :] = here
            return carry

        lax.fori_loop(0, steps, body, 0)

    return pl.pallas_call(
        kernel,
        out_shape=jax.ShapeDtypeStruct((block * steps, LANES), F32),
        in_specs=[SMEM, VMEM],
        out_specs=VMEM,
        scratch_shapes=[pltpu.VMEM((depth, LANES), F32)],
        compiler_params=params(48),
    )(offset, matrix)


def adamw(master, first, second, gradient, step_value, rate):
    first_new = BETA_ONE * first + (1.0 - BETA_ONE) * gradient
    second_new = BETA_TWO * second + (1.0 - BETA_TWO) * gradient * gradient
    first_fix = 1.0 - jnp.power(BETA_ONE, step_value)
    second_fix = 1.0 - jnp.power(BETA_TWO, step_value)
    update = rate * (
        first_new / first_fix / (jnp.sqrt(second_new / second_fix) + ADAM_EPS) + DECAY * master
    )
    master_new = master - update
    return (master_new, first_new, second_new, gradient, master_new.astype(BF16))


def adamw_flat(layout, master, first, second, gradient, step_value, rate):
    block, steps = block_rows(layout)
    fixes = jnp.stack(
        [1.0 - jnp.power(BETA_ONE, step_value), 1.0 - jnp.power(BETA_TWO, step_value)]
    )

    def kernel(fix_ref, w_ref, m_ref, v_ref, g_ref, w_out, m_out, v_out, g_out, c_out):
        view = lambda ref: ref.reshape(block, LANES)
        grad = g_ref[...]
        master_old = view(w_ref)[...]
        first_new = BETA_ONE * view(m_ref)[...] + (1.0 - BETA_ONE) * grad
        second_new = BETA_TWO * view(v_ref)[...] + (1.0 - BETA_TWO) * grad * grad
        update = rate * (
            first_new / fix_ref[0] / (jnp.sqrt(second_new / fix_ref[1]) + ADAM_EPS)
            + DECAY * master_old
        )
        view(w_out)[...] = master_old - update
        view(m_out)[...] = first_new
        view(v_out)[...] = second_new
        view(g_out)[...] = grad
        c_out[...] = w_out[...].astype(BF16)

    row = pl.BlockSpec((1, block * LANES), lambda i: (0, i))
    like = jax.ShapeDtypeStruct(master.shape, F32)
    return pl.pallas_call(
        kernel,
        grid=(steps,),
        out_shape=(like, like, like, like, jax.ShapeDtypeStruct(master.shape, BF16)),
        in_specs=[SMEM, row, row, row, pl.BlockSpec((block, LANES), lambda i: (i, 0))],
        out_specs=(row,) * 5,
        compiler_params=params(48),
    )(fixes, master, first, second, gradient)


class Ring:
    def __init__(self, parts):
        self.parts = parts
        self.inner = 2 if parts % 2 == 0 else 1
        self.outer = parts // self.inner
        self.small = self.outer <= 8
        self.next = [(d, (d + self.inner) % parts) for d in range(parts)]
        self.pair = [(d, d ^ 1) for d in range(parts)]

    def swap(self, block):
        return lax.ppermute(block, "dp", self.pair)

    def onward(self, block):
        return lax.ppermute(block, "dp", self.next)


def join(runs, *work):
    moving = [run.moving() for run in runs]
    moving, work = lax.optimization_barrier((moving, list(work)))
    for run, moved in zip(runs, moving):
        run.land(moved)
    return work[0] if len(work) == 1 else work


class Gathering:
    def __init__(self, ring, block, index):
        self.ring, self.block, self.round = ring, block, 0
        self.rounds = ring.outer if ring.small else 1
        self.at, self.side = index // ring.inner, index % ring.inner
        self.zero = jnp.zeros((), index.dtype)
        self.held = jnp.zeros((ring.outer, ring.inner) + block.shape, block.dtype)

    def send(self):
        ring = self.ring
        self.sent = {}
        if self.round >= self.rounds:
            return self
        if not ring.small:
            self.sent["all"] = gather_small(self.block[None], ring.parts)
            return self
        if ring.inner == 2:
            self.sent["other"] = ring.swap(self.block)
        if self.round < ring.outer - 1:
            self.sent["after"] = ring.onward(self.block)
        return self

    def moving(self):
        return self.sent

    def put(self, value, side):
        slot = lax.rem(self.at - self.round + self.ring.outer, self.ring.outer)
        self.held = lax.dynamic_update_slice(
            self.held, value[None, None], (slot, side) + (self.zero,) * value.ndim
        )

    def land(self, moved):
        if self.round >= self.rounds:
            return
        if "all" in moved:
            self.held = moved["all"]
        else:
            if "other" in moved:
                self.put(moved["other"], 1 - self.side)
            self.put(self.block, self.side)
            self.block = moved.get("after")
        self.round += 1

    def result(self):
        while self.round < self.rounds:
            join([self.send()])
        return self.held.reshape((self.ring.parts,) + self.held.shape[-2:])


class Shared(Gathering):
    def __init__(self, ring, block, index, share):
        super().__init__(ring, block, index)
        self.share = share
        self.far_held = jnp.zeros(self.held.shape[:2] + (share,) + block.shape[1:], block.dtype)
        self.rounds += 1
        self.chunk = None

    def send(self):
        if self.round < self.rounds - 1:
            super().send()
        else:
            self.sent = {}
        if self.chunk is not None and self.round < self.rounds:
            pairs = [(m, m ^ 2) for m in range(lax.axis_size("mp"))]
            self.sent["far"] = lax.ppermute(self.chunk, "mp", pairs)
        return self

    def land(self, moved):
        if self.round >= self.rounds:
            return
        far = moved.pop("far", None)
        if far is not None:
            if not self.ring.small:
                self.far_held = far
            else:
                slot = lax.rem(self.at - self.round + 1 + self.ring.outer, self.ring.outer)
                for number, side in ((0, self.side), (1, 1 - self.side)):
                    self.far_held = lax.dynamic_update_slice(
                        self.far_held,
                        far[number][None, None],
                        (slot, side) + (self.zero,) * (far.ndim - 1),
                    )
        if self.round == self.rounds - 1:
            self.round += 1
            return
        if "all" in moved:
            super().land(moved)
            self.chunk = self.held[:, : self.share]
        else:
            self.chunk = jnp.stack([self.block[: self.share], moved["other"][: self.share]])
            super().land(moved)

    def both(self):
        own = self.result()[:, : self.share]
        return own, self.far_held.reshape(own.shape)


class Scattering:
    def __init__(self, ring, blocks, index):
        self.ring, self.blocks = ring, blocks
        self.at, self.side = index // ring.inner, index % ring.inner
        self.left = ring.outer if ring.small else 1
        self.pending = None

    def send(self):
        ring = self.ring
        self.sent = {}
        if not self.left:
            return self
        self.left -= 1
        if not ring.small:
            self.sent["all"] = scatter_halves(self.blocks, ring.parts)
            return self
        if self.pending is not None:
            self.sent["carried"] = ring.onward(self.pending.astype(BF16))
        first = lax.rem(self.at + self.left, ring.outer) * ring.inner
        self.mine = lax.dynamic_index_in_dim(self.blocks, first + self.side, 0, False)
        if ring.inner == 2:
            given = lax.dynamic_index_in_dim(self.blocks, first + 1 - self.side, 0, False)
            self.sent["other"] = ring.swap(given)
        return self

    def moving(self):
        return self.sent

    def land(self, moved):
        if "all" in moved:
            self.pending = moved["all"]
        if "all" in moved or not moved:
            return
        total = self.mine.astype(F32)
        for value in moved.values():
            total = total + value.astype(F32)
        self.pending = total

    def result(self):
        while self.left:
            join([self.send()])
        return self.pending


def step(runs):
    runs[:] = [run for run in runs if run.round < run.rounds]
    for run in runs:
        run.send()


class Once:
    def __init__(self, arrays, steps):
        self.sent = {}
        count = lax.axis_size("mp")
        for name, array in arrays.items():
            pairs = [(m, m ^ steps) for m in range(count)]
            self.sent[name] = lax.ppermute(array, "mp", pairs)

    def moving(self):
        return self.sent

    def land(self, moved):
        self.got = moved


def in_order(pieces):
    me = lax.axis_index("mp")
    first = pieces[0]
    held = jnp.zeros((len(pieces),) + first.shape, first.dtype)
    zero = jnp.zeros((), me.dtype)
    for key, piece in pieces.items():
        held = lax.dynamic_update_slice(held, piece[None], (me ^ key,) + (zero,) * piece.ndim)
    return held


def scatter_halves(blocks, parts):
    index = lax.axis_index("dp")
    step = parts // 2
    while step:
        upper = (index // step) % 2 == 1
        low, high = blocks[:step], blocks[step:]
        mine, given = jnp.where(upper, high, low), jnp.where(upper, low, high)
        got = lax.ppermute(given.astype(BF16), "dp", [(d, d ^ step) for d in range(parts)])
        blocks = mine.astype(F32) + got.astype(F32)
        step //= 2
    return blocks[0]


def gather_small(values, parts):
    index = lax.axis_index("dp")
    step = 1
    while step < parts:
        other = lax.ppermute(values, "dp", [(d, d ^ step) for d in range(parts)])
        upper = (index // step) % 2 == 1
        values = jnp.where(
            upper, jnp.concatenate([other, values], 0), jnp.concatenate([values, other], 0)
        )
        step *= 2
    return values


def sum_mp(part):
    count = lax.axis_size("mp")
    near = [(m, m ^ 1) for m in range(count)]
    half = part.shape[0] // 2
    side = lax.axis_index("mp") % 2
    low, high = part[:half], part[half:]
    mine, given = jnp.where(side == 0, low, high), jnp.where(side == 0, high, low)
    total = mine.astype(F32) + lax.ppermute(given, "mp", near).astype(F32)
    step = 2
    while step < count:
        total = total.astype(BF16)
        far = [(m, m ^ step) for m in range(count)]
        total = total.astype(F32) + lax.ppermute(total, "mp", far).astype(F32)
        step *= 2
    total = total.astype(BF16)
    other = lax.ppermute(total, "mp", near)
    return jnp.concatenate(
        [jnp.where(side == 0, total, other), jnp.where(side == 0, other, total)], 0
    )


def rope_tables(positions, head_size, repeats):
    half_size = head_size // 2
    frequency = jnp.exp(
        -jnp.log(10000.0) * 2.0 * jnp.arange(half_size, dtype=jnp.float32) / head_size
    )
    frequency = jnp.tile(frequency, 2 * repeats)
    angles = positions.astype(jnp.float32)[:, None] * frequency[None, :]
    return jnp.cos(angles), jnp.sin(angles)


def clip_layout(frames_row, length, frame_tok, clip_slots):
    clip_len = frames_row * frame_tok
    slots = jnp.arange(clip_slots, dtype=jnp.int32)
    clip_end = jnp.sum(
        jnp.where(slots[:, None] >= slots[None, :], clip_len[None, :], 0), 1, dtype=jnp.int32
    )
    clip_start = clip_end - clip_len
    row_index = jnp.arange(length, dtype=jnp.int32)
    segment = jnp.sum(
        (row_index[:, None] >= clip_end[None, :]).astype(jnp.int32), 1, dtype=jnp.int32
    )
    member = segment[:, None] == slots[None, :]
    begin_row = jnp.sum(jnp.where(member, clip_start[None, :], 0), 1, dtype=jnp.int32)
    begin_row = begin_row + jnp.where(segment == clip_slots, clip_end[clip_slots - 1], 0)
    return segment, row_index - begin_row


def condition_rows(steps, cond_width):
    packs, clips = steps.shape
    column = jnp.arange(4 * cond_width, dtype=jnp.int32)
    half_size = cond_width // 2
    k = column // 4
    place = lax.rem(k, half_size).astype(F32)
    frequency = jnp.exp(-jnp.log(10000.0) * place / half_size)
    angles = steps.reshape(-1)[:, None] * frequency[None, :]
    waves = jnp.where((k < half_size)[None, :], jnp.cos(angles), jnp.sin(angles))
    cond = jax.nn.silu(waves).astype(BF16).reshape(packs, 1, clips, 4 * cond_width)
    part = jnp.arange(4, dtype=jnp.int32)
    own = (lax.rem(column, 4)[None, :] == part[:, None])[None, :, None, :]
    return jnp.where(own, cond, jnp.zeros((), BF16)).reshape(packs, 4 * clips, 4 * cond_width)


def dot(left, right):
    return jnp.dot(left, right, preferred_element_type=F32)


def dot_t(left, right):
    return lax.dot_general(left, right, (((1,), (1,)), ((), ())), preferred_element_type=F32)


def t_dot(left, right):
    return lax.dot_general(left, right, (((0,), (0,)), ((), ())), preferred_element_type=F32)


def row_mean(values):
    return jnp.mean(values, -1, keepdims=True)


def per_token(seg, mod_ref, part):
    total = jnp.where(seg == 0, mod_ref[part, 0:1, :], 0.0)
    for clip in range(1, mod_ref.shape[1]):
        total = total + jnp.where(seg == clip, mod_ref[part, clip : clip + 1, :], 0.0)
    return total


def per_clip(seg, values, out_ref):
    for clip in range(out_ref.shape[0]):
        out_ref[clip : clip + 1, :] = jnp.sum(jnp.where(seg == clip, values, 0.0), 0, keepdims=True)


def column_sum(values):
    return jnp.sum(values, 0, keepdims=True)


def rms_back(unit, scale, grad):
    return scale * (grad - unit * row_mean(unit * grad))


def branch_back(grad, branch, gate_tok, gain):
    scale = lax.rsqrt(row_mean(branch * branch) + EPS)
    unit = branch * scale
    opened = jnp.tanh(gate_tok)
    grad_unit = grad * opened
    dgate = grad * unit * gain * (1.0 - opened * opened)
    return rms_back(unit, scale, grad_unit * gain), dgate, column_sum(grad_unit * unit)


def modulate_back(grad, values, gain, scale_tok):
    scale = lax.rsqrt(row_mean(values * values) + EPS)
    unit = values * scale
    grad_unit = grad * unit
    dscale = grad_unit * gain
    dgain = column_sum(grad_unit * (1.0 + scale_tok))
    return rms_back(unit, scale, grad * gain * (1.0 + scale_tok)), dscale, dgain


def head_mean(values):
    width = values.shape[-1]
    rows = lax.broadcasted_iota(jnp.int32, (width, width), 0) // HEAD_DIM
    columns = lax.broadcasted_iota(jnp.int32, (width, width), 1) // HEAD_DIM
    same = jnp.where(rows == columns, 1.0 / HEAD_DIM, 0.0)
    return jnp.dot(values, same, precision=lax.Precision.HIGHEST, preferred_element_type=F32)


def turn(values, sign):
    width = values.shape[-1]
    half = HEAD_DIM // 2
    lane = lax.broadcasted_iota(jnp.int32, values.shape, 1) % HEAD_DIM
    ahead = pltpu.roll(values, width - half, 1)
    behind = pltpu.roll(values, half, 1)
    return jnp.where(lane < half, -sign * ahead, sign * behind)


def head_rms(linear):
    scale = lax.rsqrt(head_mean(linear * linear) + EPS)
    return linear * scale, scale


def head_rms_back(linear, grad, gain):
    unit, scale = head_rms(linear)
    scaled = grad * gain
    return scale * (scaled - unit * head_mean(unit * scaled)), column_sum(grad * unit)


def soft(query, keys, mask):
    scores = dot_t(query, keys) * HEAD_DIM ** (-0.5)
    scores = jnp.where(mask, scores, NEG)
    raised = jnp.exp(scores - jnp.max(scores, -1, keepdims=True))
    return raised / jnp.sum(raised, -1, keepdims=True)


def soft_back(query, keys, values, probs, grad_out):
    grad_probs = dot_t(grad_out, values)
    grad_values = t_dot(probs.astype(BF16), grad_out)
    inner_sum = jnp.sum(probs * grad_probs, -1, keepdims=True)
    grad_scores = (probs * (grad_probs - inner_sum) * HEAD_DIM ** (-0.5)).astype(BF16)
    return dot(grad_scores, keys), t_dot(grad_scores, query), grad_values


def masks(seg_ref, seg_row_ref, key_count, clip_slots):
    seg = seg_ref[...]
    key_clip = lax.broadcasted_iota(jnp.int32, (1, key_count), 1) // (key_count // clip_slots)
    return seg == seg_row_ref[...], (seg == key_clip) | (seg == clip_slots)


class Fetch:
    def __init__(self, held_ref, layout, low, high, into_ref, sems, first):
        self.copies = []
        for number, (d, start, rows, offset) in enumerate(layout.spans(low, high)):
            copy = pltpu.make_async_copy(
                held_ref.at[d, pl.ds(start, rows)],
                into_ref.at[pl.ds(offset, rows)],
                sems.at[first + number],
            )
            copy.start()
            self.copies.append(copy)

    def wait(self):
        for copy in self.copies:
            copy.wait()


def own_rows(block, i, offset):
    row = lax.broadcasted_iota(jnp.int32, block.shape, 0) + i * block.shape[0]
    lane = lax.broadcasted_iota(jnp.int32, block.shape, 1)
    mine = row * block.shape[1] + lane >= offset
    return jnp.where(mine, block.astype(F32), 0.0).astype(BF16)


def block_place(layout, index):
    first = index * layout.size // layout.unit * (layout.unit // layout.width // LANES)
    return jnp.stack([first, layout.offset(index)]).astype(jnp.int32)


def modulation_share(layout, index, rows, low, cond):
    packs, conds, depth = cond.shape
    blocks = layout.used // LANES
    first_block, count = low // LANES, depth // LANES

    def kernel(place_ref, w_ref, cond_ref, out_ref):
        out_ref[...] = jnp.zeros_like(out_ref)

        def body(i, carry):
            g = place_ref[0] + i - first_block

            @pl.when((g >= 0) & (g < count))
            def _():
                weights = w_ref[pl.ds(pl.multiple_of(i * LANES, LANES), LANES), :]
                lanes = pl.ds(pl.multiple_of(g * LANES, LANES), LANES)
                left = cond_ref[:, :, lanes].reshape(packs * conds, LANES)
                out_ref[...] += dot(left, own_rows(weights, i, place_ref[1]))

            return carry

        lax.fori_loop(0, blocks, body, 0)

    out = pl.pallas_call(
        kernel,
        out_shape=jax.ShapeDtypeStruct((packs * conds, layout.width), F32),
        in_specs=[SMEM, VMEM, VMEM],
        out_specs=VMEM,
        compiler_params=params(40),
    )(block_place(layout, index), rows, cond)
    return out.reshape(packs, conds, layout.width)


def text_share(layout, index, rows, low, text):
    groups, packs, key_count, text_cut = text.shape
    width = layout.width
    blocks = layout.used // LANES
    first_block, count = low // LANES, groups * text_cut // LANES
    step_packs = min(8, packs)
    per_cut = text_cut // LANES

    def kernel(place_ref, w_ref, text_ref, out_ref, sum_ref):
        sum_ref[...] = jnp.zeros_like(sum_ref)

        def body(i, carry):
            g = place_ref[0] + i - first_block

            @pl.when((g >= 0) & (g < 2 * count))
            def _():
                weights = w_ref[pl.ds(pl.multiple_of(i * LANES, LANES), LANES), :]
                sub = g % count
                lanes = pl.ds(pl.multiple_of(sub % per_cut * LANES, LANES), LANES)
                left = text_ref[sub // per_cut, :, :, lanes].reshape(-1, LANES)
                sum_ref[g // count] += dot(left, own_rows(weights, i, place_ref[1]))

            return carry

        lax.fori_loop(0, blocks, body, 0)
        for kind in range(2):
            out_ref[:, :, kind * width : (kind + 1) * width] = (
                sum_ref[kind].astype(BF16).reshape(step_packs, key_count, width)
            )

    return pl.pallas_call(
        kernel,
        grid=(packs // step_packs,),
        out_shape=jax.ShapeDtypeStruct((packs, key_count, 2 * width), BF16),
        in_specs=[
            SMEM,
            pl.BlockSpec(rows.shape, lambda s: (0, 0), pipeline_mode=pl.Buffered(1)),
            pl.BlockSpec(
                (groups, step_packs, key_count, text_cut),
                lambda s: (0, s, 0, 0),
                pipeline_mode=pl.Buffered(1),
            ),
        ],
        out_specs=pl.BlockSpec((step_packs, key_count, 2 * width), lambda s: (s, 0, 0)),
        scratch_shapes=[pltpu.VMEM((2, step_packs * key_count, width), F32)],
        compiler_params=params(48),
    )(block_place(layout, index), rows, text)


def attention_inputs(layout, held, tokens, seg, mods, norms, gains, cosine, sine):
    length, depth = tokens.shape
    width = layout.width
    count = len(layout.spans(0, 3 * depth))

    def kernel(
        held_ref, x_ref, seg_ref, mod_ref, norm_ref, gain_ref, cos_ref, sin_ref,
        normed_ref, q_ref, k_ref, v_ref, q_lin_ref, k_lin_ref, w_ref, sems,
    ):
        fetch = Fetch(held_ref, layout, 0, 3 * depth, w_ref, sems, 0)
        x = x_ref[...].astype(F32)
        unit = x * lax.rsqrt(row_mean(x * x) + EPS)
        normed = unit * norm_ref[0:1, :] * (1.0 + per_token(seg_ref[...], mod_ref, 0))
        normed = normed.astype(BF16)
        normed_ref[...] = normed
        fetch.wait()
        cosine, sine = cos_ref[...], sin_ref[...]
        for place, (lin_ref, out_ref) in enumerate(((q_lin_ref, q_ref), (k_lin_ref, k_ref))):
            linear = dot(normed, w_ref[place * depth : (place + 1) * depth, :])
            lin_ref[...] = linear
            rms = head_rms(linear)[0] * gain_ref[place : place + 1, :]
            out_ref[...] = (rms * cosine + turn(rms, 1.0) * sine).astype(BF16)
        v_ref[...] = dot(normed, w_ref[2 * depth : 3 * depth, :]).astype(BF16)

    low, full = (jax.ShapeDtypeStruct((length, width), t) for t in (BF16, F32))
    return pl.pallas_call(
        kernel,
        out_shape=(jax.ShapeDtypeStruct((length, depth), BF16), low, low, low, full, full),
        in_specs=[ANY] + [VMEM] * 7,
        out_specs=(VMEM,) * 6,
        scratch_shapes=[
            pltpu.VMEM((3 * depth, width), BF16),
            pltpu.SemaphoreType.DMA((count,)),
        ],
        compiler_params=params(48),
    )(held, tokens, seg, mods, norms, gains, cosine, sine)


def attention_forward(query, key, value, text_lin, seg, seg_row, gains, w_out, clips):
    length, width = query.shape
    key_count = text_lin.shape[0]
    model_width = w_out.shape[1]

    def kernel(
        q_ref, k_ref, v_ref, lin_ref, seg_ref, row_ref, gain_ref, w_ref,
        mixed_ref, cross_ref, part_ref, tk_lin_ref, tk_ref, tv_ref,
    ):
        linear = lin_ref[:, 0:width]
        tk_lin_ref[...] = linear
        tk_ref[...] = (head_rms(linear)[0] * gain_ref[2:3, :]).astype(BF16)
        tv_ref[...] = lin_ref[:, width : 2 * width].astype(BF16)
        own_mask, cross_mask = masks(seg_ref, row_ref, key_count, clips)
        own = []
        for head in range(width // HEAD_DIM):
            at = slice(head * HEAD_DIM, (head + 1) * HEAD_DIM)
            probs = soft(q_ref[:, at], k_ref[:, at], own_mask)
            own.append(dot(probs.astype(BF16), v_ref[:, at]))
            probs = soft(q_ref[:, at], tk_ref[:, at], cross_mask)
            cross_ref[:, at] = dot(probs.astype(BF16), tv_ref[:, at])
        mixed = jnp.concatenate(own, 1) + jnp.tanh(gain_ref[3:4, :]) * cross_ref[...]
        mixed = mixed.astype(BF16)
        mixed_ref[...] = mixed
        part_ref[...] = dot(mixed, w_ref[...]).astype(BF16)

    return pl.pallas_call(
        kernel,
        out_shape=(
            jax.ShapeDtypeStruct((length, width), BF16),
            jax.ShapeDtypeStruct((length, width), F32),
            jax.ShapeDtypeStruct((length, model_width), BF16),
            jax.ShapeDtypeStruct((key_count, width), F32),
            jax.ShapeDtypeStruct((key_count, width), BF16),
            jax.ShapeDtypeStruct((key_count, width), BF16),
        ),
        in_specs=[VMEM] * 8,
        out_specs=(VMEM,) * 6,
        compiler_params=params(48),
    )(query, key, value, text_lin, seg, seg_row, gains, w_out)


def ffn_forward(layout, held, tokens, attn_out, seg, mods, norms, w_down):
    length, depth = tokens.shape
    width = layout.width
    counts = [len(layout.spans(i * depth, (i + 1) * depth)) for i in range(2)]

    def kernel(
        held_ref, x_ref, branch_ref, seg_ref, mod_ref, norm_ref, down_hbm,
        middle_ref, ffn_in_ref, gate_ref, up_ref, hidden_ref, part_ref,
        wg_ref, wu_ref, wd_ref, sems,
    ):
        for_gate = Fetch(held_ref, layout, 0, depth, wg_ref, sems, 0)
        for_up = Fetch(held_ref, layout, depth, 2 * depth, wu_ref, sems, counts[0])
        for_down = pltpu.make_async_copy(down_hbm, wd_ref, sems.at[sum(counts)])
        for_down.start()
        seg = seg_ref[...]
        branch = branch_ref[...].astype(F32)
        unit = branch * lax.rsqrt(row_mean(branch * branch) + EPS)
        opened = jnp.tanh(per_token(seg, mod_ref, 1))
        middle = x_ref[...].astype(F32) + opened * unit * norm_ref[1:2, :]
        middle_ref[...] = middle
        unit = middle * lax.rsqrt(row_mean(middle * middle) + EPS)
        ffn_in = (unit * norm_ref[2:3, :] * (1.0 + per_token(seg, mod_ref, 2))).astype(BF16)
        ffn_in_ref[...] = ffn_in
        for_gate.wait()
        gate = dot(ffn_in, wg_ref[...])
        gate_ref[...] = gate
        for_up.wait()
        up = dot(ffn_in, wu_ref[...])
        up_ref[...] = up
        hidden = (jax.nn.silu(gate) * up).astype(BF16)
        hidden_ref[...] = hidden
        for_down.wait()
        part_ref[...] = dot(hidden, wd_ref[...]).astype(BF16)

    def like(columns, kind):
        return jax.ShapeDtypeStruct((length, columns), kind)

    return pl.pallas_call(
        kernel,
        out_shape=(
            like(depth, F32),
            like(depth, BF16),
            like(width, F32),
            like(width, F32),
            like(width, BF16),
            like(depth, BF16),
        ),
        in_specs=[ANY] + [VMEM] * 5 + [ANY],
        out_specs=(VMEM,) * 6,
        scratch_shapes=[
            pltpu.VMEM((depth, width), BF16),
            pltpu.VMEM((depth, width), BF16),
            pltpu.VMEM((width, depth), BF16),
            pltpu.SemaphoreType.DMA((sum(counts) + 1,)),
        ],
        compiler_params=params(56),
    )(held, tokens, attn_out, seg, mods, norms, w_down)


def ffn_backward(
    layout, held, middle, ffn_out, cotangent, ffn_in, gate, up, hidden, seg, mods, norms, w_down
):
    length, depth = middle.shape
    width = layout.width
    clips = mods.shape[1]
    counts = [len(layout.spans(i * depth, (i + 1) * depth)) for i in range(2)]
    cut = 256

    def kernel(
        held_ref, middle_ref, branch_ref, cot_ref, in_ref, gate_ref, up_ref, hidden_ref,
        seg_ref, mod_ref, norm_ref, down_hbm,
        output_ref, part_ref, gg_ref, gu_ref, gd_ref, dmod_ref, dgain_ref,
        wg_ref, wu_ref, wd_ref, sems,
    ):
        for_down = pltpu.make_async_copy(down_hbm, wd_ref, sems.at[sum(counts)])
        for_down.start()
        for_gate = Fetch(held_ref, layout, 0, depth, wg_ref, sems, 0)
        for_up = Fetch(held_ref, layout, depth, 2 * depth, wu_ref, sems, counts[0])
        seg = seg_ref[...]
        branch = branch_ref[...].astype(F32)
        gate_tok = per_token(seg, mod_ref, 3)
        gain = norm_ref[3:4, :]
        unit = branch * lax.rsqrt(row_mean(branch * branch) + EPS)
        output_ref[...] = (middle_ref[...] + jnp.tanh(gate_tok) * unit * gain).astype(BF16)
        dbranch, dgate_tok, dgain = branch_back(cot_ref[...].astype(F32), branch, gate_tok, gain)
        per_clip(seg, dgate_tok, dmod_ref)
        dgain_ref[...] = dgain
        dlow = dbranch.astype(BF16)
        for_down.wait()
        dhidden = dot_t(dlow, wd_ref[...])
        gate, up = gate_ref[...], up_ref[...]
        sigma = jax.nn.sigmoid(gate)
        dup = (dhidden * gate * sigma).astype(BF16)
        dgate = (dhidden * up * (sigma * (1.0 + gate * (1.0 - sigma)))).astype(BF16)
        for start in range(0, width, cut):
            hidden_t = hidden_ref[:, start : start + cut].T
            gd_ref[start : start + cut, :] = dot(hidden_t, dlow).astype(BF16)
        for_gate.wait()
        part = dot_t(dgate, wg_ref[...])
        for_up.wait()
        part_ref[...] = (part + dot_t(dup, wu_ref[...])).astype(BF16)
        for start in range(0, depth, cut):
            in_t = in_ref[:, start : start + cut].T
            gg_ref[start : start + cut, :] = dot(in_t, dgate).astype(BF16)
            gu_ref[start : start + cut, :] = dot(in_t, dup).astype(BF16)

    def like(rows, columns, kind):
        return jax.ShapeDtypeStruct((rows, columns), kind)

    return pl.pallas_call(
        kernel,
        out_shape=(
            like(length, depth, BF16),
            like(length, depth, BF16),
            like(depth, width, BF16),
            like(depth, width, BF16),
            like(width, depth, BF16),
            like(clips, depth, F32),
            like(1, depth, F32),
        ),
        in_specs=[ANY] + [VMEM] * 10 + [ANY],
        out_specs=(VMEM,) * 7,
        scratch_shapes=[
            pltpu.VMEM((depth, width), BF16),
            pltpu.VMEM((depth, width), BF16),
            pltpu.VMEM((width, depth), BF16),
            pltpu.SemaphoreType.DMA((sum(counts) + 1,)),
        ],
        compiler_params=params(56),
    )(
        held, middle, ffn_out, cotangent, ffn_in, gate, up, hidden, seg, mods, norms, w_down
    )


def branch_backward(dffn_in, middle, cotangent, attn_out, seg, mods, norms, w_out):
    length, depth = middle.shape
    width = w_out.shape[0]
    clips = mods.shape[1]

    def kernel(
        din_ref, middle_ref, cot_ref, branch_ref, seg_ref, mod_ref, norm_ref, wo_ref,
        dmiddle_ref, dlow_ref, dmixed_ref, dscale_ref, dgate_ref, dnorm_ref,
    ):
        seg = seg_ref[...]
        dpre, dscale, dgain = modulate_back(
            din_ref[...].astype(F32), middle_ref[...], norm_ref[2:3, :], per_token(seg, mod_ref, 2)
        )
        per_clip(seg, dscale, dscale_ref)
        dnorm_ref[1:2, :] = dgain
        dmiddle = cot_ref[...].astype(F32) + dpre
        dmiddle_ref[...] = dmiddle
        dbranch, dgate_tok, dgain = branch_back(
            dmiddle, branch_ref[...].astype(F32), per_token(seg, mod_ref, 1), norm_ref[1:2, :]
        )
        per_clip(seg, dgate_tok, dgate_ref)
        dnorm_ref[0:1, :] = dgain
        dlow = dbranch.astype(BF16)
        dlow_ref[...] = dlow
        dmixed_ref[...] = dot_t(dlow, wo_ref[...]).astype(BF16)

    def like(rows, columns, kind):
        return jax.ShapeDtypeStruct((rows, columns), kind)

    return pl.pallas_call(
        kernel,
        out_shape=(
            like(length, depth, F32),
            like(length, depth, BF16),
            like(length, width, BF16),
            like(clips, depth, F32),
            like(clips, depth, F32),
            like(2, depth, F32),
        ),
        in_specs=[VMEM] * 8,
        out_specs=(VMEM,) * 6,
        compiler_params=params(48),
    )(dffn_in, middle, cotangent, attn_out, seg, mods, norms, w_out)


def attention_backward(
    layout, held, dmixed, query, key, value, q_lin, k_lin,
    text_key, text_value, tk_lin, cross, seg, seg_row, gains, cosine, sine, clips,
):
    length, width = query.shape
    depth = layout.width * lax.axis_size("mp")
    key_count = text_key.shape[0]
    count = len(layout.spans(0, 3 * depth))

    def kernel(
        held_ref, dmixed_ref, q_ref, k_ref, v_ref, q_lin_ref, k_lin_ref, tk_ref, tv_ref,
        tk_lin_ref, cross_ref, seg_ref, row_ref, gain_ref, cos_ref, sin_ref,
        part_ref, acts_ref, dgains_ref, w_ref, dq_ref, dk_ref, dv_ref, dtk_ref, dtv_ref, sems,
    ):
        fetch = Fetch(held_ref, layout, 0, 3 * depth, w_ref, sems, 0)
        opened = jnp.tanh(gain_ref[3:4, :])
        dmixed = dmixed_ref[...]
        wide = dmixed.astype(F32)
        dgains_ref[3:4, :] = column_sum(wide * cross_ref[...]) * (1.0 - opened * opened)
        dcross = (wide * opened).astype(BF16)
        own_mask, cross_mask = masks(seg_ref, row_ref, key_count, clips)
        for head in range(width // HEAD_DIM):
            at = slice(head * HEAD_DIM, (head + 1) * HEAD_DIM)
            query = q_ref[:, at]
            probs = soft(query, k_ref[:, at], own_mask)
            dq, dk, dv = soft_back(query, k_ref[:, at], v_ref[:, at], probs, dmixed[:, at])
            probs = soft(query, tk_ref[:, at], cross_mask)
            dq_cross, dtk, dtv = soft_back(
                query, tk_ref[:, at], tv_ref[:, at], probs, dcross[:, at]
            )
            dq_ref[:, at] = dq + dq_cross
            dk_ref[:, at] = dk
            dv_ref[:, at] = dv
            dtk_ref[:, at] = dtk
            dtv_ref[:, at] = dtv
        cosine, sine = cos_ref[...], sin_ref[...]
        lows = []
        for place, (grad_ref, lin_ref) in enumerate(((dq_ref, q_lin_ref), (dk_ref, k_lin_ref))):
            grad = grad_ref[...]
            grad = grad * cosine + turn(grad * sine, -1.0)
            dlin, dgain = head_rms_back(lin_ref[...], grad, gain_ref[place : place + 1, :])
            dgains_ref[place : place + 1, :] = dgain
            lows.append(dlin.astype(BF16))
        lows.append(dv_ref[...].astype(BF16))
        dlin, dgain = head_rms_back(tk_lin_ref[...], dtk_ref[...], gain_ref[2:3, :])
        dgains_ref[2:3, :] = dgain
        for place in range(3):
            acts_ref[place * length : (place + 1) * length, :] = lows[place]
        acts_ref[3 * length : 3 * length + key_count, :] = dlin.astype(BF16)
        acts_ref[3 * length + key_count :, :] = dtv_ref[...].astype(BF16)
        fetch.wait()
        part = dot_t(lows[0], w_ref[0:depth, :])
        part = part + dot_t(lows[1], w_ref[depth : 2 * depth, :])
        part_ref[...] = (part + dot_t(lows[2], w_ref[2 * depth : 3 * depth, :])).astype(BF16)

    return pl.pallas_call(
        kernel,
        out_shape=(
            jax.ShapeDtypeStruct((length, depth), BF16),
            jax.ShapeDtypeStruct((3 * length + 2 * key_count, width), BF16),
            jax.ShapeDtypeStruct((4, width), F32),
        ),
        in_specs=[ANY] + [VMEM] * 15,
        out_specs=(VMEM,) * 3,
        scratch_shapes=[pltpu.VMEM((3 * depth, width), BF16)]
        + [pltpu.VMEM((length, width), F32)] * 3
        + [pltpu.VMEM((key_count, width), F32)] * 2
        + [pltpu.SemaphoreType.DMA((count,))],
        compiler_params=params(56),
    )(
        held, dmixed, query, key, value, q_lin, k_lin, text_key, text_value, tk_lin, cross, seg,
        seg_row, gains, cosine, sine,
    )


def shard_gradient(layout, index, normed, dattn, text, mixed, acts, ends, cond):
    groups, packs, length, width = normed.shape
    key_count, text_cut = text.shape[2:]
    conds = cond.shape[1]
    cut = LANES
    step_packs = min(8, packs)
    blocks = layout.used // cut
    first = (index * layout.size // layout.unit * (layout.unit // width // cut)).astype(jnp.int32)
    per_in = groups * width // cut
    per_text = groups * text_cut // cut
    per_cond = cond.shape[2] // cut
    kinds = [3 * per_in, 4 * per_in, 4 * per_in + 2 * per_text, 4 * per_in + 2 * per_text + per_cond]

    def kernel(first_ref, n_ref, d_ref, t_ref, m_ref, a_ref, e_ref, c_ref, out_ref, woven_ref):
        @pl.when(pl.program_id(0) == 0)
        def _():
            out_ref[...] = jnp.zeros_like(out_ref)

        def tall(block):
            return block.reshape(-1, block.shape[-1])

        def body(i, carry):
            g = first_ref[0] + i
            start = pl.multiple_of(i * cut, cut)
            rows = pl.ds(start, cut)

            @pl.when(g < kinds[0])
            def _():
                sub = g % per_in
                lanes = pl.ds(pl.multiple_of(sub % (width // cut) * cut, cut), cut)
                grads = pl.ds(pl.multiple_of(g // per_in * length, length), length)
                left = tall(n_ref[sub // (width // cut), :, :, lanes])
                out_ref[rows, :] += t_dot(left, tall(a_ref[:, grads, :]))

            @pl.when((g >= kinds[0]) & (g < kinds[1]))
            def _():
                each = cut // groups
                at = (g - kinds[0]) * each
                lanes = pl.ds(pl.multiple_of(at // LANES * LANES, LANES), LANES)
                slab = tall(m_ref[:, length : 2 * length, lanes]).astype(F32)
                slab = pltpu.roll(slab, (LANES - at % LANES) % LANES, 1)
                left = slab.T[0:each, :].astype(BF16)
                for part in range(groups):
                    value = dot(left, tall(d_ref[part]))
                    for j in range(width // LANES):
                        woven_ref[j, pl.ds(part, each, stride=groups), :] = value[
                            :, j * LANES : (j + 1) * LANES
                        ]
                woven = [woven_ref[j] for j in range(width // LANES)]
                out_ref[rows, :] += jnp.concatenate(woven, 1)

            @pl.when((g >= kinds[1]) & (g < kinds[2]))
            def _():
                sub = (g - kinds[1]) % per_text
                lanes = pl.ds(pl.multiple_of(sub % (text_cut // cut) * cut, cut), cut)
                at = 3 * length + (g - kinds[1]) // per_text * key_count
                grads = pl.ds(pl.multiple_of(at, key_count), key_count)
                left = tall(t_ref[sub // (text_cut // cut), :, :, lanes])
                out_ref[rows, :] += t_dot(left, tall(a_ref[:, grads, :]))

            @pl.when((g >= kinds[2]) & (g < kinds[3]))
            def _():
                lanes = pl.ds(pl.multiple_of((g - kinds[2]) * cut, cut), cut)
                left = tall(c_ref[:, :, lanes])
                out_ref[rows, :] += t_dot(left, tall(e_ref[:, 0:conds, :]))

            @pl.when(g == kinds[3])
            def _():
                total = jnp.sum(e_ref[:, conds : conds + 16, :].astype(F32), 0)
                out_ref[pl.ds(start, 16), :] += total

            return carry

        lax.fori_loop(0, blocks, body, 0)

    def spec(array, packs_dim):
        shape = list(array.shape)
        shape[packs_dim] = step_packs
        return pl.BlockSpec(
            tuple(shape),
            lambda s: tuple(s if d == packs_dim else 0 for d in range(len(shape))),
            pipeline_mode=pl.Buffered(1),
        )

    operands = [(normed, 1), (dattn, 1), (text, 1), (mixed, 0), (acts, 0), (ends, 0), (cond, 0)]
    return pl.pallas_call(
        kernel,
        grid=(packs // step_packs,),
        out_shape=jax.ShapeDtypeStruct((layout.used, width), F32),
        in_specs=[SMEM] + [spec(*o) for o in operands],
        out_specs=pl.BlockSpec((layout.used, width), lambda s: (0, 0)),
        scratch_shapes=[pltpu.VMEM((width // LANES, cut, LANES), F32)],
        compiler_params=params(58),
    )(first[None], *[o[0] for o in operands])


def input_backward(dnormed, tokens, dmiddle, seg, mods, norms):
    length, depth = tokens.shape
    clips = mods.shape[1]

    def kernel(d_ref, x_ref, dmiddle_ref, seg_ref, mod_ref, norm_ref, out_ref, dmod_ref, dgain_ref):
        seg = seg_ref[...]
        dpre, dscale, dgain = modulate_back(
            d_ref[...].astype(F32),
            x_ref[...].astype(F32),
            norm_ref[0:1, :],
            per_token(seg, mod_ref, 0),
        )
        per_clip(seg, dscale, dmod_ref)
        dgain_ref[...] = dgain
        out_ref[...] = (dmiddle_ref[...] + dpre).astype(BF16)

    return pl.pallas_call(
        kernel,
        out_shape=(
            jax.ShapeDtypeStruct((length, depth), BF16),
            jax.ShapeDtypeStruct((clips, depth), F32),
            jax.ShapeDtypeStruct((1, depth), F32),
        ),
        in_specs=[VMEM] * 6,
        out_specs=(VMEM,) * 3,
        compiler_params=params(32),
    )(dnormed, tokens, dmiddle, seg, mods, norms)


def local(
    tokens_in,
    text_feats,
    frame_counts,
    time_steps,
    attn_master,
    attn_first,
    attn_second,
    ffn_master,
    ffn_first,
    ffn_second,
    norm_master,
    norm_first,
    norm_second,
    step_count,
    cotangent,
):
    parts, index = lax.axis_size("dp"), lax.axis_index("dp")
    length, model_width = tokens_in.shape
    width = model_width // lax.axis_size("mp")
    clip_slots, text_len, text_width = text_feats.shape[1:]
    key_count = clip_slots * text_len
    ring = Ring(parts)
    hidden_width = ffn_master.shape[1] * parts // (3 * model_width)
    attn_lay = Layout(attn_master.shape[1] * parts, width, parts, LANES)
    ffn_lay = Layout(ffn_master.shape[1] * parts, hidden_width, parts, TILE)
    norm_size = norm_master.shape[0]
    norm_rows = -(-norm_size // width)

    def as_rows(flat):
        flat = jnp.pad(flat, ((0, 0), (0, TILE * width - norm_size)))
        return flat.reshape(flat.shape[0], TILE, width)

    segment, positions = clip_layout(frame_counts[0], length, FRAME_TOK, clip_slots)
    seg, seg_row = segment[:, None], segment[None, :]
    cosine, sine = rope_tables(positions, HEAD_DIM, width // HEAD_DIM)
    rank = lax.axis_index("mp")

    def own_cut(values):
        size = values.shape[1] // lax.axis_size("mp")
        return lax.dynamic_slice_in_dim(values, rank * size, size, 1)

    text_rows = text_feats[0].reshape(key_count, text_width)

    sizes = [model_width] * 4 + [text_width, text_width, 4 * COND, 4]
    starts = [sum(sizes[:i]) for i in range(len(sizes) + 1)]
    attn_rows = to_rows(attn_lay, attn_master, index)
    ffn_piece = to_rows(ffn_lay, ffn_master, index)
    pieces = Pieces(attn_lay, starts[4], ring)
    digits = jnp.stack([time_steps[0] // 32, time_steps[0] % 32]).astype(BF16)
    near_text = own_cut(text_rows)
    digits = jnp.pad(digits, ((0, TILE - 2), (0, near_text.shape[1] - clip_slots)))
    text_run = Shared(ring, jnp.concatenate([near_text, digits], 0), index, key_count)
    last = starts[7] - attn_lay.base[parts - 1]
    pieces.send(attn_rows)
    for _ in range(3):
        join([text_run.send()])
    cosine, sine, ffn_piece = join([pieces, text_run.send()], cosine, sine, ffn_piece)
    attn_run = Gathering(
        ring,
        jnp.concatenate(
            [
                pieces.piece(index),
                as_rows(norm_master[None])[0].astype(BF16),
                attn_rows[last : last + TILE],
            ],
            0,
        ),
        index,
    )
    ffn_run = Gathering(ring, ffn_piece, index)
    attn_run.send()
    join([text_run.send()])
    text_own, text_far = text_run.both()
    digits = text_run.result()[:, key_count : key_count + 2, :clip_slots].astype(F32)
    cond_all = condition_rows(digits[:, 0] * 32.0 + digits[:, 1], COND)
    near = Once({"own": text_own, "far": text_far}, 1)
    mod_share = join(
        [attn_run, near],
        modulation_share(attn_lay, index, attn_rows, starts[6], cond_all),
    )
    attn_run.send()
    ffn_run.send()
    text_four = in_order({0: text_own, 2: text_far, 1: near.got["own"], 3: near.got["far"]})
    text_sum = Scattering(
        ring, text_share(attn_lay, index, attn_rows, starts[4], text_four), index
    )
    text_four = join([attn_run, ffn_run, text_sum.send()], text_four)
    attn_run.send()
    ffn_run.send()
    mod_local = lax.all_to_all(mod_share, "dp", 0, 0).sum(0)
    mods = join(
        [attn_run, ffn_run, text_sum.send()],
        lax.all_gather(mod_local.reshape(4, clip_slots, width), "mp", axis=2, tiled=True),
    )
    attn_run.send()
    ffn_run.send()
    join([text_sum.send()])
    join([attn_run, ffn_run, text_sum.send()])
    attn_all = attn_run.result()
    text_lin = text_sum.result()
    ffn_run.send()
    w_out = pieces.pick(attn_all, starts[3], starts[4]).reshape(width, model_width)
    gains = attn_all[parts - 1, pieces.rows + TILE : pieces.rows + TILE + 4].astype(F32)
    norm_flat = attn_all[:, pieces.rows : pieces.rows + norm_rows].reshape(parts, -1)
    norms = norm_flat[:, :norm_size].astype(F32).reshape(4, model_width)
    normed, query, key, value, q_lin, k_lin = attention_inputs(
        pieces, attn_all, tokens_in, seg, mods, norms, gains, cosine, sine
    )
    mixed, cross, attn_part, tk_lin, text_key, text_value = attention_forward(
        query, key, value, text_lin, seg, seg_row, gains, w_out, clip_slots
    )
    attn_out = join([ffn_run], sum_mp(attn_part))
    ffn_all = ffn_run.result()

    ffn_all, near_in = join([], ffn_all, jnp.concatenate([own_cut(normed), mixed], 0))
    w_down = ffn_lay.pick(ffn_all, 2 * model_width, 3 * model_width).reshape(
        hidden_width, model_width
    )
    in_run = Shared(ring, near_in, index, length)
    early = [in_run.send()]
    middle, ffn_in, gate, up, hidden, ffn_part = join(
        early,
        *ffn_forward(ffn_lay, ffn_all, tokens_in, attn_out, seg, mods, norms, w_down),
    )
    step(early)
    ffn_out = join(early, sum_mp(ffn_part))
    step(early)
    output, dffn_part, g_gate, g_up, g_down, dmod_gate_ffn, dnorm_four = join(
        early,
        *ffn_backward(
            ffn_lay,
            ffn_all,
            middle,
            ffn_out,
            cotangent,
            ffn_in,
            gate,
            up,
            hidden,
            seg,
            mods,
            norms,
            w_down,
        ),
    )
    ffn_grads = ffn_lay.cut([g_gate, g_up, g_down.reshape(model_width, hidden_width)])
    ffn_run = Scattering(ring, ffn_grads, index)
    step(early)
    (
        dmiddle,
        dattn,
        dmixed,
        dmod_scale_ffn,
        dmod_gate_attn,
        dnorm_mid,
    ) = join(
        early + [ffn_run.send()],
        *branch_backward(
            sum_mp(dffn_part), middle, cotangent, attn_out, seg, mods, norms, w_out
        ),
    )
    step(early)
    dattn_run = Shared(ring, own_cut(dattn), index, length)
    ffn_run.send()
    join([dattn_run.send()])
    dnormed_part, acts, gain_grads = join(
        [ffn_run, dattn_run.send()] + early,
        *attention_backward(
            pieces,
            attn_all,
            dmixed,
            query,
            key,
            value,
            q_lin,
            k_lin,
            text_key,
            text_value,
            tk_lin,
            cross,
            seg,
            seg_row,
            gains,
            cosine,
            sine,
            clip_slots,
        ),
    )
    acts_run = Gathering(ring, acts, index)
    in_own, in_far = in_run.both()
    ffn_run.send()
    acts_run.send()
    join([dattn_run.send()])
    dattn_run.send()
    dnormed = join([ffn_run, acts_run, dattn_run], sum_mp(dnormed_part))
    near = Once({"own": in_own, "far": in_far}, 1)
    input_grad, dmod_scale_attn, dnorm_one = join(
        [ffn_run.send(), acts_run.send(), dattn_run.send(), near],
        *input_backward(dnormed, tokens_in, dmiddle, seg, mods, norms),
    )
    dmods = jnp.concatenate([dmod_scale_attn, dmod_gate_attn, dmod_scale_ffn, dmod_gate_ffn], 0)
    norm_grads = jnp.concatenate([dnorm_one, dnorm_mid, dnorm_four], 0)
    ends = jnp.concatenate(
        [
            own_cut(dmods),
            jnp.pad(gain_grads, ((0, TILE - 4), (0, 0))),
            norm_grads.reshape(-1, width),
        ],
        0,
    ).astype(BF16)
    normed_four = in_order({0: in_own, 2: in_far, 1: near.got["own"], 3: near.got["far"]})
    dattn_own, dattn_far = dattn_run.both()
    near = Once({"own": dattn_own, "far": dattn_far}, 1)
    ends_all, ffn_shard, normed_four = join(
        [acts_run.send(), near],
        gather_small(ends[None], parts),
        to_flat(ffn_lay, ffn_run.result(), index),
        normed_four,
    )
    dattn_four = in_order(
        {0: dattn_own, 2: dattn_far, 1: near.got["own"], 3: near.got["far"]}
    )
    step_value = step_count[0].astype(F32)
    dattn_four, *ffn_result = join(
        [acts_run.send()],
        dattn_four,
        *adamw_flat(ffn_lay, ffn_master, ffn_first, ffn_second, ffn_shard, step_value, RATE),
    )
    attn_sum = shard_gradient(
        attn_lay,
        index,
        normed_four,
        dattn_four,
        text_four,
        in_run.result(),
        acts_run.result(),
        ends_all,
        cond_all,
    )
    attn_shard = to_flat(attn_lay, attn_sum, index)
    norm_sum = ends_all[:, 2 * TILE :].astype(F32).sum(0).reshape(-1)
    norm_shard = lax.dynamic_slice_in_dim(norm_sum, index * norm_size, norm_size, 0)
    attn_result = adamw_flat(
        attn_lay, attn_master, attn_first, attn_second, attn_shard, step_value, RATE
    )
    norm_result = adamw(norm_master, norm_first, norm_second, norm_shard, step_value, RATE_NORM)
    return (
        (output, input_grad)
        + tuple(attn_result)
        + tuple(ffn_result)
        + norm_result
        + (gain_grads[3:4],)
    )


def solution(mesh):
    tokens, flat, norm = P("dp", None), P("mp", "dp"), P("dp")
    return jax.shard_map(
        local,
        mesh=mesh,
        in_specs=(tokens, P("dp", None, None, None), tokens, tokens)
        + (flat,) * 6
        + (norm,) * 3
        + (P(), tokens),
        out_specs=(tokens,) * 2 + (flat,) * 10 + (norm,) * 5 + (P("dp", "mp"),),
        check_vma=False,
    )
```

```python
import functools
import math

import jax
import jax.numpy as jnp
from jax import lax
from jax.experimental import pallas as pl
from jax.experimental.pallas import tpu as pltpu
from jax.sharding import PartitionSpec as P

HEAD_DIM = 64
COND = 1024
FRAME_TOK = 8
LANES = 128
TILE = 16

EPS = 1e-06
NEG = -1e30
BETA_ONE = 0.9
BETA_TWO = 0.95
RATE = 0.03
RATE_NORM = 0.3
DECAY = 0.1
ADAM_EPS = 1e-08

F32 = jnp.float32
BF16 = jnp.bfloat16
VMEM = pl.BlockSpec(memory_space=pltpu.VMEM)
SMEM = pl.BlockSpec(memory_space=pltpu.SMEM)
ANY = pl.BlockSpec(memory_space=pl.ANY)


def params(mib):
    return pltpu.CompilerParams(vmem_limit_bytes=mib << 20)


def round_up(value, unit):
    return -(-value // unit) * unit


class Layout:
    def __init__(self, total, width, parts, tile, spare=0):
        self.total, self.width, self.parts, self.spare = total, width, parts, spare
        self.unit = tile * width
        self.size = total // parts
        self.base = [d * self.size // self.unit * tile for d in range(parts)] + [
            round_up(-(-total // width), tile)
        ]
        self.off = [d * self.size - self.base[d] * width for d in range(parts)]
        self.used = round_up(max(-(-(o + self.size) // width) for o in self.off), tile)
        self.rows = self.used + spare
        self.lanes = width // LANES
        self.edge = round_up(max(self.off), TILE * LANES)

    def offset(self, index):
        return (index * self.size) % self.unit

    def spans(self, low, high):
        found = []
        for d in range(self.parts):
            first, last = max(low, self.base[d]), min(high, self.base[d + 1])
            if first < last:
                found.append((d, first - self.base[d], last - first, first - low))
        return found

    def pick(self, held, low, high):
        found = [held[d, first : first + rows] for d, first, rows, _ in self.spans(low, high)]
        return found[0] if len(found) == 1 else jnp.concatenate(found, 0)

    def cut(self, matrices, spares=None):
        short = self.base[self.parts - 1] + self.used - sum(m.shape[0] for m in matrices)
        if short > 0:
            matrices = matrices + [jnp.zeros((short, self.width), matrices[0].dtype)]
        whole = jnp.concatenate(matrices, 0)
        if spares is None and self.used * self.parts == whole.shape[0]:
            return whole.reshape(self.parts, self.used, self.width)
        pieces = [whole[b : b + self.used] for b in self.base[: self.parts]]
        if spares is not None:
            pieces = [jnp.concatenate([p, spares[d]], 0) for d, p in enumerate(pieces)]
        return jnp.stack(pieces)


class Pieces:
    def __init__(self, layout, high, ring):
        self.width = layout.width
        parts = layout.parts
        self.rows = round_up(-(-high // parts), LANES)
        self.holders = sum(base < high for base in layout.base[:parts])
        free = list(range(self.holders, parts))
        self.where, self.pairs = [], {}
        for d in range(self.holders):
            last = min(layout.base[d + 1], high)
            for number, low in enumerate(range(layout.base[d], last, self.rows)):
                owner = d
                if number:
                    near = [f for f in free if (f - d) % ring.inner == 0] or free
                    owner = near[-1]
                    free.remove(owner)
                    self.pairs.setdefault(number, []).append((d, owner))
                self.where.append((low, min(low + self.rows, last), owner))

    def send(self, block):
        self.first = block[: self.rows]
        self.sent = {
            number: lax.ppermute(
                block[number * self.rows : (number + 1) * self.rows], "dp", pairs
            )
            for number, pairs in self.pairs.items()
        }
        return self

    def moving(self):
        return self.sent

    def land(self, moved):
        self.got = functools.reduce(jnp.add, moved.values())

    def piece(self, index):
        return jnp.where(index < self.holders, self.first, self.got)

    def spans(self, low, high):
        found = []
        for start, end, owner in self.where:
            first, last = max(low, start), min(high, end)
            if first < last:
                found.append((owner, first - start, last - first, first - low))
        return found

    def pick(self, held, low, high):
        found = [held[d, first : first + rows] for d, first, rows, _ in self.spans(low, high)]
        return found[0] if len(found) == 1 else jnp.concatenate(found, 0)


def to_rows(layout, flat, index, spare=None):
    rows, lanes, size = layout.used, layout.lanes, layout.size
    whole = size // (8 * LANES) * 8
    tail = size - whole * LANES
    head = max(layout.edge // LANES, 8)
    depth = round_up(max(rows * lanes + head, head + whole + 8) + 8, 8)
    offset = layout.offset(index).astype(jnp.int32)[None]
    operands = [offset, flat]
    if layout.edge:
        tails = flat[:, size - layout.edge :].reshape(head, LANES)
        chain = [(d, d + 1) for d in range(layout.parts - 1)]
        operands.append(lax.ppermute(tails.astype(BF16), "dp", chain).astype(F32))
    if layout.spare:
        operands.append(spare)

    def kernel(off_ref, x_ref, *rest):
        if layout.spare:
            rest[-2][rows : rows + layout.spare, :] = rest[-3][...].astype(BF16)
        edge_ref = rest[0] if layout.edge else None
        out_ref, pad_ref = rest[-2:]
        if layout.edge:
            pad_ref[0:head, :] = edge_ref[...]
        pad_ref[pl.ds(head, whole), :] = x_ref[:, pl.ds(0, whole * LANES)].reshape(whole, LANES)
        left = depth - head - whole
        pad_ref[pl.ds(head + whole, left), :] = jnp.zeros((left, LANES), F32)
        for row in range(-(-tail // LANES)):
            count = min(LANES, tail - row * LANES)
            pad_ref[pl.ds(head + whole + row, 1), 0:count] = x_ref[
                :, pl.ds((whole + row) * LANES, count)
            ]
        off_rows, off_lane = off_ref[0] // LANES, off_ref[0] % LANES
        lane = lax.broadcasted_iota(jnp.int32, (rows, LANES), 1)
        for j in range(lanes):
            if layout.edge:
                before = pad_ref[pl.ds(head + j - off_rows - 1, rows, stride=lanes), :]
                here = pad_ref[pl.ds(head + j - off_rows, rows, stride=lanes), :]
                value = jnp.where(
                    lane < off_lane,
                    pltpu.roll(before, off_lane, 1),
                    pltpu.roll(here, off_lane, 1),
                )
            else:
                value = pad_ref[pl.ds(head + j, rows, stride=lanes), :]
            out_ref[0:rows, LANES * j : LANES * j + LANES] = value.astype(BF16)

    return pl.pallas_call(
        kernel,
        out_shape=jax.ShapeDtypeStruct((layout.rows, layout.width), BF16),
        in_specs=[SMEM] + [VMEM] * (len(operands) - 1),
        out_specs=VMEM,
        scratch_shapes=[pltpu.VMEM((depth, LANES), F32)],
        compiler_params=params(40),
    )(*operands)


def block_rows(layout):
    need = -(-layout.size // LANES)
    steps = max(1, need // 864)
    return round_up(-(-need // steps), 8), -(-need // round_up(-(-need // steps), 8))


def to_flat(layout, matrix, index):
    rows, lanes = layout.used, layout.lanes
    block, steps = block_rows(layout)
    depth = round_up(max(rows * lanes, block * steps + layout.unit // LANES + 1), 8) + 8
    offset = layout.offset(index).astype(jnp.int32)[None]

    def kernel(off_ref, x_ref, out_ref, pad_ref):
        for j in range(lanes):
            pad_ref[pl.ds(j, rows, stride=lanes), :] = x_ref[
                0:rows, LANES * j : LANES * j + LANES
            ]
        left = depth - rows * lanes
        pad_ref[pl.ds(rows * lanes, left), :] = jnp.zeros((left, LANES), F32)
        off_rows, off_lane = off_ref[0] // LANES, off_ref[0] % LANES
        turn = (LANES - off_lane) % LANES
        lane = lax.broadcasted_iota(jnp.int32, (block, LANES), 1)

        def body(step, carry):
            start = pl.multiple_of(step * block, 8)
            here = pad_ref[pl.ds(start + off_rows, block), :]
            if layout.edge:
                after = pad_ref[pl.ds(start + off_rows + 1, block), :]
                here = jnp.where(
                    lane < LANES - off_lane, pltpu.roll(here, turn, 1), pltpu.roll(after, turn, 1)
                )
            out_ref[pl.ds(start, block), :] = here
            return carry

        lax.fori_loop(0, steps, body, 0)

    return pl.pallas_call(
        kernel,
        out_shape=jax.ShapeDtypeStruct((block * steps, LANES), F32),
        in_specs=[SMEM, VMEM],
        out_specs=VMEM,
        scratch_shapes=[pltpu.VMEM((depth, LANES), F32)],
        compiler_params=params(48),
    )(offset, matrix)


def adamw(master, first, second, gradient, step_value, rate):
    first_new = BETA_ONE * first + (1.0 - BETA_ONE) * gradient
    second_new = BETA_TWO * second + (1.0 - BETA_TWO) * gradient * gradient
    first_fix = 1.0 - jnp.power(BETA_ONE, step_value)
    second_fix = 1.0 - jnp.power(BETA_TWO, step_value)
    update = rate * (
        first_new / first_fix / (jnp.sqrt(second_new / second_fix) + ADAM_EPS) + DECAY * master
    )
    master_new = master - update
    return (master_new, first_new, second_new, gradient, master_new.astype(BF16))


def adamw_flat(layout, master, first, second, gradient, step_value, rate):
    block, steps = block_rows(layout)
    fixes = jnp.stack(
        [1.0 - jnp.power(BETA_ONE, step_value), 1.0 - jnp.power(BETA_TWO, step_value)]
    )

    def kernel(fix_ref, w_ref, m_ref, v_ref, g_ref, w_out, m_out, v_out, g_out, c_out):
        view = lambda ref: ref.reshape(block, LANES)
        grad = g_ref[...]
        master_old = view(w_ref)[...]
        first_new = BETA_ONE * view(m_ref)[...] + (1.0 - BETA_ONE) * grad
        second_new = BETA_TWO * view(v_ref)[...] + (1.0 - BETA_TWO) * grad * grad
        update = rate * (
            first_new / fix_ref[0] / (jnp.sqrt(second_new / fix_ref[1]) + ADAM_EPS)
            + DECAY * master_old
        )
        view(w_out)[...] = master_old - update
        view(m_out)[...] = first_new
        view(v_out)[...] = second_new
        view(g_out)[...] = grad
        c_out[...] = w_out[...].astype(BF16)

    row = pl.BlockSpec((1, block * LANES), lambda i: (0, i))
    like = jax.ShapeDtypeStruct(master.shape, F32)
    return pl.pallas_call(
        kernel,
        grid=(steps,),
        out_shape=(like, like, like, like, jax.ShapeDtypeStruct(master.shape, BF16)),
        in_specs=[SMEM, row, row, row, pl.BlockSpec((block, LANES), lambda i: (i, 0))],
        out_specs=(row,) * 5,
        compiler_params=params(48),
    )(fixes, master, first, second, gradient)


class Ring:
    def __init__(self, parts):
        self.parts = parts
        self.inner = 2 if parts % 2 == 0 else 1
        self.outer = parts // self.inner
        self.small = self.outer <= 8
        self.next = [(d, (d + self.inner) % parts) for d in range(parts)]
        self.pair = [(d, d ^ 1) for d in range(parts)]

    def swap(self, block):
        return lax.ppermute(block, "dp", self.pair)

    def onward(self, block):
        return lax.ppermute(block, "dp", self.next)


def join(runs, *work):
    moving = [run.moving() for run in runs]
    moving, work = lax.optimization_barrier((moving, list(work)))
    for run, moved in zip(runs, moving):
        run.land(moved)
    return work[0] if len(work) == 1 else work


class Gathering:
    def __init__(self, ring, block, index):
        self.ring, self.block, self.round = ring, block, 0
        self.rounds = ring.outer if ring.small else 1
        self.at, self.side = index // ring.inner, index % ring.inner
        self.zero = jnp.zeros((), index.dtype)
        self.held = jnp.zeros((ring.outer, ring.inner) + block.shape, block.dtype)

    def send(self):
        ring = self.ring
        self.sent = {}
        if self.round >= self.rounds:
            return self
        if not ring.small:
            self.sent["all"] = gather_small(self.block[None], ring.parts)
            return self
        if ring.inner == 2:
            self.sent["other"] = ring.swap(self.block)
        if self.round < ring.outer - 1:
            self.sent["after"] = ring.onward(self.block)
        return self

    def moving(self):
        return self.sent

    def put(self, value, side):
        slot = lax.rem(self.at - self.round + self.ring.outer, self.ring.outer)
        self.held = lax.dynamic_update_slice(
            self.held, value[None, None], (slot, side) + (self.zero,) * value.ndim
        )

    def land(self, moved):
        if self.round >= self.rounds:
            return
        if "all" in moved:
            self.held = moved["all"]
        else:
            if "other" in moved:
                self.put(moved["other"], 1 - self.side)
            self.put(self.block, self.side)
            self.block = moved.get("after")
        self.round += 1

    def result(self):
        while self.round < self.rounds:
            join([self.send()])
        return self.held.reshape((self.ring.parts,) + self.held.shape[-2:])


class Shared(Gathering):
    def __init__(self, ring, block, index, share):
        super().__init__(ring, block, index)
        self.share = share
        self.far_held = jnp.zeros(self.held.shape[:2] + (share,) + block.shape[1:], block.dtype)
        self.rounds += 1
        self.chunk = None

    def send(self):
        if self.round < self.rounds - 1:
            super().send()
        else:
            self.sent = {}
        if self.chunk is not None and self.round < self.rounds:
            pairs = [(m, m ^ 2) for m in range(lax.axis_size("mp"))]
            self.sent["far"] = lax.ppermute(self.chunk, "mp", pairs)
        return self

    def land(self, moved):
        if self.round >= self.rounds:
            return
        far = moved.pop("far", None)
        if far is not None:
            if not self.ring.small:
                self.far_held = far
            else:
                slot = lax.rem(self.at - self.round + 1 + self.ring.outer, self.ring.outer)
                for number, side in ((0, self.side), (1, 1 - self.side)):
                    self.far_held = lax.dynamic_update_slice(
                        self.far_held,
                        far[number][None, None],
                        (slot, side) + (self.zero,) * (far.ndim - 1),
                    )
        if self.round == self.rounds - 1:
            self.round += 1
            return
        if "all" in moved:
            super().land(moved)
            self.chunk = self.held[:, : self.share]
        else:
            self.chunk = jnp.stack([self.block[: self.share], moved["other"][: self.share]])
            super().land(moved)

    def both(self):
        own = self.result()[:, : self.share]
        return own, self.far_held.reshape(own.shape)


class Scattering:
    def __init__(self, ring, blocks, index):
        self.ring, self.blocks = ring, blocks
        self.at, self.side = index // ring.inner, index % ring.inner
        self.left = ring.outer if ring.small else 1
        self.pending = None

    def send(self):
        ring = self.ring
        self.sent = {}
        if not self.left:
            return self
        self.left -= 1
        if not ring.small:
            self.sent["all"] = scatter_halves(self.blocks, ring.parts)
            return self
        if self.pending is not None:
            self.sent["carried"] = ring.onward(self.pending.astype(BF16))
        first = lax.rem(self.at + self.left, ring.outer) * ring.inner
        self.mine = lax.dynamic_index_in_dim(self.blocks, first + self.side, 0, False)
        if ring.inner == 2:
            given = lax.dynamic_index_in_dim(self.blocks, first + 1 - self.side, 0, False)
            self.sent["other"] = ring.swap(given)
        return self

    def moving(self):
        return self.sent

    def land(self, moved):
        if "all" in moved:
            self.pending = moved["all"]
        if "all" in moved or not moved:
            return
        total = self.mine.astype(F32)
        for value in moved.values():
            total = total + value.astype(F32)
        self.pending = total

    def result(self):
        while self.left:
            join([self.send()])
        return self.pending


def step(runs):
    runs[:] = [run for run in runs if run.round < run.rounds]
    for run in runs:
        run.send()


class Once:
    def __init__(self, arrays, steps):
        self.sent = {}
        count = lax.axis_size("mp")
        for name, array in arrays.items():
            pairs = [(m, m ^ steps) for m in range(count)]
            self.sent[name] = lax.ppermute(array, "mp", pairs)

    def moving(self):
        return self.sent

    def land(self, moved):
        self.got = moved


def in_order(pieces):
    me = lax.axis_index("mp")
    first = pieces[0]
    held = jnp.zeros((len(pieces),) + first.shape, first.dtype)
    zero = jnp.zeros((), me.dtype)
    for key, piece in pieces.items():
        held = lax.dynamic_update_slice(held, piece[None], (me ^ key,) + (zero,) * piece.ndim)
    return held


def scatter_halves(blocks, parts):
    index = lax.axis_index("dp")
    step = parts // 2
    while step:
        upper = (index // step) % 2 == 1
        low, high = blocks[:step], blocks[step:]
        mine, given = jnp.where(upper, high, low), jnp.where(upper, low, high)
        got = lax.ppermute(given.astype(BF16), "dp", [(d, d ^ step) for d in range(parts)])
        blocks = mine.astype(F32) + got.astype(F32)
        step //= 2
    return blocks[0]


def gather_small(values, parts):
    index = lax.axis_index("dp")
    step = 1
    while step < parts:
        other = lax.ppermute(values, "dp", [(d, d ^ step) for d in range(parts)])
        upper = (index // step) % 2 == 1
        values = jnp.where(
            upper, jnp.concatenate([other, values], 0), jnp.concatenate([values, other], 0)
        )
        step *= 2
    return values


def sum_mp(part):
    count = lax.axis_size("mp")
    near = [(m, m ^ 1) for m in range(count)]
    half = part.shape[0] // 2
    side = lax.axis_index("mp") % 2
    low, high = part[:half], part[half:]
    mine, given = jnp.where(side == 0, low, high), jnp.where(side == 0, high, low)
    total = mine.astype(F32) + lax.ppermute(given, "mp", near).astype(F32)
    step = 2
    while step < count:
        total = total.astype(BF16)
        far = [(m, m ^ step) for m in range(count)]
        total = total.astype(F32) + lax.ppermute(total, "mp", far).astype(F32)
        step *= 2
    total = total.astype(BF16)
    other = lax.ppermute(total, "mp", near)
    return jnp.concatenate(
        [jnp.where(side == 0, total, other), jnp.where(side == 0, other, total)], 0
    )


def rope_tables(positions, head_size, repeats):
    half_size = head_size // 2
    frequency = jnp.exp(
        -jnp.log(10000.0) * 2.0 * jnp.arange(half_size, dtype=jnp.float32) / head_size
    )
    frequency = jnp.tile(frequency, 2 * repeats)
    angles = positions.astype(jnp.float32)[:, None] * frequency[None, :]
    return jnp.cos(angles), jnp.sin(angles)


def clip_layout(frames_row, length, frame_tok, clip_slots):
    clip_len = frames_row * frame_tok
    slots = jnp.arange(clip_slots, dtype=jnp.int32)
    clip_end = jnp.sum(
        jnp.where(slots[:, None] >= slots[None, :], clip_len[None, :], 0), 1, dtype=jnp.int32
    )
    clip_start = clip_end - clip_len
    row_index = jnp.arange(length, dtype=jnp.int32)
    segment = jnp.sum(
        (row_index[:, None] >= clip_end[None, :]).astype(jnp.int32), 1, dtype=jnp.int32
    )
    member = segment[:, None] == slots[None, :]
    begin_row = jnp.sum(jnp.where(member, clip_start[None, :], 0), 1, dtype=jnp.int32)
    begin_row = begin_row + jnp.where(segment == clip_slots, clip_end[clip_slots - 1], 0)
    return segment, row_index - begin_row


def condition_rows(steps, cond_width):
    packs, clips = steps.shape
    column = jnp.arange(4 * cond_width, dtype=jnp.int32)
    half_size = cond_width // 2
    k = column // 4
    place = lax.rem(k, half_size).astype(F32)
    frequency = jnp.exp(-jnp.log(10000.0) * place / half_size)
    angles = steps.reshape(-1)[:, None] * frequency[None, :]
    waves = jnp.where((k < half_size)[None, :], jnp.cos(angles), jnp.sin(angles))
    cond = jax.nn.silu(waves).astype(BF16).reshape(packs, 1, clips, 4 * cond_width)
    part = jnp.arange(4, dtype=jnp.int32)
    own = (lax.rem(column, 4)[None, :] == part[:, None])[None, :, None, :]
    return jnp.where(own, cond, jnp.zeros((), BF16)).reshape(packs, 4 * clips, 4 * cond_width)


def dot(left, right):
    return jnp.dot(left, right, preferred_element_type=F32)


def dot_t(left, right):
    return lax.dot_general(left, right, (((1,), (1,)), ((), ())), preferred_element_type=F32)


def t_dot(left, right):
    return lax.dot_general(left, right, (((0,), (0,)), ((), ())), preferred_element_type=F32)


def row_mean(values):
    return jnp.mean(values, -1, keepdims=True)


def per_token(seg, mod_ref, part):
    total = jnp.where(seg == 0, mod_ref[part, 0:1, :], 0.0)
    for clip in range(1, mod_ref.shape[1]):
        total = total + jnp.where(seg == clip, mod_ref[part, clip : clip + 1, :], 0.0)
    return total


def per_clip(seg, values, out_ref):
    for clip in range(out_ref.shape[0]):
        out_ref[clip : clip + 1, :] = jnp.sum(jnp.where(seg == clip, values, 0.0), 0, keepdims=True)


def column_sum(values):
    return jnp.sum(values, 0, keepdims=True)


def rms_back(unit, scale, grad):
    return scale * (grad - unit * row_mean(unit * grad))


def branch_back(grad, branch, gate_tok, gain):
    scale = lax.rsqrt(row_mean(branch * branch) + EPS)
    unit = branch * scale
    opened = jnp.tanh(gate_tok)
    grad_unit = grad * opened
    dgate = grad * unit * gain * (1.0 - opened * opened)
    return rms_back(unit, scale, grad_unit * gain), dgate, column_sum(grad_unit * unit)


def modulate_back(grad, values, gain, scale_tok):
    scale = lax.rsqrt(row_mean(values * values) + EPS)
    unit = values * scale
    grad_unit = grad * unit
    dscale = grad_unit * gain
    dgain = column_sum(grad_unit * (1.0 + scale_tok))
    return rms_back(unit, scale, grad * gain * (1.0 + scale_tok)), dscale, dgain


def head_mean(values):
    width = values.shape[-1]
    rows = lax.broadcasted_iota(jnp.int32, (width, width), 0) // HEAD_DIM
    columns = lax.broadcasted_iota(jnp.int32, (width, width), 1) // HEAD_DIM
    same = jnp.where(rows == columns, 1.0 / HEAD_DIM, 0.0)
    return jnp.dot(values, same, precision=lax.Precision.HIGHEST, preferred_element_type=F32)


def turn(values, sign):
    width = values.shape[-1]
    half = HEAD_DIM // 2
    lane = lax.broadcasted_iota(jnp.int32, values.shape, 1) % HEAD_DIM
    ahead = pltpu.roll(values, width - half, 1)
    behind = pltpu.roll(values, half, 1)
    return jnp.where(lane < half, -sign * ahead, sign * behind)


def head_rms(linear):
    scale = lax.rsqrt(head_mean(linear * linear) + EPS)
    return linear * scale, scale


def head_rms_back(linear, grad, gain):
    unit, scale = head_rms(linear)
    scaled = grad * gain
    return scale * (scaled - unit * head_mean(unit * scaled)), column_sum(grad * unit)


def soft(query, keys, mask):
    scores = dot_t(query, keys) * HEAD_DIM ** (-0.5)
    scores = jnp.where(mask, scores, NEG)
    raised = jnp.exp(scores - jnp.max(scores, -1, keepdims=True))
    return raised / jnp.sum(raised, -1, keepdims=True)


def soft_back(query, keys, values, probs, grad_out):
    grad_probs = dot_t(grad_out, values)
    grad_values = t_dot(probs.astype(BF16), grad_out)
    inner_sum = jnp.sum(probs * grad_probs, -1, keepdims=True)
    grad_scores = (probs * (grad_probs - inner_sum) * HEAD_DIM ** (-0.5)).astype(BF16)
    return dot(grad_scores, keys), t_dot(grad_scores, query), grad_values


def masks(seg_ref, seg_row_ref, key_count, clip_slots):
    seg = seg_ref[...]
    key_clip = lax.broadcasted_iota(jnp.int32, (1, key_count), 1) // (key_count // clip_slots)
    return seg == seg_row_ref[...], (seg == key_clip) | (seg == clip_slots)


class Fetch:
    def __init__(self, held_ref, layout, low, high, into_ref, sems, first):
        self.copies = []
        for number, (d, start, rows, offset) in enumerate(layout.spans(low, high)):
            copy = pltpu.make_async_copy(
                held_ref.at[d, pl.ds(start, rows)],
                into_ref.at[pl.ds(offset, rows)],
                sems.at[first + number],
            )
            copy.start()
            self.copies.append(copy)

    def wait(self):
        for copy in self.copies:
            copy.wait()


def own_rows(block, i, offset):
    row = lax.broadcasted_iota(jnp.int32, block.shape, 0) + i * block.shape[0]
    lane = lax.broadcasted_iota(jnp.int32, block.shape, 1)
    mine = row * block.shape[1] + lane >= offset
    return jnp.where(mine, block.astype(F32), 0.0).astype(BF16)


def block_place(layout, index):
    first = index * layout.size // layout.unit * (layout.unit // layout.width // LANES)
    return jnp.stack([first, layout.offset(index)]).astype(jnp.int32)


def modulation_share(layout, index, rows, low, cond):
    packs, conds, depth = cond.shape
    blocks = layout.used // LANES
    first_block, count = low // LANES, depth // LANES

    def kernel(place_ref, w_ref, cond_ref, out_ref):
        out_ref[...] = jnp.zeros_like(out_ref)

        def body(i, carry):
            g = place_ref[0] + i - first_block

            @pl.when((g >= 0) & (g < count))
            def _():
                weights = w_ref[pl.ds(pl.multiple_of(i * LANES, LANES), LANES), :]
                lanes = pl.ds(pl.multiple_of(g * LANES, LANES), LANES)
                left = cond_ref[:, :, lanes].reshape(packs * conds, LANES)
                out_ref[...] += dot(left, own_rows(weights, i, place_ref[1]))

            return carry

        lax.fori_loop(0, blocks, body, 0)

    out = pl.pallas_call(
        kernel,
        out_shape=jax.ShapeDtypeStruct((packs * conds, layout.width), F32),
        in_specs=[SMEM, VMEM, VMEM],
        out_specs=VMEM,
        compiler_params=params(40),
    )(block_place(layout, index), rows, cond)
    return out.reshape(packs, conds, layout.width)


def text_share(layout, index, rows, low, text):
    groups, packs, key_count, text_cut = text.shape
    width = layout.width
    blocks = layout.used // LANES
    first_block, count = low // LANES, groups * text_cut // LANES
    step_packs = min(8, packs)
    per_cut = text_cut // LANES

    def kernel(place_ref, w_ref, text_ref, out_ref, sum_ref):
        sum_ref[...] = jnp.zeros_like(sum_ref)

        def body(i, carry):
            g = place_ref[0] + i - first_block

            @pl.when((g >= 0) & (g < 2 * count))
            def _():
                weights = w_ref[pl.ds(pl.multiple_of(i * LANES, LANES), LANES), :]
                sub = g % count
                lanes = pl.ds(pl.multiple_of(sub % per_cut * LANES, LANES), LANES)
                left = text_ref[sub // per_cut, :, :, lanes].reshape(-1, LANES)
                sum_ref[g // count] += dot(left, own_rows(weights, i, place_ref[1]))

            return carry

        lax.fori_loop(0, blocks, body, 0)
        for kind in range(2):
            out_ref[:, :, kind * width : (kind + 1) * width] = (
                sum_ref[kind].astype(BF16).reshape(step_packs, key_count, width)
            )

    return pl.pallas_call(
        kernel,
        grid=(packs // step_packs,),
        out_shape=jax.ShapeDtypeStruct((packs, key_count, 2 * width), BF16),
        in_specs=[
            SMEM,
            pl.BlockSpec(rows.shape, lambda s: (0, 0), pipeline_mode=pl.Buffered(1)),
            pl.BlockSpec(
                (groups, step_packs, key_count, text_cut),
                lambda s: (0, s, 0, 0),
                pipeline_mode=pl.Buffered(1),
            ),
        ],
        out_specs=pl.BlockSpec((step_packs, key_count, 2 * width), lambda s: (s, 0, 0)),
        scratch_shapes=[pltpu.VMEM((2, step_packs * key_count, width), F32)],
        compiler_params=params(48),
    )(block_place(layout, index), rows, text)


def attention_inputs(layout, held, tokens, seg, mods, norms, gains, cosine, sine):
    length, depth = tokens.shape
    width = layout.width
    count = len(layout.spans(0, 3 * depth))

    def kernel(
        held_ref, x_ref, seg_ref, mod_ref, norm_ref, gain_ref, cos_ref, sin_ref,
        normed_ref, q_ref, k_ref, v_ref, q_lin_ref, k_lin_ref, w_ref, sems,
    ):
        fetch = Fetch(held_ref, layout, 0, 3 * depth, w_ref, sems, 0)
        x = x_ref[...].astype(F32)
        unit = x * lax.rsqrt(row_mean(x * x) + EPS)
        normed = unit * norm_ref[0:1, :] * (1.0 + per_token(seg_ref[...], mod_ref, 0))
        normed = normed.astype(BF16)
        normed_ref[...] = normed
        fetch.wait()
        cosine, sine = cos_ref[...], sin_ref[...]
        for place, (lin_ref, out_ref) in enumerate(((q_lin_ref, q_ref), (k_lin_ref, k_ref))):
            linear = dot(normed, w_ref[place * depth : (place + 1) * depth, :])
            lin_ref[...] = linear
            rms = head_rms(linear)[0] * gain_ref[place : place + 1, :]
            out_ref[...] = (rms * cosine + turn(rms, 1.0) * sine).astype(BF16)
        v_ref[...] = dot(normed, w_ref[2 * depth : 3 * depth, :]).astype(BF16)

    low, full = (jax.ShapeDtypeStruct((length, width), t) for t in (BF16, F32))
    return pl.pallas_call(
        kernel,
        out_shape=(jax.ShapeDtypeStruct((length, depth), BF16), low, low, low, full, full),
        in_specs=[ANY] + [VMEM] * 7,
        out_specs=(VMEM,) * 6,
        scratch_shapes=[
            pltpu.VMEM((3 * depth, width), BF16),
            pltpu.SemaphoreType.DMA((count,)),
        ],
        compiler_params=params(48),
    )(held, tokens, seg, mods, norms, gains, cosine, sine)


def attention_forward(query, key, value, text_lin, seg, seg_row, gains, w_out, clips):
    length, width = query.shape
    key_count = text_lin.shape[0]
    model_width = w_out.shape[1]

    def kernel(
        q_ref, k_ref, v_ref, lin_ref, seg_ref, row_ref, gain_ref, w_ref,
        mixed_ref, cross_ref, part_ref, tk_lin_ref, tk_ref, tv_ref,
    ):
        linear = lin_ref[:, 0:width]
        tk_lin_ref[...] = linear
        tk_ref[...] = (head_rms(linear)[0] * gain_ref[2:3, :]).astype(BF16)
        tv_ref[...] = lin_ref[:, width : 2 * width].astype(BF16)
        own_mask, cross_mask = masks(seg_ref, row_ref, key_count, clips)
        own = []
        for head in range(width // HEAD_DIM):
            at = slice(head * HEAD_DIM, (head + 1) * HEAD_DIM)
            probs = soft(q_ref[:, at], k_ref[:, at], own_mask)
            own.append(dot(probs.astype(BF16), v_ref[:, at]))
            probs = soft(q_ref[:, at], tk_ref[:, at], cross_mask)
            cross_ref[:, at] = dot(probs.astype(BF16), tv_ref[:, at])
        mixed = jnp.concatenate(own, 1) + jnp.tanh(gain_ref[3:4, :]) * cross_ref[...]
        mixed = mixed.astype(BF16)
        mixed_ref[...] = mixed
        part_ref[...] = dot(mixed, w_ref[...]).astype(BF16)

    return pl.pallas_call(
        kernel,
        out_shape=(
            jax.ShapeDtypeStruct((length, width), BF16),
            jax.ShapeDtypeStruct((length, width), F32),
            jax.ShapeDtypeStruct((length, model_width), BF16),
            jax.ShapeDtypeStruct((key_count, width), F32),
            jax.ShapeDtypeStruct((key_count, width), BF16),
            jax.ShapeDtypeStruct((key_count, width), BF16),
        ),
        in_specs=[VMEM] * 8,
        out_specs=(VMEM,) * 6,
        compiler_params=params(48),
    )(query, key, value, text_lin, seg, seg_row, gains, w_out)


def ffn_forward(layout, held, tokens, attn_out, seg, mods, norms, w_down):
    length, depth = tokens.shape
    width = layout.width
    counts = [len(layout.spans(i * depth, (i + 1) * depth)) for i in range(2)]

    def kernel(
        held_ref, x_ref, branch_ref, seg_ref, mod_ref, norm_ref, down_hbm,
        middle_ref, ffn_in_ref, gate_ref, up_ref, hidden_ref, part_ref,
        wg_ref, wu_ref, wd_ref, sems,
    ):
        for_gate = Fetch(held_ref, layout, 0, depth, wg_ref, sems, 0)
        for_up = Fetch(held_ref, layout, depth, 2 * depth, wu_ref, sems, counts[0])
        for_down = pltpu.make_async_copy(down_hbm, wd_ref, sems.at[sum(counts)])
        for_down.start()
        seg = seg_ref[...]
        branch = branch_ref[...].astype(F32)
        unit = branch * lax.rsqrt(row_mean(branch * branch) + EPS)
        opened = jnp.tanh(per_token(seg, mod_ref, 1))
        middle = x_ref[...].astype(F32) + opened * unit * norm_ref[1:2, :]
        middle_ref[...] = middle
        unit = middle * lax.rsqrt(row_mean(middle * middle) + EPS)
        ffn_in = (unit * norm_ref[2:3, :] * (1.0 + per_token(seg, mod_ref, 2))).astype(BF16)
        ffn_in_ref[...] = ffn_in
        for_gate.wait()
        gate = dot(ffn_in, wg_ref[...])
        gate_ref[...] = gate
        for_up.wait()
        up = dot(ffn_in, wu_ref[...])
        up_ref[...] = up
        hidden = (jax.nn.silu(gate) * up).astype(BF16)
        hidden_ref[...] = hidden
        for_down.wait()
        part_ref[...] = dot(hidden, wd_ref[...]).astype(BF16)

    def like(columns, kind):
        return jax.ShapeDtypeStruct((length, columns), kind)

    return pl.pallas_call(
        kernel,
        out_shape=(
            like(depth, F32),
            like(depth, BF16),
            like(width, F32),
            like(width, F32),
            like(width, BF16),
            like(depth, BF16),
        ),
        in_specs=[ANY] + [VMEM] * 5 + [ANY],
        out_specs=(VMEM,) * 6,
        scratch_shapes=[
            pltpu.VMEM((depth, width), BF16),
            pltpu.VMEM((depth, width), BF16),
            pltpu.VMEM((width, depth), BF16),
            pltpu.SemaphoreType.DMA((sum(counts) + 1,)),
        ],
        compiler_params=params(56),
    )(held, tokens, attn_out, seg, mods, norms, w_down)


def ffn_backward(
    layout, held, middle, ffn_out, cotangent, ffn_in, gate, up, hidden, seg, mods, norms, w_down
):
    length, depth = middle.shape
    width = layout.width
    clips = mods.shape[1]
    counts = [len(layout.spans(i * depth, (i + 1) * depth)) for i in range(2)]
    cut = 256

    def kernel(
        held_ref, middle_ref, branch_ref, cot_ref, in_ref, gate_ref, up_ref, hidden_ref,
        seg_ref, mod_ref, norm_ref, down_hbm,
        output_ref, part_ref, grads_ref, dmod_ref, dgain_ref,
        wg_ref, wu_ref, wd_ref, woven_ref, sems,
    ):
        for_down = pltpu.make_async_copy(down_hbm, wd_ref, sems.at[sum(counts)])
        for_down.start()
        for_gate = Fetch(held_ref, layout, 0, depth, wg_ref, sems, 0)
        for_up = Fetch(held_ref, layout, depth, 2 * depth, wu_ref, sems, counts[0])
        seg = seg_ref[...]
        branch = branch_ref[...].astype(F32)
        gate_tok = per_token(seg, mod_ref, 3)
        gain = norm_ref[3:4, :]
        unit = branch * lax.rsqrt(row_mean(branch * branch) + EPS)
        output_ref[...] = (middle_ref[...] + jnp.tanh(gate_tok) * unit * gain).astype(BF16)
        dbranch, dgate_tok, dgain = branch_back(cot_ref[...].astype(F32), branch, gate_tok, gain)
        per_clip(seg, dgate_tok, dmod_ref)
        dgain_ref[...] = dgain
        dlow = dbranch.astype(BF16)
        for_down.wait()
        dhidden = dot_t(dlow, wd_ref[...])
        gate, up = gate_ref[...], up_ref[...]
        sigma = jax.nn.sigmoid(gate)
        dup = (dhidden * gate * sigma).astype(BF16)
        dgate = (dhidden * up * (sigma * (1.0 + gate * (1.0 - sigma)))).astype(BF16)
        half = width // 2
        unit_row = lax.broadcasted_iota(jnp.int32, (width, half), 0)
        unit_column = lax.broadcasted_iota(jnp.int32, (width, half), 1)
        chosen = []
        for parity in range(2):
            pick = jnp.where(unit_row == 2 * unit_column + parity, 1.0, 0.0).astype(BF16)
            chosen.append(dot(hidden_ref[...], pick).astype(BF16))
        for start in range(0, half, cut):
            pair = [dot(c[:, start : start + cut].T, dlow) for c in chosen]
            for place in range(3):
                for j in range(width // LANES):
                    at = place * width + j * LANES
                    woven_ref[j, pl.ds(3 * start + place, cut, stride=3), :] = pair[at // depth][
                        :, at % depth : at % depth + LANES
                    ]
        for j in range(width // LANES):
            grads_ref[2 * depth : 3 * depth, j * LANES : (j + 1) * LANES] = woven_ref[j].astype(
                BF16
            )
        for_gate.wait()
        part = dot_t(dgate, wg_ref[...])
        for_up.wait()
        part_ref[...] = (part + dot_t(dup, wu_ref[...])).astype(BF16)
        for start in range(0, depth, cut):
            in_t = in_ref[:, start : start + cut].T
            grads_ref[start : start + cut, :] = dot(in_t, dgate).astype(BF16)
            grads_ref[depth + start : depth + start + cut, :] = dot(in_t, dup).astype(BF16)

    def like(rows, columns, kind):
        return jax.ShapeDtypeStruct((rows, columns), kind)

    return pl.pallas_call(
        kernel,
        out_shape=(
            like(length, depth, BF16),
            like(length, depth, BF16),
            like(3 * depth, width, BF16),
            like(clips, depth, F32),
            like(1, depth, F32),
        ),
        in_specs=[ANY] + [VMEM] * 10 + [ANY],
        out_specs=(VMEM,) * 5,
        scratch_shapes=[
            pltpu.VMEM((depth, width), BF16),
            pltpu.VMEM((depth, width), BF16),
            pltpu.VMEM((width, depth), BF16),
            pltpu.VMEM((width // LANES, depth, LANES), F32),
            pltpu.SemaphoreType.DMA((sum(counts) + 1,)),
        ],
        compiler_params=params(56),
    )(
        held, middle, ffn_out, cotangent, ffn_in, gate, up, hidden, seg, mods, norms, w_down
    )


def branch_backward(dffn_in, middle, cotangent, attn_out, seg, mods, norms, w_out):
    length, depth = middle.shape
    width = w_out.shape[0]
    clips = mods.shape[1]

    def kernel(
        din_ref, middle_ref, cot_ref, branch_ref, seg_ref, mod_ref, norm_ref, wo_ref,
        dmiddle_ref, dlow_ref, dmixed_ref, dscale_ref, dgate_ref, dnorm_ref,
    ):
        seg = seg_ref[...]
        dpre, dscale, dgain = modulate_back(
            din_ref[...].astype(F32), middle_ref[...], norm_ref[2:3, :], per_token(seg, mod_ref, 2)
        )
        per_clip(seg, dscale, dscale_ref)
        dnorm_ref[1:2, :] = dgain
        dmiddle = cot_ref[...].astype(F32) + dpre
        dmiddle_ref[...] = dmiddle
        dbranch, dgate_tok, dgain = branch_back(
            dmiddle, branch_ref[...].astype(F32), per_token(seg, mod_ref, 1), norm_ref[1:2, :]
        )
        per_clip(seg, dgate_tok, dgate_ref)
        dnorm_ref[0:1, :] = dgain
        dlow = dbranch.astype(BF16)
        dlow_ref[...] = dlow
        dmixed_ref[...] = dot_t(dlow, wo_ref[...]).astype(BF16)

    def like(rows, columns, kind):
        return jax.ShapeDtypeStruct((rows, columns), kind)

    return pl.pallas_call(
        kernel,
        out_shape=(
            like(length, depth, F32),
            like(length, depth, BF16),
            like(length, width, BF16),
            like(clips, depth, F32),
            like(clips, depth, F32),
            like(2, depth, F32),
        ),
        in_specs=[VMEM] * 8,
        out_specs=(VMEM,) * 6,
        compiler_params=params(48),
    )(dffn_in, middle, cotangent, attn_out, seg, mods, norms, w_out)


def attention_backward(
    layout, held, dmixed, query, key, value, q_lin, k_lin,
    text_key, text_value, tk_lin, cross, seg, seg_row, gains, cosine, sine, clips,
):
    length, width = query.shape
    depth = layout.width * lax.axis_size("mp")
    key_count = text_key.shape[0]
    count = len(layout.spans(0, 3 * depth))

    def kernel(
        held_ref, dmixed_ref, q_ref, k_ref, v_ref, q_lin_ref, k_lin_ref, tk_ref, tv_ref,
        tk_lin_ref, cross_ref, seg_ref, row_ref, gain_ref, cos_ref, sin_ref,
        part_ref, acts_ref, dgains_ref, w_ref, dq_ref, dk_ref, dv_ref, dtk_ref, dtv_ref, sems,
    ):
        fetch = Fetch(held_ref, layout, 0, 3 * depth, w_ref, sems, 0)
        opened = jnp.tanh(gain_ref[3:4, :])
        dmixed = dmixed_ref[...]
        wide = dmixed.astype(F32)
        dgains_ref[3:4, :] = column_sum(wide * cross_ref[...]) * (1.0 - opened * opened)
        dcross = (wide * opened).astype(BF16)
        own_mask, cross_mask = masks(seg_ref, row_ref, key_count, clips)
        for head in range(width // HEAD_DIM):
            at = slice(head * HEAD_DIM, (head + 1) * HEAD_DIM)
            query = q_ref[:, at]
            probs = soft(query, k_ref[:, at], own_mask)
            dq, dk, dv = soft_back(query, k_ref[:, at], v_ref[:, at], probs, dmixed[:, at])
            probs = soft(query, tk_ref[:, at], cross_mask)
            dq_cross, dtk, dtv = soft_back(
                query, tk_ref[:, at], tv_ref[:, at], probs, dcross[:, at]
            )
            dq_ref[:, at] = dq + dq_cross
            dk_ref[:, at] = dk
            dv_ref[:, at] = dv
            dtk_ref[:, at] = dtk
            dtv_ref[:, at] = dtv
        cosine, sine = cos_ref[...], sin_ref[...]
        lows = []
        for place, (grad_ref, lin_ref) in enumerate(((dq_ref, q_lin_ref), (dk_ref, k_lin_ref))):
            grad = grad_ref[...]
            grad = grad * cosine + turn(grad * sine, -1.0)
            dlin, dgain = head_rms_back(lin_ref[...], grad, gain_ref[place : place + 1, :])
            dgains_ref[place : place + 1, :] = dgain
            lows.append(dlin.astype(BF16))
        lows.append(dv_ref[...].astype(BF16))
        dlin, dgain = head_rms_back(tk_lin_ref[...], dtk_ref[...], gain_ref[2:3, :])
        dgains_ref[2:3, :] = dgain
        for place in range(3):
            acts_ref[place * length : (place + 1) * length, :] = lows[place]
        acts_ref[3 * length : 3 * length + key_count, :] = dlin.astype(BF16)
        acts_ref[3 * length + key_count :, :] = dtv_ref[...].astype(BF16)
        fetch.wait()
        part = dot_t(lows[0], w_ref[0:depth, :])
        part = part + dot_t(lows[1], w_ref[depth : 2 * depth, :])
        part_ref[...] = (part + dot_t(lows[2], w_ref[2 * depth : 3 * depth, :])).astype(BF16)

    return pl.pallas_call(
        kernel,
        out_shape=(
            jax.ShapeDtypeStruct((length, depth), BF16),
            jax.ShapeDtypeStruct((3 * length + 2 * key_count, width), BF16),
            jax.ShapeDtypeStruct((4, width), F32),
        ),
        in_specs=[ANY] + [VMEM] * 15,
        out_specs=(VMEM,) * 3,
        scratch_shapes=[pltpu.VMEM((3 * depth, width), BF16)]
        + [pltpu.VMEM((length, width), F32)] * 3
        + [pltpu.VMEM((key_count, width), F32)] * 2
        + [pltpu.SemaphoreType.DMA((count,))],
        compiler_params=params(56),
    )(
        held, dmixed, query, key, value, q_lin, k_lin, text_key, text_value, tk_lin, cross, seg,
        seg_row, gains, cosine, sine,
    )


def shard_gradient(layout, index, normed, dattn, text, mixed, acts, ends, cond):
    groups = len(normed)
    packs, length, width = normed[0].shape
    key_count, text_cut = text.shape[2:]
    conds = cond.shape[1]
    cut = LANES
    step_packs = min(8, packs)
    blocks = layout.used // cut
    first = (index * layout.size // layout.unit * (layout.unit // width // cut)).astype(jnp.int32)
    per_in = groups * width // cut
    per_text = groups * text_cut // cut
    per_cond = cond.shape[2] // cut
    kinds = [3 * per_in, 4 * per_in, 4 * per_in + 2 * per_text, 4 * per_in + 2 * per_text + per_cond]

    def kernel(first_ref, t_ref, m_ref, a_ref, e_ref, c_ref, *rest):
        n_refs, d_refs = rest[:groups], rest[groups : 2 * groups]
        out_ref, woven_ref = rest[2 * groups :]
        me = first_ref[1]

        @pl.when(pl.program_id(0) == 0)
        def _():
            out_ref[...] = jnp.zeros_like(out_ref)

        def tall(block):
            return block.reshape(-1, block.shape[-1])

        def body(i, carry):
            g = first_ref[0] + i
            start = pl.multiple_of(i * cut, cut)
            rows = pl.ds(start, cut)

            @pl.when(g < kinds[0])
            def _():
                sub = g % per_in
                lanes = pl.ds(pl.multiple_of(sub % (width // cut) * cut, cut), cut)
                grads = pl.ds(pl.multiple_of(g // per_in * length, length), length)
                right = tall(a_ref[:, grads, :])
                for key in range(groups):

                    @pl.when(sub // (width // cut) == me ^ key)
                    def _():
                        out_ref[rows, :] += t_dot(tall(n_refs[key][:, :, lanes]), right)

            @pl.when((g >= kinds[0]) & (g < kinds[1]))
            def _():
                each = cut // groups
                at = (g - kinds[0]) * each
                lanes = pl.ds(pl.multiple_of(at // LANES * LANES, LANES), LANES)
                slab = tall(m_ref[:, length : 2 * length, lanes]).astype(F32)
                slab = pltpu.roll(slab, (LANES - at % LANES) % LANES, 1)
                left = slab.T[0:each, :].astype(BF16)
                for key in range(groups):
                    value = dot(left, tall(d_refs[key][...]))
                    for j in range(width // LANES):
                        woven_ref[j, pl.ds(me ^ key, each, stride=groups), :] = value[
                            :, j * LANES : (j + 1) * LANES
                        ]
                woven = [woven_ref[j] for j in range(width // LANES)]
                out_ref[rows, :] += jnp.concatenate(woven, 1)

            @pl.when((g >= kinds[1]) & (g < kinds[2]))
            def _():
                sub = (g - kinds[1]) % per_text
                lanes = pl.ds(pl.multiple_of(sub % (text_cut // cut) * cut, cut), cut)
                at = 3 * length + (g - kinds[1]) // per_text * key_count
                grads = pl.ds(pl.multiple_of(at, key_count), key_count)
                left = tall(t_ref[sub // (text_cut // cut), :, :, lanes])
                out_ref[rows, :] += t_dot(left, tall(a_ref[:, grads, :]))

            @pl.when((g >= kinds[2]) & (g < kinds[3]))
            def _():
                lanes = pl.ds(pl.multiple_of((g - kinds[2]) * cut, cut), cut)
                left = tall(c_ref[:, :, lanes])
                out_ref[rows, :] += t_dot(left, tall(e_ref[:, 0:conds, :]))

            @pl.when(g == kinds[3])
            def _():
                total = jnp.sum(e_ref[:, conds : conds + 16, :].astype(F32), 0)
                out_ref[pl.ds(start, 16), :] += total

            return carry

        lax.fori_loop(0, blocks, body, 0)

    def spec(array, packs_dim):
        shape = list(array.shape)
        shape[packs_dim] = step_packs
        return pl.BlockSpec(
            tuple(shape),
            lambda s: tuple(s if d == packs_dim else 0 for d in range(len(shape))),
            pipeline_mode=pl.Buffered(1),
        )

    operands = [(text, 1), (mixed, 0), (acts, 0), (ends, 0), (cond, 0)]
    operands += [(array, 0) for array in normed + dattn]
    return pl.pallas_call(
        kernel,
        grid=(packs // step_packs,),
        out_shape=jax.ShapeDtypeStruct((layout.used, width), F32),
        in_specs=[SMEM] + [spec(*o) for o in operands],
        out_specs=pl.BlockSpec((layout.used, width), lambda s: (0, 0)),
        scratch_shapes=[pltpu.VMEM((width // LANES, cut, LANES), F32)],
        compiler_params=params(58),
    )(jnp.stack([first, lax.axis_index("mp").astype(jnp.int32)]), *[o[0] for o in operands])


def input_backward(dnormed, tokens, dmiddle, seg, mods, norms):
    length, depth = tokens.shape
    clips = mods.shape[1]

    def kernel(d_ref, x_ref, dmiddle_ref, seg_ref, mod_ref, norm_ref, out_ref, dmod_ref, dgain_ref):
        seg = seg_ref[...]
        dpre, dscale, dgain = modulate_back(
            d_ref[...].astype(F32),
            x_ref[...].astype(F32),
            norm_ref[0:1, :],
            per_token(seg, mod_ref, 0),
        )
        per_clip(seg, dscale, dmod_ref)
        dgain_ref[...] = dgain
        out_ref[...] = (dmiddle_ref[...] + dpre).astype(BF16)

    return pl.pallas_call(
        kernel,
        out_shape=(
            jax.ShapeDtypeStruct((length, depth), BF16),
            jax.ShapeDtypeStruct((clips, depth), F32),
            jax.ShapeDtypeStruct((1, depth), F32),
        ),
        in_specs=[VMEM] * 6,
        out_specs=(VMEM,) * 3,
        compiler_params=params(32),
    )(dnormed, tokens, dmiddle, seg, mods, norms)


def local(
    tokens_in,
    text_feats,
    frame_counts,
    time_steps,
    attn_master,
    attn_first,
    attn_second,
    ffn_master,
    ffn_first,
    ffn_second,
    norm_master,
    norm_first,
    norm_second,
    step_count,
    cotangent,
):
    parts, index = lax.axis_size("dp"), lax.axis_index("dp")
    length, model_width = tokens_in.shape
    width = model_width // lax.axis_size("mp")
    clip_slots, text_len, text_width = text_feats.shape[1:]
    key_count = clip_slots * text_len
    ring = Ring(parts)
    hidden_width = ffn_master.shape[1] * parts // (3 * model_width)
    attn_lay = Layout(attn_master.shape[1] * parts, width, parts, LANES)
    ffn_lay = Layout(ffn_master.shape[1] * parts, hidden_width, parts, TILE)
    norm_size = norm_master.shape[0]
    norm_rows = -(-norm_size // width)

    def as_rows(flat):
        flat = jnp.pad(flat, ((0, 0), (0, TILE * width - norm_size)))
        return flat.reshape(flat.shape[0], TILE, width)

    segment, positions = clip_layout(frame_counts[0], length, FRAME_TOK, clip_slots)
    seg, seg_row = segment[:, None], segment[None, :]
    cosine, sine = rope_tables(positions, HEAD_DIM, width // HEAD_DIM)
    rank = lax.axis_index("mp")

    def own_cut(values):
        size = values.shape[1] // lax.axis_size("mp")
        return lax.dynamic_slice_in_dim(values, rank * size, size, 1)

    text_rows = text_feats[0].reshape(key_count, text_width)

    sizes = [model_width] * 4 + [text_width, text_width, 4 * COND, 4]
    starts = [sum(sizes[:i]) for i in range(len(sizes) + 1)]
    attn_rows = to_rows(attn_lay, attn_master, index)
    attn_rows, ffn_flat, time_steps = join([], attn_rows, ffn_master, time_steps)
    ffn_piece = to_rows(ffn_lay, ffn_flat, index)
    pieces = Pieces(attn_lay, starts[4], ring)
    digits = jnp.stack([time_steps[0] // 32, time_steps[0] % 32]).astype(BF16)
    near_text = own_cut(text_rows)
    digits = jnp.pad(digits, ((0, TILE - 2), (0, near_text.shape[1] - clip_slots)))
    text_run = Shared(ring, jnp.concatenate([near_text, digits], 0), index, key_count)
    last = starts[7] - attn_lay.base[parts - 1]
    pieces.send(attn_rows)
    for _ in range(3):
        join([text_run.send()])
    cosine, sine, ffn_piece = join([pieces, text_run.send()], cosine, sine, ffn_piece)
    attn_run = Gathering(
        ring,
        jnp.concatenate(
            [
                pieces.piece(index),
                as_rows(norm_master[None])[0].astype(BF16),
                attn_rows[last : last + TILE],
            ],
            0,
        ),
        index,
    )
    ffn_run = Gathering(ring, ffn_piece, index)
    attn_run.send()
    join([text_run.send()])
    text_own, text_far = text_run.both()
    digits = text_run.result()[:, key_count : key_count + 2, :clip_slots].astype(F32)
    cond_all = condition_rows(digits[:, 0] * 32.0 + digits[:, 1], COND)
    near = Once({"own": text_own, "far": text_far}, 1)
    mod_share = join(
        [attn_run, near],
        modulation_share(attn_lay, index, attn_rows, starts[6], cond_all),
    )
    attn_run.send()
    ffn_run.send()
    text_four = in_order({0: text_own, 2: text_far, 1: near.got["own"], 3: near.got["far"]})
    text_sum = Scattering(
        ring, text_share(attn_lay, index, attn_rows, starts[4], text_four), index
    )
    text_four = join([attn_run, ffn_run, text_sum.send()], text_four)
    attn_run.send()
    ffn_run.send()
    mod_local = lax.all_to_all(mod_share, "dp", 0, 0).sum(0)
    mods = join(
        [attn_run, ffn_run, text_sum.send()],
        lax.all_gather(mod_local.reshape(4, clip_slots, width), "mp", axis=2, tiled=True),
    )
    attn_run.send()
    ffn_run.send()
    join([text_sum.send()])
    join([attn_run, ffn_run, text_sum.send()])
    attn_all = attn_run.result()
    text_lin = text_sum.result()
    ffn_run.send()
    w_out = pieces.pick(attn_all, starts[3], starts[4]).reshape(width, model_width)
    gains = attn_all[parts - 1, pieces.rows + TILE : pieces.rows + TILE + 4].astype(F32)
    norm_flat = attn_all[:, pieces.rows : pieces.rows + norm_rows].reshape(parts, -1)
    norms = norm_flat[:, :norm_size].astype(F32).reshape(4, model_width)
    normed, query, key, value, q_lin, k_lin = attention_inputs(
        pieces, attn_all, tokens_in, seg, mods, norms, gains, cosine, sine
    )
    mixed, cross, attn_part, tk_lin, text_key, text_value = attention_forward(
        query, key, value, text_lin, seg, seg_row, gains, w_out, clip_slots
    )
    attn_out = join([ffn_run], sum_mp(attn_part))
    ffn_all = ffn_run.result()

    ffn_all, near_in = join([], ffn_all, jnp.concatenate([own_cut(normed), mixed], 0))
    w_down = ffn_lay.pick(ffn_all, 2 * model_width, 3 * model_width).reshape(
        hidden_width, model_width
    )
    in_run = Shared(ring, near_in, index, length)
    early = [in_run.send()]
    middle, ffn_in, gate, up, hidden, ffn_part = join(
        early,
        *ffn_forward(ffn_lay, ffn_all, tokens_in, attn_out, seg, mods, norms, w_down),
    )
    step(early)
    ffn_out = join(early, sum_mp(ffn_part))
    step(early)
    output, dffn_part, ffn_grads, dmod_gate_ffn, dnorm_four = join(
        early,
        *ffn_backward(
            ffn_lay,
            ffn_all,
            middle,
            ffn_out,
            cotangent,
            ffn_in,
            gate,
            up,
            hidden,
            seg,
            mods,
            norms,
            w_down,
        ),
    )
    ffn_run = Scattering(ring, ffn_lay.cut([ffn_grads]), index)
    step(early)
    (
        dmiddle,
        dattn,
        dmixed,
        dmod_scale_ffn,
        dmod_gate_attn,
        dnorm_mid,
    ) = join(
        early + [ffn_run.send()],
        *branch_backward(
            sum_mp(dffn_part), middle, cotangent, attn_out, seg, mods, norms, w_out
        ),
    )
    step(early)
    dattn_run = Shared(ring, own_cut(dattn), index, length)
    ffn_run.send()
    join([dattn_run.send()])
    dnormed_part, acts, gain_grads = join(
        [ffn_run, dattn_run.send()] + early,
        *attention_backward(
            pieces,
            attn_all,
            dmixed,
            query,
            key,
            value,
            q_lin,
            k_lin,
            text_key,
            text_value,
            tk_lin,
            cross,
            seg,
            seg_row,
            gains,
            cosine,
            sine,
            clip_slots,
        ),
    )
    acts_run = Gathering(ring, acts, index)
    in_own, in_far = in_run.both()
    ffn_run.send()
    acts_run.send()
    join([dattn_run.send()])
    dattn_run.send()
    dnormed = join([ffn_run, acts_run, dattn_run], sum_mp(dnormed_part))
    near = Once({"own": in_own, "far": in_far}, 1)
    input_grad, dmod_scale_attn, dnorm_one = join(
        [ffn_run.send(), acts_run.send(), dattn_run.send(), near],
        *input_backward(dnormed, tokens_in, dmiddle, seg, mods, norms),
    )
    dmods = jnp.concatenate([dmod_scale_attn, dmod_gate_attn, dmod_scale_ffn, dmod_gate_ffn], 0)
    norm_grads = jnp.concatenate([dnorm_one, dnorm_mid, dnorm_four], 0)
    ends = jnp.concatenate(
        [
            own_cut(dmods),
            jnp.pad(gain_grads, ((0, TILE - 4), (0, 0))),
            norm_grads.reshape(-1, width),
        ],
        0,
    ).astype(BF16)
    normed_four = [in_own, near.got["own"], in_far, near.got["far"]]
    dattn_own, dattn_far = dattn_run.both()
    near = Once({"own": dattn_own, "far": dattn_far}, 1)
    ends_all, ffn_shard = join(
        [acts_run.send(), near],
        gather_small(ends[None], parts),
        to_flat(ffn_lay, ffn_run.result(), index),
    )
    dattn_four = [dattn_own, near.got["own"], dattn_far, near.got["far"]]
    step_value = step_count[0].astype(F32)
    ffn_result = join(
        [acts_run.send()],
        *adamw_flat(ffn_lay, ffn_master, ffn_first, ffn_second, ffn_shard, step_value, RATE),
    )
    attn_sum = shard_gradient(
        attn_lay,
        index,
        normed_four,
        dattn_four,
        text_four,
        in_run.result(),
        acts_run.result(),
        ends_all,
        cond_all,
    )
    attn_shard = to_flat(attn_lay, attn_sum, index)
    norm_sum = ends_all[:, 2 * TILE :].astype(F32).sum(0).reshape(-1)
    norm_shard = lax.dynamic_slice_in_dim(norm_sum, index * norm_size, norm_size, 0)
    attn_result = adamw_flat(
        attn_lay, attn_master, attn_first, attn_second, attn_shard, step_value, RATE
    )
    norm_result = adamw(norm_master, norm_first, norm_second, norm_shard, step_value, RATE_NORM)
    return (
        (output, input_grad)
        + tuple(attn_result)
        + tuple(ffn_result)
        + norm_result
        + (gain_grads[3:4],)
    )


def solution(mesh):
    tokens, flat, norm = P("dp", None), P("mp", "dp"), P("dp")
    return jax.shard_map(
        local,
        mesh=mesh,
        in_specs=(tokens, P("dp", None, None, None), tokens, tokens)
        + (flat,) * 6
        + (norm,) * 3
        + (P(), tokens),
        out_specs=(tokens,) * 2 + (flat,) * 10 + (norm,) * 5 + (P("dp", "mp"),),
        check_vma=False,
    )
```

```python
import functools
import math

import jax
import jax.numpy as jnp
from jax import lax
from jax.experimental import pallas as pl
from jax.experimental.pallas import tpu as pltpu
from jax.sharding import PartitionSpec as P

HEAD_DIM = 64
COND = 1024
FRAME_TOK = 8
LANES = 128
TILE = 16

EPS = 1e-06
NEG = -1e30
BETA_ONE = 0.9
BETA_TWO = 0.95
RATE = 0.03
RATE_NORM = 0.3
DECAY = 0.1
ADAM_EPS = 1e-08

F32 = jnp.float32
BF16 = jnp.bfloat16
VMEM = pl.BlockSpec(memory_space=pltpu.VMEM)
SMEM = pl.BlockSpec(memory_space=pltpu.SMEM)
ANY = pl.BlockSpec(memory_space=pl.ANY)


def params(mib):
    return pltpu.CompilerParams(vmem_limit_bytes=mib << 20)


def round_up(value, unit):
    return -(-value // unit) * unit


class Layout:
    def __init__(self, total, width, parts, tile, spare=0):
        self.total, self.width, self.parts, self.spare = total, width, parts, spare
        self.unit = tile * width
        self.size = total // parts
        self.base = [d * self.size // self.unit * tile for d in range(parts)] + [
            round_up(-(-total // width), tile)
        ]
        self.off = [d * self.size - self.base[d] * width for d in range(parts)]
        self.used = round_up(max(-(-(o + self.size) // width) for o in self.off), tile)
        self.rows = self.used + spare
        self.lanes = width // LANES
        self.edge = round_up(max(self.off), TILE * LANES)

    def offset(self, index):
        return (index * self.size) % self.unit

    def spans(self, low, high):
        found = []
        for d in range(self.parts):
            first, last = max(low, self.base[d]), min(high, self.base[d + 1])
            if first < last:
                found.append((d, first - self.base[d], last - first, first - low))
        return found

    def pick(self, held, low, high):
        found = [held[d, first : first + rows] for d, first, rows, _ in self.spans(low, high)]
        return found[0] if len(found) == 1 else jnp.concatenate(found, 0)

    def cut(self, matrices, spares=None):
        short = self.base[self.parts - 1] + self.used - sum(m.shape[0] for m in matrices)
        if short > 0:
            matrices = matrices + [jnp.zeros((short, self.width), matrices[0].dtype)]
        whole = jnp.concatenate(matrices, 0)
        if spares is None and self.used * self.parts == whole.shape[0]:
            return whole.reshape(self.parts, self.used, self.width)
        pieces = [whole[b : b + self.used] for b in self.base[: self.parts]]
        if spares is not None:
            pieces = [jnp.concatenate([p, spares[d]], 0) for d, p in enumerate(pieces)]
        return jnp.stack(pieces)


class Pieces:
    def __init__(self, layout, high, ring):
        self.width = layout.width
        parts = layout.parts
        self.rows = round_up(-(-high // parts), LANES)
        self.holders = sum(base < high for base in layout.base[:parts])
        free = list(range(self.holders, parts))
        self.where, self.pairs = [], {}
        for d in range(self.holders):
            last = min(layout.base[d + 1], high)
            for number, low in enumerate(range(layout.base[d], last, self.rows)):
                owner = d
                if number:
                    near = [f for f in free if (f - d) % ring.inner == 0] or free
                    owner = near[-1]
                    free.remove(owner)
                    self.pairs.setdefault(number, []).append((d, owner))
                self.where.append((low, min(low + self.rows, last), owner))

    def send(self, block):
        self.first = block[: self.rows]
        self.sent = {
            number: lax.ppermute(
                block[number * self.rows : (number + 1) * self.rows], "dp", pairs
            )
            for number, pairs in self.pairs.items()
        }
        return self

    def moving(self):
        return self.sent

    def land(self, moved):
        self.got = functools.reduce(jnp.add, moved.values())

    def piece(self, index):
        return jnp.where(index < self.holders, self.first, self.got)

    def spans(self, low, high):
        found = []
        for start, end, owner in self.where:
            first, last = max(low, start), min(high, end)
            if first < last:
                found.append((owner, first - start, last - first, first - low))
        return found

    def pick(self, held, low, high):
        found = [held[d, first : first + rows] for d, first, rows, _ in self.spans(low, high)]
        return found[0] if len(found) == 1 else jnp.concatenate(found, 0)


def to_rows(layout, flat, index, spare=None):
    rows, lanes, size = layout.used, layout.lanes, layout.size
    whole = size // (8 * LANES) * 8
    tail = size - whole * LANES
    head = max(layout.edge // LANES, 8)
    depth = round_up(max(rows * lanes + head, head + whole + 8) + 8, 8)
    offset = layout.offset(index).astype(jnp.int32)[None]
    operands = [offset, flat]
    if layout.edge:
        tails = flat[:, size - layout.edge :].reshape(head, LANES)
        chain = [(d, d + 1) for d in range(layout.parts - 1)]
        operands.append(lax.ppermute(tails.astype(BF16), "dp", chain).astype(F32))
    if layout.spare:
        operands.append(spare)

    def kernel(off_ref, x_ref, *rest):
        if layout.spare:
            rest[-2][rows : rows + layout.spare, :] = rest[-3][...].astype(BF16)
        edge_ref = rest[0] if layout.edge else None
        out_ref, pad_ref = rest[-2:]
        if layout.edge:
            pad_ref[0:head, :] = edge_ref[...]
        pad_ref[pl.ds(head, whole), :] = x_ref[:, pl.ds(0, whole * LANES)].reshape(whole, LANES)
        left = depth - head - whole
        pad_ref[pl.ds(head + whole, left), :] = jnp.zeros((left, LANES), F32)
        for row in range(-(-tail // LANES)):
            count = min(LANES, tail - row * LANES)
            pad_ref[pl.ds(head + whole + row, 1), 0:count] = x_ref[
                :, pl.ds((whole + row) * LANES, count)
            ]
        off_rows, off_lane = off_ref[0] // LANES, off_ref[0] % LANES
        lane = lax.broadcasted_iota(jnp.int32, (rows, LANES), 1)
        for j in range(lanes):
            if layout.edge:
                before = pad_ref[pl.ds(head + j - off_rows - 1, rows, stride=lanes), :]
                here = pad_ref[pl.ds(head + j - off_rows, rows, stride=lanes), :]
                value = jnp.where(
                    lane < off_lane,
                    pltpu.roll(before, off_lane, 1),
                    pltpu.roll(here, off_lane, 1),
                )
            else:
                value = pad_ref[pl.ds(head + j, rows, stride=lanes), :]
            out_ref[0:rows, LANES * j : LANES * j + LANES] = value.astype(BF16)

    return pl.pallas_call(
        kernel,
        out_shape=jax.ShapeDtypeStruct((layout.rows, layout.width), BF16),
        in_specs=[SMEM] + [VMEM] * (len(operands) - 1),
        out_specs=VMEM,
        scratch_shapes=[pltpu.VMEM((depth, LANES), F32)],
        compiler_params=params(40),
    )(*operands)


def block_rows(layout):
    need = -(-layout.size // LANES)
    steps = max(1, need // 864)
    return round_up(-(-need // steps), 8), -(-need // round_up(-(-need // steps), 8))


def to_flat(layout, matrix, index):
    rows, lanes = layout.used, layout.lanes
    block, steps = block_rows(layout)
    depth = round_up(max(rows * lanes, block * steps + layout.unit // LANES + 1), 8) + 8
    offset = layout.offset(index).astype(jnp.int32)[None]

    def kernel(off_ref, x_ref, out_ref, pad_ref):
        for j in range(lanes):
            pad_ref[pl.ds(j, rows, stride=lanes), :] = x_ref[
                0:rows, LANES * j : LANES * j + LANES
            ]
        left = depth - rows * lanes
        pad_ref[pl.ds(rows * lanes, left), :] = jnp.zeros((left, LANES), F32)
        off_rows, off_lane = off_ref[0] // LANES, off_ref[0] % LANES
        turn = (LANES - off_lane) % LANES
        lane = lax.broadcasted_iota(jnp.int32, (block, LANES), 1)

        def body(step, carry):
            start = pl.multiple_of(step * block, 8)
            here = pad_ref[pl.ds(start + off_rows, block), :]
            if layout.edge:
                after = pad_ref[pl.ds(start + off_rows + 1, block), :]
                here = jnp.where(
                    lane < LANES - off_lane, pltpu.roll(here, turn, 1), pltpu.roll(after, turn, 1)
                )
            out_ref[pl.ds(start, block), :] = here
            return carry

        lax.fori_loop(0, steps, body, 0)

    return pl.pallas_call(
        kernel,
        out_shape=jax.ShapeDtypeStruct((block * steps, LANES), F32),
        in_specs=[SMEM, VMEM],
        out_specs=VMEM,
        scratch_shapes=[pltpu.VMEM((depth, LANES), F32)],
        compiler_params=params(48),
    )(offset, matrix)


def adamw(master, first, second, gradient, step_value, rate):
    first_new = BETA_ONE * first + (1.0 - BETA_ONE) * gradient
    second_new = BETA_TWO * second + (1.0 - BETA_TWO) * gradient * gradient
    first_fix = 1.0 - jnp.power(BETA_ONE, step_value)
    second_fix = 1.0 - jnp.power(BETA_TWO, step_value)
    update = rate * (
        first_new / first_fix / (jnp.sqrt(second_new / second_fix) + ADAM_EPS) + DECAY * master
    )
    master_new = master - update
    return (master_new, first_new, second_new, gradient, master_new.astype(BF16))


def adamw_flat(layout, master, first, second, gradient, step_value, rate):
    block, steps = block_rows(layout)
    fixes = jnp.stack(
        [1.0 - jnp.power(BETA_ONE, step_value), 1.0 - jnp.power(BETA_TWO, step_value)]
    )

    def kernel(fix_ref, w_ref, m_ref, v_ref, g_ref, w_out, m_out, v_out, g_out, c_out):
        view = lambda ref: ref.reshape(block, LANES)
        grad = g_ref[...]
        master_old = view(w_ref)[...]
        first_new = BETA_ONE * view(m_ref)[...] + (1.0 - BETA_ONE) * grad
        second_new = BETA_TWO * view(v_ref)[...] + (1.0 - BETA_TWO) * grad * grad
        update = rate * (
            first_new / fix_ref[0] / (jnp.sqrt(second_new / fix_ref[1]) + ADAM_EPS)
            + DECAY * master_old
        )
        view(w_out)[...] = master_old - update
        view(m_out)[...] = first_new
        view(v_out)[...] = second_new
        view(g_out)[...] = grad
        c_out[...] = w_out[...].astype(BF16)

    row = pl.BlockSpec((1, block * LANES), lambda i: (0, i))
    like = jax.ShapeDtypeStruct(master.shape, F32)
    return pl.pallas_call(
        kernel,
        grid=(steps,),
        out_shape=(like, like, like, like, jax.ShapeDtypeStruct(master.shape, BF16)),
        in_specs=[SMEM, row, row, row, pl.BlockSpec((block, LANES), lambda i: (i, 0))],
        out_specs=(row,) * 5,
        compiler_params=params(48),
    )(fixes, master, first, second, gradient)


class Ring:
    def __init__(self, parts):
        self.parts = parts
        self.inner = 2 if parts % 2 == 0 else 1
        self.outer = parts // self.inner
        self.small = self.outer <= 8
        self.next = [(d, (d + self.inner) % parts) for d in range(parts)]
        self.pair = [(d, d ^ 1) for d in range(parts)]

    def swap(self, block):
        return lax.ppermute(block, "dp", self.pair)

    def onward(self, block):
        return lax.ppermute(block, "dp", self.next)


def join(runs, *work):
    moving = [run.moving() for run in runs]
    moving, work = lax.optimization_barrier((moving, list(work)))
    for run, moved in zip(runs, moving):
        run.land(moved)
    return work[0] if len(work) == 1 else work


class Gathering:
    def __init__(self, ring, block, index):
        self.ring, self.block, self.round = ring, block, 0
        self.rounds = ring.outer if ring.small else 1
        self.at, self.side = index // ring.inner, index % ring.inner
        self.zero = jnp.zeros((), index.dtype)
        self.held = jnp.zeros((ring.outer, ring.inner) + block.shape, block.dtype)

    def send(self):
        ring = self.ring
        self.sent = {}
        if self.round >= self.rounds:
            return self
        if not ring.small:
            self.sent["all"] = gather_small(self.block[None], ring.parts)
            return self
        if ring.inner == 2:
            self.sent["other"] = ring.swap(self.block)
        if self.round < ring.outer - 1:
            self.sent["after"] = ring.onward(self.block)
        return self

    def moving(self):
        return self.sent

    def put(self, value, side):
        slot = lax.rem(self.at - self.round + self.ring.outer, self.ring.outer)
        self.held = lax.dynamic_update_slice(
            self.held, value[None, None], (slot, side) + (self.zero,) * value.ndim
        )

    def land(self, moved):
        if self.round >= self.rounds:
            return
        if "all" in moved:
            self.held = moved["all"]
        else:
            if "other" in moved:
                self.put(moved["other"], 1 - self.side)
            self.put(self.block, self.side)
            self.block = moved.get("after")
        self.round += 1

    def result(self):
        while self.round < self.rounds:
            join([self.send()])
        return self.held.reshape((self.ring.parts,) + self.held.shape[-2:])


class Shared(Gathering):
    def __init__(self, ring, block, index, share):
        super().__init__(ring, block, index)
        self.share = share
        self.far_held = jnp.zeros(self.held.shape[:2] + (share,) + block.shape[1:], block.dtype)
        self.rounds += 1
        self.chunk = None

    def send(self):
        if self.round < self.rounds - 1:
            super().send()
        else:
            self.sent = {}
        if self.chunk is not None and self.round < self.rounds:
            pairs = [(m, m ^ 2) for m in range(lax.axis_size("mp"))]
            self.sent["far"] = lax.ppermute(self.chunk, "mp", pairs)
        return self

    def land(self, moved):
        if self.round >= self.rounds:
            return
        far = moved.pop("far", None)
        if far is not None:
            if not self.ring.small:
                self.far_held = far
            else:
                slot = lax.rem(self.at - self.round + 1 + self.ring.outer, self.ring.outer)
                for number, side in ((0, self.side), (1, 1 - self.side)):
                    self.far_held = lax.dynamic_update_slice(
                        self.far_held,
                        far[number][None, None],
                        (slot, side) + (self.zero,) * (far.ndim - 1),
                    )
        if self.round == self.rounds - 1:
            self.round += 1
            return
        if "all" in moved:
            super().land(moved)
            self.chunk = self.held[:, : self.share]
        else:
            self.chunk = jnp.stack([self.block[: self.share], moved["other"][: self.share]])
            super().land(moved)

    def both(self):
        own = self.result()[:, : self.share]
        return own, self.far_held.reshape(own.shape)


class Scattering:
    def __init__(self, ring, blocks, index):
        self.ring, self.blocks = ring, blocks
        self.at, self.side = index // ring.inner, index % ring.inner
        self.left = ring.outer if ring.small else 1
        self.pending = None

    def send(self):
        ring = self.ring
        self.sent = {}
        if not self.left:
            return self
        self.left -= 1
        if not ring.small:
            self.sent["all"] = scatter_halves(self.blocks, ring.parts)
            return self
        if self.pending is not None:
            self.sent["carried"] = ring.onward(self.pending.astype(BF16))
        first = lax.rem(self.at + self.left, ring.outer) * ring.inner
        self.mine = lax.dynamic_index_in_dim(self.blocks, first + self.side, 0, False)
        if ring.inner == 2:
            given = lax.dynamic_index_in_dim(self.blocks, first + 1 - self.side, 0, False)
            self.sent["other"] = ring.swap(given)
        return self

    def moving(self):
        return self.sent

    def land(self, moved):
        if "all" in moved:
            self.pending = moved["all"]
        if "all" in moved or not moved:
            return
        total = self.mine.astype(F32)
        for value in moved.values():
            total = total + value.astype(F32)
        self.pending = total

    def result(self):
        while self.left:
            join([self.send()])
        return self.pending


def step(runs):
    runs[:] = [run for run in runs if run.round < run.rounds]
    for run in runs:
        run.send()


class Once:
    def __init__(self, arrays, steps):
        self.sent = {}
        count = lax.axis_size("mp")
        for name, array in arrays.items():
            pairs = [(m, m ^ steps) for m in range(count)]
            self.sent[name] = lax.ppermute(array, "mp", pairs)

    def moving(self):
        return self.sent

    def land(self, moved):
        self.got = moved


def in_order(pieces):
    me = lax.axis_index("mp")
    first = pieces[0]
    held = jnp.zeros((len(pieces),) + first.shape, first.dtype)
    zero = jnp.zeros((), me.dtype)
    for key, piece in pieces.items():
        held = lax.dynamic_update_slice(held, piece[None], (me ^ key,) + (zero,) * piece.ndim)
    return held


def scatter_halves(blocks, parts):
    index = lax.axis_index("dp")
    step = parts // 2
    while step:
        upper = (index // step) % 2 == 1
        low, high = blocks[:step], blocks[step:]
        mine, given = jnp.where(upper, high, low), jnp.where(upper, low, high)
        got = lax.ppermute(given.astype(BF16), "dp", [(d, d ^ step) for d in range(parts)])
        blocks = mine.astype(F32) + got.astype(F32)
        step //= 2
    return blocks[0]


def gather_small(values, parts):
    index = lax.axis_index("dp")
    step = 1
    while step < parts:
        other = lax.ppermute(values, "dp", [(d, d ^ step) for d in range(parts)])
        upper = (index // step) % 2 == 1
        values = jnp.where(
            upper, jnp.concatenate([other, values], 0), jnp.concatenate([values, other], 0)
        )
        step *= 2
    return values


def sum_mp(part):
    count = lax.axis_size("mp")
    near = [(m, m ^ 1) for m in range(count)]
    half = part.shape[0] // 2
    side = lax.axis_index("mp") % 2
    low, high = part[:half], part[half:]
    mine, given = jnp.where(side == 0, low, high), jnp.where(side == 0, high, low)
    total = mine.astype(F32) + lax.ppermute(given, "mp", near).astype(F32)
    step = 2
    while step < count:
        total = total.astype(BF16)
        far = [(m, m ^ step) for m in range(count)]
        total = total.astype(F32) + lax.ppermute(total, "mp", far).astype(F32)
        step *= 2
    total = total.astype(BF16)
    other = lax.ppermute(total, "mp", near)
    return jnp.concatenate(
        [jnp.where(side == 0, total, other), jnp.where(side == 0, other, total)], 0
    )


def rope_tables(positions, head_size, repeats):
    half_size = head_size // 2
    frequency = jnp.exp(
        -jnp.log(10000.0) * 2.0 * jnp.arange(half_size, dtype=jnp.float32) / head_size
    )
    frequency = jnp.tile(frequency, 2 * repeats)
    angles = positions.astype(jnp.float32)[:, None] * frequency[None, :]
    return jnp.cos(angles), jnp.sin(angles)


def clip_layout(frames_row, length, frame_tok, clip_slots):
    clip_len = frames_row * frame_tok
    slots = jnp.arange(clip_slots, dtype=jnp.int32)
    clip_end = jnp.sum(
        jnp.where(slots[:, None] >= slots[None, :], clip_len[None, :], 0), 1, dtype=jnp.int32
    )
    clip_start = clip_end - clip_len
    row_index = jnp.arange(length, dtype=jnp.int32)
    segment = jnp.sum(
        (row_index[:, None] >= clip_end[None, :]).astype(jnp.int32), 1, dtype=jnp.int32
    )
    member = segment[:, None] == slots[None, :]
    begin_row = jnp.sum(jnp.where(member, clip_start[None, :], 0), 1, dtype=jnp.int32)
    begin_row = begin_row + jnp.where(segment == clip_slots, clip_end[clip_slots - 1], 0)
    return segment, row_index - begin_row


def condition_rows(steps, cond_width):
    packs, clips = steps.shape
    column = jnp.arange(4 * cond_width, dtype=jnp.int32)
    half_size = cond_width // 2
    k = column // 4
    place = lax.rem(k, half_size).astype(F32)
    frequency = jnp.exp(-jnp.log(10000.0) * place / half_size)
    angles = steps.reshape(-1)[:, None] * frequency[None, :]
    waves = jnp.where((k < half_size)[None, :], jnp.cos(angles), jnp.sin(angles))
    cond = jax.nn.silu(waves).astype(BF16).reshape(packs, 1, clips, 4 * cond_width)
    part = jnp.arange(4, dtype=jnp.int32)
    own = (lax.rem(column, 4)[None, :] == part[:, None])[None, :, None, :]
    return jnp.where(own, cond, jnp.zeros((), BF16)).reshape(packs, 4 * clips, 4 * cond_width)


def dot(left, right):
    return jnp.dot(left, right, preferred_element_type=F32)


def dot_t(left, right):
    return lax.dot_general(left, right, (((1,), (1,)), ((), ())), preferred_element_type=F32)


def t_dot(left, right):
    return lax.dot_general(left, right, (((0,), (0,)), ((), ())), preferred_element_type=F32)


def row_mean(values):
    return jnp.mean(values, -1, keepdims=True)


def per_token(seg, mod_ref, part):
    total = jnp.where(seg == 0, mod_ref[part, 0:1, :], 0.0)
    for clip in range(1, mod_ref.shape[1]):
        total = total + jnp.where(seg == clip, mod_ref[part, clip : clip + 1, :], 0.0)
    return total


def per_clip(seg, values, out_ref):
    for clip in range(out_ref.shape[0]):
        out_ref[clip : clip + 1, :] = jnp.sum(jnp.where(seg == clip, values, 0.0), 0, keepdims=True)


def column_sum(values):
    return jnp.sum(values, 0, keepdims=True)


def rms_back(unit, scale, grad):
    return scale * (grad - unit * row_mean(unit * grad))


def branch_back(grad, branch, gate_tok, gain):
    scale = lax.rsqrt(row_mean(branch * branch) + EPS)
    unit = branch * scale
    opened = jnp.tanh(gate_tok)
    grad_unit = grad * opened
    dgate = grad * unit * gain * (1.0 - opened * opened)
    return rms_back(unit, scale, grad_unit * gain), dgate, column_sum(grad_unit * unit)


def modulate_back(grad, values, gain, scale_tok):
    scale = lax.rsqrt(row_mean(values * values) + EPS)
    unit = values * scale
    grad_unit = grad * unit
    dscale = grad_unit * gain
    dgain = column_sum(grad_unit * (1.0 + scale_tok))
    return rms_back(unit, scale, grad * gain * (1.0 + scale_tok)), dscale, dgain


def head_mean(values):
    width = values.shape[-1]
    rows = lax.broadcasted_iota(jnp.int32, (width, width), 0) // HEAD_DIM
    columns = lax.broadcasted_iota(jnp.int32, (width, width), 1) // HEAD_DIM
    same = jnp.where(rows == columns, 1.0 / HEAD_DIM, 0.0)
    return jnp.dot(values, same, precision=lax.Precision.HIGHEST, preferred_element_type=F32)


def turn(values, sign):
    width = values.shape[-1]
    half = HEAD_DIM // 2
    lane = lax.broadcasted_iota(jnp.int32, values.shape, 1) % HEAD_DIM
    ahead = pltpu.roll(values, width - half, 1)
    behind = pltpu.roll(values, half, 1)
    return jnp.where(lane < half, -sign * ahead, sign * behind)


def head_rms(linear):
    scale = lax.rsqrt(head_mean(linear * linear) + EPS)
    return linear * scale, scale


def head_rms_back(linear, grad, gain):
    unit, scale = head_rms(linear)
    scaled = grad * gain
    return scale * (scaled - unit * head_mean(unit * scaled)), column_sum(grad * unit)


def soft(query, keys, mask):
    scores = dot_t(query, keys) * HEAD_DIM ** (-0.5)
    scores = jnp.where(mask, scores, NEG)
    raised = jnp.exp(scores - jnp.max(scores, -1, keepdims=True))
    return raised / jnp.sum(raised, -1, keepdims=True)


def soft_back(query, keys, values, probs, grad_out):
    grad_probs = dot_t(grad_out, values)
    grad_values = t_dot(probs.astype(BF16), grad_out)
    inner_sum = jnp.sum(probs * grad_probs, -1, keepdims=True)
    grad_scores = (probs * (grad_probs - inner_sum) * HEAD_DIM ** (-0.5)).astype(BF16)
    return dot(grad_scores, keys), t_dot(grad_scores, query), grad_values


def masks(seg_ref, seg_row_ref, key_count, clip_slots):
    seg = seg_ref[...]
    key_clip = lax.broadcasted_iota(jnp.int32, (1, key_count), 1) // (key_count // clip_slots)
    return seg == seg_row_ref[...], (seg == key_clip) | (seg == clip_slots)


class Fetch:
    def __init__(self, held_ref, layout, low, high, into_ref, sems, first):
        self.copies = []
        for number, (d, start, rows, offset) in enumerate(layout.spans(low, high)):
            copy = pltpu.make_async_copy(
                held_ref.at[d, pl.ds(start, rows)],
                into_ref.at[pl.ds(offset, rows)],
                sems.at[first + number],
            )
            copy.start()
            self.copies.append(copy)

    def wait(self):
        for copy in self.copies:
            copy.wait()


def own_rows(block, i, offset):
    row = lax.broadcasted_iota(jnp.int32, block.shape, 0) + i * block.shape[0]
    lane = lax.broadcasted_iota(jnp.int32, block.shape, 1)
    mine = row * block.shape[1] + lane >= offset
    return jnp.where(mine, block.astype(F32), 0.0).astype(BF16)


def block_place(layout, index):
    first = index * layout.size // layout.unit * (layout.unit // layout.width // LANES)
    return jnp.stack([first, layout.offset(index)]).astype(jnp.int32)


def modulation_share(layout, index, rows, low, cond):
    packs, conds, depth = cond.shape
    blocks = layout.used // LANES
    first_block, count = low // LANES, depth // LANES

    def kernel(place_ref, w_ref, cond_ref, out_ref):
        out_ref[...] = jnp.zeros_like(out_ref)

        def body(i, carry):
            g = place_ref[0] + i - first_block

            @pl.when((g >= 0) & (g < count))
            def _():
                weights = w_ref[pl.ds(pl.multiple_of(i * LANES, LANES), LANES), :]
                lanes = pl.ds(pl.multiple_of(g * LANES, LANES), LANES)
                left = cond_ref[:, :, lanes].reshape(packs * conds, LANES)
                out_ref[...] += dot(left, own_rows(weights, i, place_ref[1]))

            return carry

        lax.fori_loop(0, blocks, body, 0)

    out = pl.pallas_call(
        kernel,
        out_shape=jax.ShapeDtypeStruct((packs * conds, layout.width), F32),
        in_specs=[SMEM, VMEM, VMEM],
        out_specs=VMEM,
        compiler_params=params(40),
    )(block_place(layout, index), rows, cond)
    return out.reshape(packs, conds, layout.width)


def text_share(layout, index, rows, low, text):
    groups, packs, key_count, text_cut = text.shape
    width = layout.width
    blocks = layout.used // LANES
    first_block, count = low // LANES, groups * text_cut // LANES
    step_packs = min(8, packs)
    per_cut = text_cut // LANES

    def kernel(place_ref, w_ref, text_ref, out_ref, sum_ref):
        sum_ref[...] = jnp.zeros_like(sum_ref)

        def body(i, carry):
            g = place_ref[0] + i - first_block

            @pl.when((g >= 0) & (g < 2 * count))
            def _():
                weights = w_ref[pl.ds(pl.multiple_of(i * LANES, LANES), LANES), :]
                sub = g % count
                lanes = pl.ds(pl.multiple_of(sub % per_cut * LANES, LANES), LANES)
                left = text_ref[sub // per_cut, :, :, lanes].reshape(-1, LANES)
                sum_ref[g // count] += dot(left, own_rows(weights, i, place_ref[1]))

            return carry

        lax.fori_loop(0, blocks, body, 0)
        for kind in range(2):
            out_ref[:, :, kind * width : (kind + 1) * width] = (
                sum_ref[kind].astype(BF16).reshape(step_packs, key_count, width)
            )

    return pl.pallas_call(
        kernel,
        grid=(packs // step_packs,),
        out_shape=jax.ShapeDtypeStruct((packs, key_count, 2 * width), BF16),
        in_specs=[
            SMEM,
            pl.BlockSpec(rows.shape, lambda s: (0, 0), pipeline_mode=pl.Buffered(1)),
            pl.BlockSpec(
                (groups, step_packs, key_count, text_cut),
                lambda s: (0, s, 0, 0),
                pipeline_mode=pl.Buffered(1),
            ),
        ],
        out_specs=pl.BlockSpec((step_packs, key_count, 2 * width), lambda s: (s, 0, 0)),
        scratch_shapes=[pltpu.VMEM((2, step_packs * key_count, width), F32)],
        compiler_params=params(48),
    )(block_place(layout, index), rows, text)


def attention_inputs(layout, held, tokens, seg, mods, norms, gains, cosine, sine):
    length, depth = tokens.shape
    width = layout.width
    count = len(layout.spans(0, 3 * depth))

    def kernel(
        held_ref, x_ref, seg_ref, mod_ref, norm_ref, gain_ref, cos_ref, sin_ref,
        normed_ref, q_ref, k_ref, v_ref, q_lin_ref, k_lin_ref, w_ref, sems,
    ):
        fetch = Fetch(held_ref, layout, 0, 3 * depth, w_ref, sems, 0)
        x = x_ref[...].astype(F32)
        unit = x * lax.rsqrt(row_mean(x * x) + EPS)
        normed = unit * norm_ref[0:1, :] * (1.0 + per_token(seg_ref[...], mod_ref, 0))
        normed = normed.astype(BF16)
        normed_ref[...] = normed
        fetch.wait()
        cosine, sine = cos_ref[...], sin_ref[...]
        for place, (lin_ref, out_ref) in enumerate(((q_lin_ref, q_ref), (k_lin_ref, k_ref))):
            linear = dot(normed, w_ref[place * depth : (place + 1) * depth, :])
            lin_ref[...] = linear
            rms = head_rms(linear)[0] * gain_ref[place : place + 1, :]
            out_ref[...] = (rms * cosine + turn(rms, 1.0) * sine).astype(BF16)
        v_ref[...] = dot(normed, w_ref[2 * depth : 3 * depth, :]).astype(BF16)

    low, full = (jax.ShapeDtypeStruct((length, width), t) for t in (BF16, F32))
    return pl.pallas_call(
        kernel,
        out_shape=(jax.ShapeDtypeStruct((length, depth), BF16), low, low, low, full, full),
        in_specs=[ANY] + [VMEM] * 7,
        out_specs=(VMEM,) * 6,
        scratch_shapes=[
            pltpu.VMEM((3 * depth, width), BF16),
            pltpu.SemaphoreType.DMA((count,)),
        ],
        compiler_params=params(48),
    )(held, tokens, seg, mods, norms, gains, cosine, sine)


def attention_forward(query, key, value, text_lin, seg, seg_row, gains, w_out, clips):
    length, width = query.shape
    key_count = text_lin.shape[0]
    model_width = w_out.shape[1]

    def kernel(
        q_ref, k_ref, v_ref, lin_ref, seg_ref, row_ref, gain_ref, w_ref,
        mixed_ref, cross_ref, part_ref, tk_lin_ref, tk_ref, tv_ref,
    ):
        linear = lin_ref[:, 0:width]
        tk_lin_ref[...] = linear
        tk_ref[...] = (head_rms(linear)[0] * gain_ref[2:3, :]).astype(BF16)
        tv_ref[...] = lin_ref[:, width : 2 * width].astype(BF16)
        own_mask, cross_mask = masks(seg_ref, row_ref, key_count, clips)
        own = []
        for head in range(width // HEAD_DIM):
            at = slice(head * HEAD_DIM, (head + 1) * HEAD_DIM)
            probs = soft(q_ref[:, at], k_ref[:, at], own_mask)
            own.append(dot(probs.astype(BF16), v_ref[:, at]))
            probs = soft(q_ref[:, at], tk_ref[:, at], cross_mask)
            cross_ref[:, at] = dot(probs.astype(BF16), tv_ref[:, at])
        mixed = jnp.concatenate(own, 1) + jnp.tanh(gain_ref[3:4, :]) * cross_ref[...]
        mixed = mixed.astype(BF16)
        mixed_ref[...] = mixed
        part_ref[...] = dot(mixed, w_ref[...]).astype(BF16)

    return pl.pallas_call(
        kernel,
        out_shape=(
            jax.ShapeDtypeStruct((length, width), BF16),
            jax.ShapeDtypeStruct((length, width), F32),
            jax.ShapeDtypeStruct((length, model_width), BF16),
            jax.ShapeDtypeStruct((key_count, width), F32),
            jax.ShapeDtypeStruct((key_count, width), BF16),
            jax.ShapeDtypeStruct((key_count, width), BF16),
        ),
        in_specs=[VMEM] * 8,
        out_specs=(VMEM,) * 6,
        compiler_params=params(48),
    )(query, key, value, text_lin, seg, seg_row, gains, w_out)


def ffn_forward(layout, held, tokens, attn_out, seg, mods, norms):
    length, depth = tokens.shape
    width = layout.width
    counts = [len(layout.spans(i * depth, (i + 1) * depth)) for i in range(3)]

    def kernel(
        held_ref, x_ref, branch_ref, seg_ref, mod_ref, norm_ref,
        middle_ref, ffn_in_ref, gate_ref, up_ref, hidden_ref, part_ref, wd_ref,
        wg_ref, wu_ref, flat_ref, woven_ref, plain_ref, sems,
    ):
        for_down = Fetch(held_ref, layout, 2 * depth, 3 * depth, flat_ref, sems, sum(counts[:2]))
        for_gate = Fetch(held_ref, layout, 0, depth, wg_ref, sems, 0)
        for_up = Fetch(held_ref, layout, depth, 2 * depth, wu_ref, sems, counts[0])
        seg = seg_ref[...]
        branch = branch_ref[...].astype(F32)
        unit = branch * lax.rsqrt(row_mean(branch * branch) + EPS)
        opened = jnp.tanh(per_token(seg, mod_ref, 1))
        middle = x_ref[...].astype(F32) + opened * unit * norm_ref[1:2, :]
        middle_ref[...] = middle
        unit = middle * lax.rsqrt(row_mean(middle * middle) + EPS)
        ffn_in = (unit * norm_ref[2:3, :] * (1.0 + per_token(seg, mod_ref, 2))).astype(BF16)
        ffn_in_ref[...] = ffn_in
        for_down.wait()
        for j in range(width // LANES):
            woven_ref[j] = flat_ref[:, j * LANES : (j + 1) * LANES].astype(F32)
        half = width // 2
        for parity in range(2):
            for i in range(depth // LANES):
                at = parity * depth + i * LANES
                plain_ref[i, pl.ds(parity, half, stride=2), :] = woven_ref[
                    at % width // LANES, pl.ds(at // width, half, stride=3), :
                ]
        for i in range(depth // LANES):
            wd_ref[:, i * LANES : (i + 1) * LANES] = plain_ref[i].astype(BF16)
        for_gate.wait()
        gate = dot(ffn_in, wg_ref[...])
        gate_ref[...] = gate
        for_up.wait()
        up = dot(ffn_in, wu_ref[...])
        up_ref[...] = up
        hidden = (jax.nn.silu(gate) * up).astype(BF16)
        hidden_ref[...] = hidden
        part_ref[...] = dot(hidden, wd_ref[...]).astype(BF16)

    def like(columns, kind):
        return jax.ShapeDtypeStruct((length, columns), kind)

    return pl.pallas_call(
        kernel,
        out_shape=(
            like(depth, F32),
            like(depth, BF16),
            like(width, F32),
            like(width, F32),
            like(width, BF16),
            like(depth, BF16),
            jax.ShapeDtypeStruct((width, depth), BF16),
        ),
        in_specs=[ANY] + [VMEM] * 5,
        out_specs=(VMEM,) * 7,
        scratch_shapes=[
            pltpu.VMEM((depth, width), BF16),
            pltpu.VMEM((depth, width), BF16),
            pltpu.VMEM((depth, width), BF16),
            pltpu.VMEM((width // LANES, depth, LANES), F32),
            pltpu.VMEM((depth // LANES, width, LANES), F32),
            pltpu.SemaphoreType.DMA((sum(counts),)),
        ],
        compiler_params=params(56),
    )(held, tokens, attn_out, seg, mods, norms)


def ffn_backward(
    layout, held, middle, ffn_out, cotangent, ffn_in, gate, up, hidden, seg, mods, norms, w_down
):
    length, depth = middle.shape
    width = layout.width
    clips = mods.shape[1]
    counts = [len(layout.spans(i * depth, (i + 1) * depth)) for i in range(2)]
    cut = 256

    def kernel(
        held_ref, middle_ref, branch_ref, cot_ref, in_ref, gate_ref, up_ref, hidden_ref,
        seg_ref, mod_ref, norm_ref, down_hbm,
        output_ref, part_ref, grads_ref, dmod_ref, dgain_ref,
        wg_ref, wu_ref, wd_ref, woven_ref, sems,
    ):
        for_down = pltpu.make_async_copy(down_hbm, wd_ref, sems.at[sum(counts)])
        for_down.start()
        for_gate = Fetch(held_ref, layout, 0, depth, wg_ref, sems, 0)
        for_up = Fetch(held_ref, layout, depth, 2 * depth, wu_ref, sems, counts[0])
        seg = seg_ref[...]
        branch = branch_ref[...].astype(F32)
        gate_tok = per_token(seg, mod_ref, 3)
        gain = norm_ref[3:4, :]
        unit = branch * lax.rsqrt(row_mean(branch * branch) + EPS)
        output_ref[...] = (middle_ref[...] + jnp.tanh(gate_tok) * unit * gain).astype(BF16)
        dbranch, dgate_tok, dgain = branch_back(cot_ref[...].astype(F32), branch, gate_tok, gain)
        per_clip(seg, dgate_tok, dmod_ref)
        dgain_ref[...] = dgain
        dlow = dbranch.astype(BF16)
        for_down.wait()
        dhidden = dot_t(dlow, wd_ref[...])
        gate, up = gate_ref[...], up_ref[...]
        sigma = jax.nn.sigmoid(gate)
        dup = (dhidden * gate * sigma).astype(BF16)
        dgate = (dhidden * up * (sigma * (1.0 + gate * (1.0 - sigma)))).astype(BF16)
        half = width // 2
        unit_row = lax.broadcasted_iota(jnp.int32, (width, half), 0)
        unit_column = lax.broadcasted_iota(jnp.int32, (width, half), 1)
        chosen = []
        for parity in range(2):
            pick = jnp.where(unit_row == 2 * unit_column + parity, 1.0, 0.0).astype(BF16)
            chosen.append(dot(hidden_ref[...], pick).astype(BF16))
        for start in range(0, half, cut):
            pair = [dot(c[:, start : start + cut].T, dlow) for c in chosen]
            for place in range(3):
                for j in range(width // LANES):
                    at = place * width + j * LANES
                    woven_ref[j, pl.ds(3 * start + place, cut, stride=3), :] = pair[at // depth][
                        :, at % depth : at % depth + LANES
                    ]
        for j in range(width // LANES):
            grads_ref[2 * depth : 3 * depth, j * LANES : (j + 1) * LANES] = woven_ref[j].astype(
                BF16
            )
        for_gate.wait()
        part = dot_t(dgate, wg_ref[...])
        for_up.wait()
        part_ref[...] = (part + dot_t(dup, wu_ref[...])).astype(BF16)
        for start in range(0, depth, cut):
            in_t = in_ref[:, start : start + cut].T
            grads_ref[start : start + cut, :] = dot(in_t, dgate).astype(BF16)
            grads_ref[depth + start : depth + start + cut, :] = dot(in_t, dup).astype(BF16)

    def like(rows, columns, kind):
        return jax.ShapeDtypeStruct((rows, columns), kind)

    return pl.pallas_call(
        kernel,
        out_shape=(
            like(length, depth, BF16),
            like(length, depth, BF16),
            like(3 * depth, width, BF16),
            like(clips, depth, F32),
            like(1, depth, F32),
        ),
        in_specs=[ANY] + [VMEM] * 10 + [ANY],
        out_specs=(VMEM,) * 5,
        scratch_shapes=[
            pltpu.VMEM((depth, width), BF16),
            pltpu.VMEM((depth, width), BF16),
            pltpu.VMEM((width, depth), BF16),
            pltpu.VMEM((width // LANES, depth, LANES), F32),
            pltpu.SemaphoreType.DMA((sum(counts) + 1,)),
        ],
        compiler_params=params(56),
    )(
        held, middle, ffn_out, cotangent, ffn_in, gate, up, hidden, seg, mods, norms, w_down
    )


def branch_backward(dffn_in, middle, cotangent, attn_out, seg, mods, norms, w_out):
    length, depth = middle.shape
    width = w_out.shape[0]
    clips = mods.shape[1]

    def kernel(
        din_ref, middle_ref, cot_ref, branch_ref, seg_ref, mod_ref, norm_ref, wo_ref,
        dmiddle_ref, dlow_ref, dmixed_ref, dscale_ref, dgate_ref, dnorm_ref,
    ):
        seg = seg_ref[...]
        dpre, dscale, dgain = modulate_back(
            din_ref[...].astype(F32), middle_ref[...], norm_ref[2:3, :], per_token(seg, mod_ref, 2)
        )
        per_clip(seg, dscale, dscale_ref)
        dnorm_ref[1:2, :] = dgain
        dmiddle = cot_ref[...].astype(F32) + dpre
        dmiddle_ref[...] = dmiddle
        dbranch, dgate_tok, dgain = branch_back(
            dmiddle, branch_ref[...].astype(F32), per_token(seg, mod_ref, 1), norm_ref[1:2, :]
        )
        per_clip(seg, dgate_tok, dgate_ref)
        dnorm_ref[0:1, :] = dgain
        dlow = dbranch.astype(BF16)
        dlow_ref[...] = dlow
        dmixed_ref[...] = dot_t(dlow, wo_ref[...]).astype(BF16)

    def like(rows, columns, kind):
        return jax.ShapeDtypeStruct((rows, columns), kind)

    return pl.pallas_call(
        kernel,
        out_shape=(
            like(length, depth, F32),
            like(length, depth, BF16),
            like(length, width, BF16),
            like(clips, depth, F32),
            like(clips, depth, F32),
            like(2, depth, F32),
        ),
        in_specs=[VMEM] * 8,
        out_specs=(VMEM,) * 6,
        compiler_params=params(48),
    )(dffn_in, middle, cotangent, attn_out, seg, mods, norms, w_out)


def attention_backward(
    layout, held, dmixed, query, key, value, q_lin, k_lin,
    text_key, text_value, tk_lin, cross, seg, seg_row, gains, cosine, sine, clips,
):
    length, width = query.shape
    depth = layout.width * lax.axis_size("mp")
    key_count = text_key.shape[0]
    count = len(layout.spans(0, 3 * depth))

    def kernel(
        held_ref, dmixed_ref, q_ref, k_ref, v_ref, q_lin_ref, k_lin_ref, tk_ref, tv_ref,
        tk_lin_ref, cross_ref, seg_ref, row_ref, gain_ref, cos_ref, sin_ref,
        part_ref, acts_ref, dgains_ref, w_ref, dq_ref, dk_ref, dv_ref, dtk_ref, dtv_ref, sems,
    ):
        fetch = Fetch(held_ref, layout, 0, 3 * depth, w_ref, sems, 0)
        opened = jnp.tanh(gain_ref[3:4, :])
        dmixed = dmixed_ref[...]
        wide = dmixed.astype(F32)
        dgains_ref[3:4, :] = column_sum(wide * cross_ref[...]) * (1.0 - opened * opened)
        dcross = (wide * opened).astype(BF16)
        own_mask, cross_mask = masks(seg_ref, row_ref, key_count, clips)
        for head in range(width // HEAD_DIM):
            at = slice(head * HEAD_DIM, (head + 1) * HEAD_DIM)
            query = q_ref[:, at]
            probs = soft(query, k_ref[:, at], own_mask)
            dq, dk, dv = soft_back(query, k_ref[:, at], v_ref[:, at], probs, dmixed[:, at])
            probs = soft(query, tk_ref[:, at], cross_mask)
            dq_cross, dtk, dtv = soft_back(
                query, tk_ref[:, at], tv_ref[:, at], probs, dcross[:, at]
            )
            dq_ref[:, at] = dq + dq_cross
            dk_ref[:, at] = dk
            dv_ref[:, at] = dv
            dtk_ref[:, at] = dtk
            dtv_ref[:, at] = dtv
        cosine, sine = cos_ref[...], sin_ref[...]
        lows = []
        for place, (grad_ref, lin_ref) in enumerate(((dq_ref, q_lin_ref), (dk_ref, k_lin_ref))):
            grad = grad_ref[...]
            grad = grad * cosine + turn(grad * sine, -1.0)
            dlin, dgain = head_rms_back(lin_ref[...], grad, gain_ref[place : place + 1, :])
            dgains_ref[place : place + 1, :] = dgain
            lows.append(dlin.astype(BF16))
        lows.append(dv_ref[...].astype(BF16))
        dlin, dgain = head_rms_back(tk_lin_ref[...], dtk_ref[...], gain_ref[2:3, :])
        dgains_ref[2:3, :] = dgain
        for place in range(3):
            acts_ref[place * length : (place + 1) * length, :] = lows[place]
        acts_ref[3 * length : 3 * length + key_count, :] = dlin.astype(BF16)
        acts_ref[3 * length + key_count :, :] = dtv_ref[...].astype(BF16)
        fetch.wait()
        part = dot_t(lows[0], w_ref[0:depth, :])
        part = part + dot_t(lows[1], w_ref[depth : 2 * depth, :])
        part_ref[...] = (part + dot_t(lows[2], w_ref[2 * depth : 3 * depth, :])).astype(BF16)

    return pl.pallas_call(
        kernel,
        out_shape=(
            jax.ShapeDtypeStruct((length, depth), BF16),
            jax.ShapeDtypeStruct((3 * length + 2 * key_count, width), BF16),
            jax.ShapeDtypeStruct((4, width), F32),
        ),
        in_specs=[ANY] + [VMEM] * 15,
        out_specs=(VMEM,) * 3,
        scratch_shapes=[pltpu.VMEM((3 * depth, width), BF16)]
        + [pltpu.VMEM((length, width), F32)] * 3
        + [pltpu.VMEM((key_count, width), F32)] * 2
        + [pltpu.SemaphoreType.DMA((count,))],
        compiler_params=params(56),
    )(
        held, dmixed, query, key, value, q_lin, k_lin, text_key, text_value, tk_lin, cross, seg,
        seg_row, gains, cosine, sine,
    )


def shard_gradient(layout, index, normed, dattn, text, mixed, acts, ends, cond):
    groups = len(normed)
    packs, length, width = normed[0].shape
    key_count, text_cut = text.shape[2:]
    conds = cond.shape[1]
    cut = LANES
    step_packs = min(8, packs)
    blocks = layout.used // cut
    first = (index * layout.size // layout.unit * (layout.unit // width // cut)).astype(jnp.int32)
    per_in = groups * width // cut
    per_text = groups * text_cut // cut
    per_cond = cond.shape[2] // cut
    kinds = [3 * per_in, 4 * per_in, 4 * per_in + 2 * per_text, 4 * per_in + 2 * per_text + per_cond]

    def kernel(first_ref, t_ref, m_ref, a_ref, e_ref, c_ref, *rest):
        n_refs, d_refs = rest[:groups], rest[groups : 2 * groups]
        out_ref, woven_ref = rest[2 * groups :]
        me = first_ref[1]

        @pl.when(pl.program_id(0) == 0)
        def _():
            out_ref[...] = jnp.zeros_like(out_ref)

        def tall(block):
            return block.reshape(-1, block.shape[-1])

        def body(i, carry):
            g = first_ref[0] + i
            start = pl.multiple_of(i * cut, cut)
            rows = pl.ds(start, cut)

            @pl.when(g < kinds[0])
            def _():
                sub = g % per_in
                lanes = pl.ds(pl.multiple_of(sub % (width // cut) * cut, cut), cut)
                grads = pl.ds(pl.multiple_of(g // per_in * length, length), length)
                right = tall(a_ref[:, grads, :])
                for key in range(groups):

                    @pl.when(sub // (width // cut) == me ^ key)
                    def _():
                        out_ref[rows, :] += t_dot(tall(n_refs[key][:, :, lanes]), right)

            @pl.when((g >= kinds[0]) & (g < kinds[1]))
            def _():
                each = cut // groups
                at = (g - kinds[0]) * each
                lanes = pl.ds(pl.multiple_of(at // LANES * LANES, LANES), LANES)
                slab = tall(m_ref[:, length : 2 * length, lanes]).astype(F32)
                slab = pltpu.roll(slab, (LANES - at % LANES) % LANES, 1)
                left = slab.T[0:each, :].astype(BF16)
                for key in range(groups):
                    value = dot(left, tall(d_refs[key][...]))
                    for j in range(width // LANES):
                        woven_ref[j, pl.ds(me ^ key, each, stride=groups), :] = value[
                            :, j * LANES : (j + 1) * LANES
                        ]
                woven = [woven_ref[j] for j in range(width // LANES)]
                out_ref[rows, :] += jnp.concatenate(woven, 1)

            @pl.when((g >= kinds[1]) & (g < kinds[2]))
            def _():
                sub = (g - kinds[1]) % per_text
                lanes = pl.ds(pl.multiple_of(sub % (text_cut // cut) * cut, cut), cut)
                at = 3 * length + (g - kinds[1]) // per_text * key_count
                grads = pl.ds(pl.multiple_of(at, key_count), key_count)
                left = tall(t_ref[sub // (text_cut // cut), :, :, lanes])
                out_ref[rows, :] += t_dot(left, tall(a_ref[:, grads, :]))

            @pl.when((g >= kinds[2]) & (g < kinds[3]))
            def _():
                lanes = pl.ds(pl.multiple_of((g - kinds[2]) * cut, cut), cut)
                left = tall(c_ref[:, :, lanes])
                out_ref[rows, :] += t_dot(left, tall(e_ref[:, 0:conds, :]))

            @pl.when(g == kinds[3])
            def _():
                total = jnp.sum(e_ref[:, conds : conds + 16, :].astype(F32), 0)
                out_ref[pl.ds(start, 16), :] += total

            return carry

        lax.fori_loop(0, blocks, body, 0)

    def spec(array, packs_dim):
        shape = list(array.shape)
        shape[packs_dim] = step_packs
        return pl.BlockSpec(
            tuple(shape),
            lambda s: tuple(s if d == packs_dim else 0 for d in range(len(shape))),
            pipeline_mode=pl.Buffered(1),
        )

    operands = [(text, 1), (mixed, 0), (acts, 0), (ends, 0), (cond, 0)]
    operands += [(array, 0) for array in normed + dattn]
    return pl.pallas_call(
        kernel,
        grid=(packs // step_packs,),
        out_shape=jax.ShapeDtypeStruct((layout.used, width), F32),
        in_specs=[SMEM] + [spec(*o) for o in operands],
        out_specs=pl.BlockSpec((layout.used, width), lambda s: (0, 0)),
        scratch_shapes=[pltpu.VMEM((width // LANES, cut, LANES), F32)],
        compiler_params=params(58),
    )(jnp.stack([first, lax.axis_index("mp").astype(jnp.int32)]), *[o[0] for o in operands])


def input_backward(dnormed, tokens, dmiddle, seg, mods, norms):
    length, depth = tokens.shape
    clips = mods.shape[1]

    def kernel(d_ref, x_ref, dmiddle_ref, seg_ref, mod_ref, norm_ref, out_ref, dmod_ref, dgain_ref):
        seg = seg_ref[...]
        dpre, dscale, dgain = modulate_back(
            d_ref[...].astype(F32),
            x_ref[...].astype(F32),
            norm_ref[0:1, :],
            per_token(seg, mod_ref, 0),
        )
        per_clip(seg, dscale, dmod_ref)
        dgain_ref[...] = dgain
        out_ref[...] = (dmiddle_ref[...] + dpre).astype(BF16)

    return pl.pallas_call(
        kernel,
        out_shape=(
            jax.ShapeDtypeStruct((length, depth), BF16),
            jax.ShapeDtypeStruct((clips, depth), F32),
            jax.ShapeDtypeStruct((1, depth), F32),
        ),
        in_specs=[VMEM] * 6,
        out_specs=(VMEM,) * 3,
        compiler_params=params(32),
    )(dnormed, tokens, dmiddle, seg, mods, norms)


def local(
    tokens_in,
    text_feats,
    frame_counts,
    time_steps,
    attn_master,
    attn_first,
    attn_second,
    ffn_master,
    ffn_first,
    ffn_second,
    norm_master,
    norm_first,
    norm_second,
    step_count,
    cotangent,
):
    parts, index = lax.axis_size("dp"), lax.axis_index("dp")
    length, model_width = tokens_in.shape
    width = model_width // lax.axis_size("mp")
    clip_slots, text_len, text_width = text_feats.shape[1:]
    key_count = clip_slots * text_len
    ring = Ring(parts)
    hidden_width = ffn_master.shape[1] * parts // (3 * model_width)
    attn_lay = Layout(attn_master.shape[1] * parts, width, parts, LANES)
    ffn_lay = Layout(ffn_master.shape[1] * parts, hidden_width, parts, TILE)
    norm_size = norm_master.shape[0]
    norm_rows = -(-norm_size // width)

    def as_rows(flat):
        flat = jnp.pad(flat, ((0, 0), (0, TILE * width - norm_size)))
        return flat.reshape(flat.shape[0], TILE, width)

    segment, positions = clip_layout(frame_counts[0], length, FRAME_TOK, clip_slots)
    seg, seg_row = segment[:, None], segment[None, :]
    cosine, sine = rope_tables(positions, HEAD_DIM, width // HEAD_DIM)
    rank = lax.axis_index("mp")

    def own_cut(values):
        size = values.shape[1] // lax.axis_size("mp")
        return lax.dynamic_slice_in_dim(values, rank * size, size, 1)

    text_rows = text_feats[0].reshape(key_count, text_width)

    sizes = [model_width] * 4 + [text_width, text_width, 4 * COND, 4]
    starts = [sum(sizes[:i]) for i in range(len(sizes) + 1)]
    attn_rows = to_rows(attn_lay, attn_master, index)
    attn_rows, ffn_flat, time_steps = join([], attn_rows, ffn_master, time_steps)
    ffn_piece = to_rows(ffn_lay, ffn_flat, index)
    pieces = Pieces(attn_lay, starts[4], ring)
    digits = jnp.stack([time_steps[0] // 32, time_steps[0] % 32]).astype(BF16)
    near_text = own_cut(text_rows)
    digits = jnp.pad(digits, ((0, TILE - 2), (0, near_text.shape[1] - clip_slots)))
    text_run = Shared(ring, jnp.concatenate([near_text, digits], 0), index, key_count)
    last = starts[7] - attn_lay.base[parts - 1]
    pieces.send(attn_rows)
    for _ in range(3):
        join([text_run.send()])
    cosine, sine, ffn_piece = join([pieces, text_run.send()], cosine, sine, ffn_piece)
    attn_run = Gathering(
        ring,
        jnp.concatenate(
            [
                pieces.piece(index),
                as_rows(norm_master[None])[0].astype(BF16),
                attn_rows[last : last + TILE],
            ],
            0,
        ),
        index,
    )
    ffn_run = Gathering(ring, ffn_piece, index)
    attn_run.send()
    join([text_run.send()])
    text_own, text_far = text_run.both()
    digits = text_run.result()[:, key_count : key_count + 2, :clip_slots].astype(F32)
    cond_all = condition_rows(digits[:, 0] * 32.0 + digits[:, 1], COND)
    near = Once({"own": text_own, "far": text_far}, 1)
    mod_share = join(
        [attn_run, near],
        modulation_share(attn_lay, index, attn_rows, starts[6], cond_all),
    )
    attn_run.send()
    ffn_run.send()
    text_four = in_order({0: text_own, 2: text_far, 1: near.got["own"], 3: near.got["far"]})
    text_sum = Scattering(
        ring, text_share(attn_lay, index, attn_rows, starts[4], text_four), index
    )
    text_four = join([attn_run, ffn_run, text_sum.send()], text_four)
    attn_run.send()
    ffn_run.send()
    mod_local = lax.all_to_all(mod_share, "dp", 0, 0).sum(0)
    mods = join(
        [attn_run, ffn_run, text_sum.send()],
        lax.all_gather(mod_local.reshape(4, clip_slots, width), "mp", axis=2, tiled=True),
    )
    attn_run.send()
    ffn_run.send()
    join([text_sum.send()])
    join([attn_run, ffn_run, text_sum.send()])
    attn_all = attn_run.result()
    text_lin = text_sum.result()
    ffn_run.send()
    w_out = pieces.pick(attn_all, starts[3], starts[4]).reshape(width, model_width)
    gains = attn_all[parts - 1, pieces.rows + TILE : pieces.rows + TILE + 4].astype(F32)
    norm_flat = attn_all[:, pieces.rows : pieces.rows + norm_rows].reshape(parts, -1)
    norms = norm_flat[:, :norm_size].astype(F32).reshape(4, model_width)
    normed, query, key, value, q_lin, k_lin = attention_inputs(
        pieces, attn_all, tokens_in, seg, mods, norms, gains, cosine, sine
    )
    mixed, cross, attn_part, tk_lin, text_key, text_value = attention_forward(
        query, key, value, text_lin, seg, seg_row, gains, w_out, clip_slots
    )
    attn_out = join([ffn_run], sum_mp(attn_part))
    ffn_all = ffn_run.result()

    ffn_all, near_in = join([], ffn_all, jnp.concatenate([own_cut(normed), mixed], 0))
    in_run = Shared(ring, near_in, index, length)
    early = [in_run.send()]
    middle, ffn_in, gate, up, hidden, ffn_part, w_down = join(
        early,
        *ffn_forward(ffn_lay, ffn_all, tokens_in, attn_out, seg, mods, norms),
    )
    step(early)
    ffn_out = join(early, sum_mp(ffn_part))
    step(early)
    output, dffn_part, ffn_grads, dmod_gate_ffn, dnorm_four = join(
        early,
        *ffn_backward(
            ffn_lay,
            ffn_all,
            middle,
            ffn_out,
            cotangent,
            ffn_in,
            gate,
            up,
            hidden,
            seg,
            mods,
            norms,
            w_down,
        ),
    )
    ffn_run = Scattering(ring, ffn_lay.cut([ffn_grads]), index)
    step(early)
    (
        dmiddle,
        dattn,
        dmixed,
        dmod_scale_ffn,
        dmod_gate_attn,
        dnorm_mid,
    ) = join(
        early + [ffn_run.send()],
        *branch_backward(
            sum_mp(dffn_part), middle, cotangent, attn_out, seg, mods, norms, w_out
        ),
    )
    step(early)
    dattn_run = Shared(ring, own_cut(dattn), index, length)
    ffn_run.send()
    join([dattn_run.send()])
    dnormed_part, acts, gain_grads = join(
        [ffn_run, dattn_run.send()] + early,
        *attention_backward(
            pieces,
            attn_all,
            dmixed,
            query,
            key,
            value,
            q_lin,
            k_lin,
            text_key,
            text_value,
            tk_lin,
            cross,
            seg,
            seg_row,
            gains,
            cosine,
            sine,
            clip_slots,
        ),
    )
    acts_run = Gathering(ring, acts, index)
    in_own, in_far = in_run.both()
    ffn_run.send()
    acts_run.send()
    join([dattn_run.send()])
    dattn_run.send()
    dnormed = join([ffn_run, acts_run, dattn_run], sum_mp(dnormed_part))
    near = Once({"own": in_own, "far": in_far}, 1)
    input_grad, dmod_scale_attn, dnorm_one = join(
        [ffn_run.send(), acts_run.send(), dattn_run.send(), near],
        *input_backward(dnormed, tokens_in, dmiddle, seg, mods, norms),
    )
    dmods = jnp.concatenate([dmod_scale_attn, dmod_gate_attn, dmod_scale_ffn, dmod_gate_ffn], 0)
    norm_grads = jnp.concatenate([dnorm_one, dnorm_mid, dnorm_four], 0)
    ends = jnp.concatenate(
        [
            own_cut(dmods),
            jnp.pad(gain_grads, ((0, TILE - 4), (0, 0))),
            norm_grads.reshape(-1, width),
        ],
        0,
    ).astype(BF16)
    normed_four = [in_own, near.got["own"], in_far, near.got["far"]]
    dattn_own, dattn_far = dattn_run.both()
    near = Once({"own": dattn_own, "far": dattn_far}, 1)
    ends_all, ffn_shard = join(
        [acts_run.send(), near],
        gather_small(ends[None], parts),
        to_flat(ffn_lay, ffn_run.result(), index),
    )
    dattn_four = [dattn_own, near.got["own"], dattn_far, near.got["far"]]
    step_value = step_count[0].astype(F32)
    ffn_result = join(
        [acts_run.send()],
        *adamw_flat(ffn_lay, ffn_master, ffn_first, ffn_second, ffn_shard, step_value, RATE),
    )
    attn_sum = shard_gradient(
        attn_lay,
        index,
        normed_four,
        dattn_four,
        text_four,
        in_run.result(),
        acts_run.result(),
        ends_all,
        cond_all,
    )
    attn_shard = to_flat(attn_lay, attn_sum, index)
    norm_sum = ends_all[:, 2 * TILE :].astype(F32).sum(0).reshape(-1)
    norm_shard = lax.dynamic_slice_in_dim(norm_sum, index * norm_size, norm_size, 0)
    attn_result = adamw_flat(
        attn_lay, attn_master, attn_first, attn_second, attn_shard, step_value, RATE
    )
    norm_result = adamw(norm_master, norm_first, norm_second, norm_shard, step_value, RATE_NORM)
    return (
        (output, input_grad)
        + tuple(attn_result)
        + tuple(ffn_result)
        + norm_result
        + (gain_grads[3:4],)
    )


def solution(mesh):
    tokens, flat, norm = P("dp", None), P("mp", "dp"), P("dp")
    return jax.shard_map(
        local,
        mesh=mesh,
        in_specs=(tokens, P("dp", None, None, None), tokens, tokens)
        + (flat,) * 6
        + (norm,) * 3
        + (P(), tokens),
        out_specs=(tokens,) * 2 + (flat,) * 10 + (norm,) * 5 + (P("dp", "mp"),),
        check_vma=False,
    )
```
